32 devices in a mesh: wide: 8 (over y, x, core), narrow: 4 (over z).
Axes of the slice: x: 2, y: 2, z: 4, core: 2. Of those that a mesh axis runs over, the one named last changes fastest.
Arguments:
- tokens: bfloat16 [32, 128, 2048], P(('wide', 'narrow')), may hold values from -6 to 6
- conv_state: float32 [32, 3, 2816], P(('wide', 'narrow')), may hold values from -6 to 6
- recur_state: float32 [32, 2816], P(('wide', 'narrow')), may hold values from -6 to 6
- fresh_rows: int32 [32], P(('wide', 'narrow')), may hold values 0 or 1
- gain_mixer: bfloat16 [2048], P(('wide', 'narrow')), may hold values from 0.5 to 1.5
- proj_input: bfloat16 [2048, 2816], P(('wide', 'narrow')), may hold values from -0.125 to 0.125
- proj_gate: bfloat16 [2048, 2816], P(('wide', 'narrow')), may hold values from -0.125 to 0.125
- conv_kernel: bfloat16 [4, 2816], P(None, ('wide', 'narrow')), may hold values from -3 to 3
- decay_param: bfloat16 [2816], P(('wide', 'narrow')), may hold values from 1 to 9
- gate_recur: bfloat16 [2816, 176], P(('wide', 'narrow')), may hold values from -0.4375 to 0.4375
- gate_input: bfloat16 [2816, 176], P(('wide', 'narrow')), may hold values from -0.4375 to 0.4375
- proj_output: bfloat16 [2816, 2048], P(('wide', 'narrow')), may hold values from -0.4375 to 0.4375
- gain_mlp: bfloat16 [2048], P(('wide', 'narrow')), may hold values from 0.5 to 1.5
- mlp_gate: bfloat16 [2048, 6144], P(('wide', 'narrow')), may hold values from -0.125 to 0.125
- mlp_up: bfloat16 [2048, 6144], P(('wide', 'narrow')), may hold values from -0.125 to 0.125
- mlp_down: bfloat16 [6144, 2048], P(('wide', 'narrow')), may hold values from -0.15625 to 0.15625
- cotangent: bfloat16 [32, 128, 2048], P(('wide', 'narrow')), may hold values from -6 to 6
Outputs:
- output: bfloat16 [32, 128, 2048], P(('wide', 'narrow'))
- grad_tokens: bfloat16 [32, 128, 2048], P(('wide', 'narrow'))
- grad_conv_state: float32 [32, 3, 2816], P(('wide', 'narrow'))
- grad_recur_state: float32 [32, 2816], P(('wide', 'narrow'))
- grad_gain_mixer: float32 [2048], P(('wide', 'narrow'))
- grad_proj_input: float32 [2048, 2816], P(('wide', 'narrow'))
- grad_proj_gate: float32 [2048, 2816], P(('wide', 'narrow'))
- grad_conv_kernel: float32 [4, 2816], P(None, ('wide', 'narrow'))
- grad_decay_param: float32 [2816], P(('wide', 'narrow'))
- grad_gate_recur: float32 [2816, 176], P(('wide', 'narrow'))
- grad_gate_input: float32 [2816, 176], P(('wide', 'narrow'))
- grad_proj_output: float32 [2816, 2048], P(('wide', 'narrow'))
- grad_gain_mlp: float32 [2048], P(('wide', 'narrow'))
- grad_mlp_gate: float32 [2048, 6144], P(('wide', 'narrow'))
- grad_mlp_up: float32 [2048, 6144], P(('wide', 'narrow'))
- grad_mlp_down: float32 [6144, 2048], P(('wide', 'narrow'))
The draws below stay inside these ranges and needn't reach their ends.
Inputs may be any that keep to these rules, and one draw needn't show every extreme that they name: `fresh_rows`: 1 marks a row whose given states are replaced by zeros.
All inputs are finite; a program needn't handle non-finite values. No bound on the sum of `fresh_rows` on one device may be relied on, other than what follows from the above.
Results may differ from the reference program's by a relative error of at most 0.012.
Values may be sent and summed in bfloat16 or wider, within the bound.
A program may use at most 448 MiB of HBM per device.

```python
import math
import jax
import jax.numpy as jnp
from jax import lax

D = 2048
LRU = 2816
FF = 6144
BLOCKS = 16
BLK = 176
CONV = 4
TOK = 128
ROWS = 32


def place_ends(entries, key, smallest, high):
    extent = entries.shape
    place = [jax.random.randint(jax.random.fold_in(key, axis), (), 0, extent[axis]) for axis in range(len(extent))]
    entries = entries.at[tuple(place)].set(smallest)
    longest = extent.index(max(extent))
    place[longest] = (place[longest] + 1) % extent[longest]
    return entries.at[tuple(place)].set(high)


def with_spikes(values, stream_key, source, target, parts, factor):
    def block_of(position):
        return (jnp.arange(values.shape[position]) // (values.shape[position] // parts)).reshape((-1,) + (1,) * (values.ndim - 1 - position))

    first = jax.random.permutation(stream_key, parts)[block_of(target)]
    second = (block_of(target) + parts // 2) % parts
    return jnp.where((block_of(source) == first) | (block_of(source) == second), factor * values, values)


def block_scale(own_key, dims, cuts, low, largest):
    loudness, own = 1.0, jax.random.fold_in(own_key, 6)
    for position, shards_of in cuts:
        draws = jnp.exp(jax.random.uniform(jax.random.fold_in(own, position), (shards_of,), jnp.float32, low / len(cuts), largest / len(cuts)))
        loudness = loudness * jnp.repeat(draws, dims[position] // shards_of).reshape([-1 if axis == position else 1 for axis in range(len(dims))])
    return loudness


def bell_draw(key, shape, spread, limit, cuts=(), kind=jnp.bfloat16):
    values = jax.random.normal(key, shape, jnp.float32) * spread
    if len(cuts) > 0:
        values = block_scale(key, shape, cuts, -0.22, 0.18) * values
    return jnp.clip(values, min=-limit, max=limit).astype(kind)


def gaussian_with(stream_key, extent, scale, reach, cuts, heavy, kind=jnp.bfloat16):
    values = scale * jax.random.normal(stream_key, extent, jnp.float32)
    if cuts:
        values = values * block_scale(stream_key, extent, cuts, -0.22, 0.18)
    return jnp.clip(with_spikes(values, jax.random.fold_in(stream_key, 3), *heavy), -reach, reach).astype(kind)


def setup_inputs(seed: int = 0) -> dict:
    key_of = jax.random.split(jax.random.key(seed), 18)
    tokens = gaussian_with(key_of[0], (ROWS, TOK, D), 1.0, 6.0, ((0, 32),), (0, 2, 32, 2.75))
    conv_state = bell_draw(key_of[1], (ROWS, CONV - 1, LRU), 1.0, 6.0, ((0, 32),), jnp.float32)
    recur_state = bell_draw(key_of[2], (ROWS, LRU), 1.0, 6.0, ((0, 32),), jnp.float32)
    fresh_rows = place_ends((jax.random.randint(key_of[3], (ROWS,), 0, 2) < 1).astype(jnp.int32), jax.random.fold_in(key_of[3], 1), 0, 1)
    gain_mixer = jnp.clip(1.0 + 0.1 * jax.random.normal(key_of[4], (D,), jnp.float32), 0.5, 1.5).astype(jnp.bfloat16)
    proj_input = bell_draw(key_of[5], (D, LRU), D ** -0.5, 0.125, ((0, 32),))
    proj_gate = bell_draw(key_of[6], (D, LRU), D ** -0.5, 0.125, ((0, 32),))
    conv_kernel = bell_draw(key_of[7], (CONV, LRU), CONV ** -0.5, 3.0, ((1, 32),))
    decay_param = jnp.clip(1.0 + 8.0 * jax.random.uniform(key_of[8], (LRU,), jnp.float32) ** block_scale(key_of[8], (LRU,), ((0, 32),), -0.2, 0.2), 1.0, 9.0).astype(jnp.bfloat16)
    gate_recur = bell_draw(key_of[9], (LRU, BLK), BLK ** -0.5, 0.4375, ((0, 32),))
    gate_input = bell_draw(key_of[10], (LRU, BLK), BLK ** -0.5, 0.4375, ((0, 32),))
    proj_output = bell_draw(key_of[11], (LRU, D), (LRU // 16) ** -0.5, 0.4375, ((0, 32),))
    gain_mlp = jnp.clip(1.0 + 0.1 * jax.random.normal(key_of[12], (D,), jnp.float32), 0.5, 1.5).astype(jnp.bfloat16)
    mlp_gate = bell_draw(key_of[13], (D, FF), D ** -0.5, 0.125, ((0, 32),))
    mlp_up = bell_draw(key_of[14], (D, FF), D ** -0.5, 0.125, ((0, 32),))
    mlp_down = bell_draw(key_of[15], (FF, D), (FF // 4) ** -0.5, 0.15625, ((0, 32),))
    cotangent = bell_draw(key_of[16], (ROWS, TOK, D), 1.0, 6.0, ((0, 32),))
    return dict(tokens=tokens, conv_state=conv_state, recur_state=recur_state, fresh_rows=fresh_rows, gain_mixer=gain_mixer, proj_input=proj_input, proj_gate=proj_gate, conv_kernel=conv_kernel, decay_param=decay_param, gate_recur=gate_recur, gate_input=gate_input, proj_output=proj_output, gain_mlp=gain_mlp, mlp_gate=mlp_gate, mlp_up=mlp_up, mlp_down=mlp_down, cotangent=cotangent)


@jax.custom_vjp
def low(v):
    return lax.optimization_barrier(v.astype(jnp.bfloat16)).astype(jnp.float32)

@jax.custom_vjp
def low_back(v):
    return v

def low_keep(v):
    return (low(v), None)

def low_pass(kept, grad):
    return (grad,)

def back_keep(v):
    return (v, None)

def back_low(kept, grad):
    return (low(grad),)
low.defvjp(low_keep, low_pass)
low_back.defvjp(back_keep, back_low)
epsilon = 1e-06

def matmul_high(left_side, right_side):
    return jnp.dot(left_side, right_side, precision=lax.Precision.HIGHEST, preferred_element_type=jnp.float32)

def norm_scale(values, gain_vec):
    return values * lax.rsqrt(lax.optimization_barrier(jnp.mean(values * values, axis=-1, keepdims=True)) + epsilon) * gain_vec

def conv_apply(values, history, kernel):
    joined = jnp.concatenate([history, values], axis=0)
    length = values.shape[0]
    kernel_taps = kernel.shape[0]
    result = jnp.zeros_like(values)
    for offset in range(kernel_taps):
        first_row = kernel_taps - 1 - offset
        result = result + kernel[offset] * joined[first_row:first_row + length]
    return result

def block_mix(values, matrix):
    length = values.shape[0]
    shaped = values.reshape(length, BLOCKS, BLK)
    mixed_out = jnp.einsum('tki,kij->tkj', shaped, matrix.reshape(BLOCKS, BLK, BLK), precision=lax.Precision.HIGHEST)
    return mixed_out.reshape(length, BLOCKS * BLK)

def recurrence(log_decay, scan_in, initial):

    def advance(carried, pieces):
        carried = jnp.exp(pieces[0]) * carried + pieces[1]
        return (carried, carried)
    last_state, states = lax.scan(advance, initial, (log_decay, scan_in))
    return states

def row_forward(tokens_row, history, initial, keep_row, gain_mixer, proj_input, proj_gate, conv_kernel, decay_param, gate_recur, gate_input, proj_output, gain_mlp, mlp_gate, mlp_up, mlp_down):
    normed_one = low(norm_scale(tokens_row, gain_mixer))
    branch_in = low_back(matmul_high(normed_one, proj_input))
    gate_logits = low_back(matmul_high(normed_one, proj_gate))
    conv_out = low(conv_apply(branch_in, history * keep_row, conv_kernel))
    recur_logits = low_back(block_mix(conv_out, gate_recur))
    input_logits = low_back(block_mix(conv_out, gate_input))
    log_decay = -8.0 * jax.nn.sigmoid(recur_logits) * jax.nn.softplus(-decay_param)
    scan_in = jnp.sqrt(-jnp.expm1(2.0 * log_decay)) * jax.nn.sigmoid(input_logits) * conv_out
    hidden = recurrence(log_decay, scan_in, initial * keep_row)
    mixed_out = low(hidden * jax.nn.gelu(gate_logits))
    after_mixer = tokens_row + low_back(matmul_high(mixed_out, proj_output))
    normed_two = low(norm_scale(after_mixer, gain_mlp))
    gate_part = low_back(matmul_high(normed_two, mlp_gate))
    up_part = low_back(matmul_high(normed_two, mlp_up))
    activated = low(jax.nn.gelu(gate_part) * up_part)
    return after_mixer + matmul_high(activated, mlp_down)

def reference(tokens, conv_state, recur_state, fresh_rows, gain_mixer, proj_input, proj_gate, conv_kernel, decay_param, gate_recur, gate_input, proj_output, gain_mlp, mlp_gate, mlp_up, mlp_down, cotangent):
    weights = tuple((matrix.astype(jnp.float32) for matrix in (gain_mixer, proj_input, proj_gate, conv_kernel, decay_param, gate_recur, gate_input, proj_output, gain_mlp, mlp_gate, mlp_up, mlp_down)))
    group_rows = math.gcd(ROWS, max(1, 4096 // TOK))
    group_count = ROWS // group_rows
    keep_rows = (1 - fresh_rows).astype(jnp.float32)

    def grouped(array):
        return array.reshape((group_count, group_rows) + array.shape[1:])
    batch_data = (grouped(tokens.astype(jnp.float32)), grouped(conv_state), grouped(recur_state), grouped(keep_rows), grouped(cotangent.astype(jnp.float32)))

    def one_group(running, batch_item):
        tokens_grp, history_grp, initial_grp, keep_grp, cotan_grp = batch_item

        def forward(tokens_in, history_in, initial_in, *params):

            def single(tokens_row, history, initial, keep_row):
                return row_forward(tokens_row, history, initial, keep_row, *params)
            return jax.vmap(single)(tokens_in, history_in, initial_in, keep_grp)
        result, pullback = jax.vjp(forward, tokens_grp, history_grp, initial_grp, *weights)
        gradients = pullback(cotan_grp)
        running = tuple((before + update for before, update in zip(running, gradients[3:])))
        return (running, (result, gradients[0], gradients[1], gradients[2]))
    zeros_init = tuple((jnp.zeros_like(matrix) for matrix in weights))
    totals, (results, grad_tok, grad_hist, grad_init) = lax.scan(one_group, zeros_init, batch_data)
    return (results.reshape(tokens.shape).astype(jnp.bfloat16), grad_tok.reshape(tokens.shape).astype(jnp.bfloat16), grad_hist.reshape(conv_state.shape), grad_init.reshape(recur_state.shape), totals[0], totals[1], totals[2], totals[3], totals[4], totals[5], totals[6], totals[7], totals[8], totals[9], totals[10], totals[11])
```

```python
import functools
import itertools
from functools import reduce

import jax
import jax.numpy as jnp
from jax import lax
from jax.experimental import pallas as pl
from jax.experimental.pallas import tpu as pltpu
from jax.sharding import PartitionSpec as P

BLOCKS = 16
BLK = 176
SCAN_BLOCK = 16


epsilon = 1e-06
contract_rows = (((0,), (0,)), ((), ()))
contract_cols = (((1,), (1,)), ((), ()))


def plain_product(left_side, right_side):
    return jnp.dot(left_side, right_side, preferred_element_type=jnp.float32)


def rows_product(left_side, right_side):
    return lax.dot_general(left_side, right_side, contract_rows, preferred_element_type=jnp.float32)


def cols_product(left_side, right_side):
    return lax.dot_general(left_side, right_side, contract_cols, preferred_element_type=jnp.float32)


def norm_scale(values, gain_vec):
    return (
        values * lax.rsqrt(jnp.mean(values * values, axis=-1, keepdims=True) + epsilon) * gain_vec
    )


def conv_apply(values, history, kernel):
    joined = jnp.concatenate([history, values], axis=0)
    length = values.shape[0]
    kernel_taps = kernel.shape[0]
    result = jnp.zeros_like(values)
    for offset in range(kernel_taps):
        first_row = kernel_taps - 1 - offset
        result = result + kernel[offset] * joined[first_row : first_row + length]
    return result


def block_mix(values, matrix):
    length = values.shape[0]
    mixed_out = jnp.einsum(
        "tki,kij->tkj",
        values.reshape(length, BLOCKS, BLK),
        matrix.reshape(BLOCKS, BLK, BLK),
        preferred_element_type=jnp.float32,
    )
    return mixed_out.reshape(length, BLOCKS * BLK)


def block_back(grad_logits, matrix):
    length = grad_logits.shape[0]
    spread_back = jnp.einsum(
        "tkj,kij->tki",
        grad_logits.reshape(length, BLOCKS, BLK),
        matrix.reshape(BLOCKS, BLK, BLK),
        preferred_element_type=jnp.float32,
    )
    return spread_back.reshape(length, BLOCKS * BLK)


def block_grad(values, grad_logits):
    length = values.shape[0]
    summed = jnp.einsum(
        "tki,tkj->kij",
        values.reshape(length, BLOCKS, BLK),
        grad_logits.reshape(length, BLOCKS, BLK),
        preferred_element_type=jnp.float32,
    )
    return summed.reshape(BLOCKS * BLK, BLK)


def gate_apply(recur_logits, input_logits, conv_float, decay_float):
    log_decay = -8.0 * jax.nn.sigmoid(recur_logits) * jax.nn.softplus(-decay_float)
    scan_in = jnp.sqrt(-jnp.expm1(2.0 * log_decay)) * jax.nn.sigmoid(input_logits) * conv_float
    return (log_decay, scan_in)


def branch_apply(hidden, gate_logits):
    return hidden * jax.nn.gelu(gate_logits)


def mlp_apply(gate_part, up_part):
    return jax.nn.gelu(gate_part) * up_part


def block_scan(log_decay, scan_in, initial):
    length, channels = scan_in.shape
    block_count = length // SCAN_BLOCK
    positions = jnp.arange(SCAN_BLOCK)
    causal = (positions[:, None] >= positions[None, :])[:, :, None]

    def advance(carried, pieces):
        decay_piece, input_piece = pieces
        cumulative = jnp.cumsum(decay_piece, axis=0)
        spread = jnp.where(causal, cumulative[:, None, :] - cumulative[None, :, :], 0.0)
        factors = jnp.where(causal, jnp.exp(spread), 0.0)
        states = jnp.sum(factors * input_piece[None, :, :], axis=1) + jnp.exp(cumulative) * carried
        return (states[-1], states)

    last_state, states = lax.scan(
        advance,
        initial,
        (
            log_decay.reshape(block_count, SCAN_BLOCK, channels),
            scan_in.reshape(block_count, SCAN_BLOCK, channels),
        ),
    )
    return states.reshape(length, channels)


def scan_back(log_decay, hidden, initial, grad_hidden):
    following = jnp.concatenate([log_decay[1:], jnp.zeros_like(log_decay[:1])], axis=0)
    carried = block_scan(following[::-1], grad_hidden[::-1], jnp.zeros_like(initial))[::-1]
    previous = jnp.concatenate([initial[None], hidden[:-1]], axis=0)
    grad_log_decay = carried * jnp.exp(log_decay) * previous
    grad_initial = jnp.exp(log_decay[0]) * carried[0]
    return (grad_log_decay, carried, grad_initial)


def mixer_forward(tokens_row, history, initial, keep_row, mixer):
    (
        gain_vec,
        proj_input,
        proj_gate,
        conv_kernel,
        decay_param,
        gate_recur,
        gate_input,
        proj_output,
    ) = mixer
    values = tokens_row.astype(jnp.float32)
    normed_one = norm_scale(values, gain_vec.astype(jnp.float32)).astype(jnp.bfloat16)
    branch_in = plain_product(normed_one, proj_input)
    gate_logits = plain_product(normed_one, proj_gate)
    history_kept = history * keep_row
    kernel_float = conv_kernel.astype(jnp.float32)
    conv_out = conv_apply(branch_in, history_kept, kernel_float).astype(jnp.bfloat16)
    recur_logits = block_mix(conv_out, gate_recur)
    input_logits = block_mix(conv_out, gate_input)
    decay_float = decay_param.astype(jnp.float32)
    conv_float = conv_out.astype(jnp.float32)
    log_decay, scan_in = gate_apply(recur_logits, input_logits, conv_float, decay_float)
    initial_kept = initial * keep_row
    hidden = block_scan(log_decay, scan_in, initial_kept)
    mixed_out = branch_apply(hidden, gate_logits).astype(jnp.bfloat16)
    after_mixer = values + plain_product(mixed_out, proj_output)
    kept = (
        values,
        normed_one,
        branch_in,
        gate_logits,
        history_kept,
        kernel_float,
        conv_out,
        conv_float,
        recur_logits,
        input_logits,
        decay_float,
        log_decay,
        initial_kept,
        hidden,
        mixed_out,
    )
    return (after_mixer, kept)


def mlp_forward(after_mixer, mlp):
    gain_vec, mlp_gate, mlp_up, mlp_down = mlp
    normed_two = norm_scale(after_mixer, gain_vec.astype(jnp.float32)).astype(jnp.bfloat16)
    gate_part = plain_product(normed_two, mlp_gate)
    up_part = plain_product(normed_two, mlp_up)
    activated = mlp_apply(gate_part, up_part).astype(jnp.bfloat16)
    result = after_mixer + plain_product(activated, mlp_down)
    return (result, (after_mixer, normed_two, gate_part, up_part, activated))


def mlp_backward(grad_result, mlp, kept):
    gain_vec, mlp_gate, mlp_up, mlp_down = mlp
    after_mixer, normed_two, gate_part, up_part, activated = kept
    grad_activated = cols_product(grad_result, mlp_down)
    grad_down = rows_product(activated, grad_result)
    unused, mlp_pull = jax.vjp(mlp_apply, gate_part, up_part)
    grad_gate_part, grad_up_part = mlp_pull(grad_activated)
    grad_gate_part = grad_gate_part.astype(jnp.bfloat16)
    grad_up_part = grad_up_part.astype(jnp.bfloat16)
    grad_normed = cols_product(grad_gate_part, mlp_gate) + cols_product(grad_up_part, mlp_up)
    grad_mlp_gate = rows_product(normed_two, grad_gate_part)
    grad_mlp_up = rows_product(normed_two, grad_up_part)
    unused, norm_pull = jax.vjp(norm_scale, after_mixer, gain_vec.astype(jnp.float32))
    grad_values, grad_gain = norm_pull(grad_normed)
    grad_after = grad_result.astype(jnp.float32) + grad_values
    return (grad_after, (grad_gain, grad_mlp_gate, grad_mlp_up, grad_down))


def mixer_backward(grad_after, mixer, kept, keep_row):
    (
        gain_vec,
        proj_input,
        proj_gate,
        conv_kernel,
        decay_param,
        gate_recur,
        gate_input,
        proj_output,
    ) = mixer
    (
        values,
        normed_one,
        branch_in,
        gate_logits,
        history_kept,
        kernel_float,
        conv_out,
        conv_float,
        recur_logits,
        input_logits,
        decay_float,
        log_decay,
        initial_kept,
        hidden,
        mixed_out,
    ) = kept
    grad_mixed = grad_after.astype(jnp.bfloat16)
    grad_proj_output = rows_product(mixed_out, grad_mixed)
    grad_branch = cols_product(grad_mixed, proj_output)
    unused, branch_pull = jax.vjp(branch_apply, hidden, gate_logits)
    grad_hidden, grad_gate_logits = branch_pull(grad_branch)
    grad_gate_logits = grad_gate_logits.astype(jnp.bfloat16)
    grad_log_decay, grad_scan_in, grad_initial = scan_back(
        log_decay, hidden, initial_kept, grad_hidden
    )
    unused, gate_pull = jax.vjp(gate_apply, recur_logits, input_logits, conv_float, decay_float)
    grad_recur_logits, grad_input_logits, grad_conv, grad_decay = gate_pull(
        (grad_log_decay, grad_scan_in)
    )
    grad_recur_logits = grad_recur_logits.astype(jnp.bfloat16)
    grad_input_logits = grad_input_logits.astype(jnp.bfloat16)
    grad_gate_recur = block_grad(conv_out, grad_recur_logits)
    grad_gate_input = block_grad(conv_out, grad_input_logits)
    grad_conv = (
        grad_conv
        + block_back(grad_recur_logits, gate_recur)
        + block_back(grad_input_logits, gate_input)
    )
    unused, conv_pull = jax.vjp(conv_apply, branch_in, history_kept, kernel_float)
    grad_branch_in, grad_history, grad_kernel = conv_pull(grad_conv)
    grad_branch_low = grad_branch_in.astype(jnp.bfloat16)
    grad_proj_input = rows_product(normed_one, grad_branch_low)
    grad_proj_gate = rows_product(normed_one, grad_gate_logits)
    grad_normed = cols_product(grad_branch_low, proj_input) + cols_product(
        grad_gate_logits, proj_gate
    )
    unused, norm_pull = jax.vjp(norm_scale, values, gain_vec.astype(jnp.float32))
    grad_values, grad_gain = norm_pull(grad_normed)
    grad_tokens = (grad_after + grad_values).astype(jnp.bfloat16)
    weight_terms = (
        grad_gain,
        grad_proj_input,
        grad_proj_gate,
        grad_kernel,
        grad_decay,
        grad_gate_recur,
        grad_gate_input,
        grad_proj_output,
    )
    return (grad_tokens, grad_history * keep_row, grad_initial * keep_row, weight_terms)


def add_terms(first_terms, second_terms):
    return tuple(
        (left_side + right_side for left_side, right_side in zip(first_terms, second_terms))
    )


def shards(
    tokens,
    conv_state,
    recur_state,
    fresh_rows,
    gain_mixer,
    proj_input,
    proj_gate,
    conv_kernel,
    decay_param,
    gate_recur,
    gate_input,
    proj_output,
    gain_mlp,
    mlp_gate,
    mlp_up,
    mlp_down,
    cotangent,
):
    mixer_full = (
        lax.all_gather(gain_mixer, ("wide", "narrow"), axis=0, tiled=True),
        lax.all_gather(proj_input, ("wide", "narrow"), axis=0, tiled=True),
        lax.all_gather(proj_gate, ("wide", "narrow"), axis=0, tiled=True),
        lax.all_gather(conv_kernel, ("wide", "narrow"), axis=1, tiled=True),
        lax.all_gather(decay_param, ("wide", "narrow"), axis=0, tiled=True),
        lax.all_gather(gate_recur, ("wide", "narrow"), axis=0, tiled=True),
        lax.all_gather(gate_input, ("wide", "narrow"), axis=0, tiled=True),
        lax.all_gather(proj_output, ("wide", "narrow"), axis=0, tiled=True),
    )
    mlp_full = (
        lax.all_gather(gain_mlp, ("wide", "narrow"), axis=0, tiled=True),
        lax.all_gather(mlp_gate, ("wide", "narrow"), axis=0, tiled=True),
        lax.all_gather(mlp_up, ("wide", "narrow"), axis=0, tiled=True),
        lax.all_gather(mlp_down, ("wide", "narrow"), axis=0, tiled=True),
    )
    keep_rows = (1 - fresh_rows).astype(jnp.float32)
    stored = []
    row_index = 0
    after_mixer, mixer_kept = mixer_forward(
        tokens[row_index],
        conv_state[row_index],
        recur_state[row_index],
        keep_rows[row_index],
        mixer_full,
    )
    result, mlp_kept = mlp_forward(after_mixer, mlp_full)
    outputs = [result.astype(jnp.bfloat16)]
    stored.append((mixer_kept, mlp_kept))
    mixer_back = (
        lax.all_gather(gain_mixer, ("wide", "narrow"), axis=0, tiled=True),
        lax.all_gather(proj_input, ("wide", "narrow"), axis=0, tiled=True),
        lax.all_gather(proj_gate, ("wide", "narrow"), axis=0, tiled=True),
        lax.all_gather(conv_kernel, ("wide", "narrow"), axis=1, tiled=True),
        lax.all_gather(decay_param, ("wide", "narrow"), axis=0, tiled=True),
        lax.all_gather(gate_recur, ("wide", "narrow"), axis=0, tiled=True),
        lax.all_gather(gate_input, ("wide", "narrow"), axis=0, tiled=True),
        lax.all_gather(proj_output, ("wide", "narrow"), axis=0, tiled=True),
    )
    mlp_back = (
        lax.all_gather(gain_mlp, ("wide", "narrow"), axis=0, tiled=True),
        lax.all_gather(mlp_gate, ("wide", "narrow"), axis=0, tiled=True),
        lax.all_gather(mlp_up, ("wide", "narrow"), axis=0, tiled=True),
        lax.all_gather(mlp_down, ("wide", "narrow"), axis=0, tiled=True),
    )
    stored = []
    row_index = 0
    after_mixer, mixer_kept = mixer_forward(
        tokens[row_index],
        conv_state[row_index],
        recur_state[row_index],
        keep_rows[row_index],
        mixer_back,
    )
    unused, mlp_kept = mlp_forward(after_mixer, mlp_back)
    stored.append((mixer_kept, mlp_kept))
    row_index = 0
    grad_after, row_terms = mlp_backward(cotangent[row_index], mlp_back, stored[row_index][1])
    after_grads = [grad_after]
    mlp_terms = [row_terms]
    mlp_total = reduce(add_terms, mlp_terms)
    mlp_sums = (
        lax.psum_scatter(mlp_total[0], ("wide", "narrow"), scatter_dimension=0, tiled=True),
        lax.psum_scatter(mlp_total[1], ("wide", "narrow"), scatter_dimension=0, tiled=True),
        lax.psum_scatter(mlp_total[2], ("wide", "narrow"), scatter_dimension=0, tiled=True),
        lax.psum_scatter(mlp_total[3], ("wide", "narrow"), scatter_dimension=0, tiled=True),
    )
    row_index = 0
    grad_tokens, grad_history, grad_initial, row_terms = mixer_backward(
        after_grads[row_index], mixer_back, stored[row_index][0], keep_rows[row_index]
    )
    token_grads = [grad_tokens]
    history_grads = [grad_history]
    initial_grads = [grad_initial]
    mixer_terms = [row_terms]
    mixer_total = reduce(add_terms, mixer_terms)
    mixer_sums = (
        lax.psum_scatter(mixer_total[0], ("wide", "narrow"), scatter_dimension=0, tiled=True),
        lax.psum_scatter(mixer_total[1], ("wide", "narrow"), scatter_dimension=0, tiled=True),
        lax.psum_scatter(mixer_total[2], ("wide", "narrow"), scatter_dimension=0, tiled=True),
        lax.psum_scatter(mixer_total[3], ("wide", "narrow"), scatter_dimension=1, tiled=True),
        lax.psum_scatter(mixer_total[4], ("wide", "narrow"), scatter_dimension=0, tiled=True),
        lax.psum_scatter(mixer_total[5], ("wide", "narrow"), scatter_dimension=0, tiled=True),
        lax.psum_scatter(mixer_total[6], ("wide", "narrow"), scatter_dimension=0, tiled=True),
        lax.psum_scatter(mixer_total[7], ("wide", "narrow"), scatter_dimension=0, tiled=True),
    )
    return (
        jnp.stack(outputs),
        jnp.stack(token_grads),
        jnp.stack(history_grads),
        jnp.stack(initial_grads),
        mixer_sums[0],
        mixer_sums[1],
        mixer_sums[2],
        mixer_sums[3],
        mixer_sums[4],
        mixer_sums[5],
        mixer_sums[6],
        mixer_sums[7],
        mlp_sums[0],
        mlp_sums[1],
        mlp_sums[2],
        mlp_sums[3],
    )


COLUMNS = 4
LOWS = 2
PARTS = COLUMNS * LOWS
TOK = 128
CHUNK = 88
LANES = 96
WIDTH = 4 * LANES
SPAN = PARTS * TOK
MESH = pl.DeviceIdType.MESH
VMEM_BYTES = 60 * 1024 * 1024
low_type = jnp.bfloat16
full_type = jnp.float32


class Place:
    def __init__(self):
        wide = lax.axis_index("wide")
        self.z = lax.axis_index("narrow")
        self.column, self.core = wide // 2, wide % 2
        self.half, self.low = self.z // 2, self.z % 2
        self.part = self.column * 2 + self.low
        self.index = wide * 4 + self.z
        self.own = (self.column // 2, self.column % 2, self.low)

    def shifted(self, by_y, by_x, by_low, by_half):
        column = (self.column // 2 + by_y) % 2 * 2 + (self.column % 2 + by_x) % 2
        low, half = (self.low + by_low) % 2, (self.half + by_half) % 2
        return (column, low, half)

    def neighbour(self, axis):
        y, x, low = (1 - at if axis == here else at for here, at in enumerate(self.own))
        return (y * 4 + x * 2 + self.core, self.half * 2 + low)

    def cube(self, fixed, other=None):
        return tuple(
            1 - at if axis == other else at if axis in fixed else slice(None)
            for axis, at in enumerate(self.own)
        )

    def sibling(self):
        return (self.column * 2 + 1 - self.core, self.z)


def greet_all(place):
    barrier = pltpu.get_barrier_semaphore()

    @pl.loop(1, 32)
    def _(step):
        other = (place.index + step) % 32
        pl.semaphore_signal(
            barrier, inc=1, device_id=(other // 4, other % 4), device_id_type=MESH
        )

    pl.semaphore_wait(barrier, 31)


def remote(source, target, send, receive, device):
    return pltpu.make_async_remote_copy(
        src_ref=source,
        dst_ref=target,
        send_sem=send,
        recv_sem=receive,
        device_id=device,
        device_id_type=MESH,
    )


def await_bytes(view, semaphore):
    pltpu.make_async_copy(view, view, semaphore).wait()


class Spread:
    def __init__(self, pick):
        self.pick = pick

    def start(self, place, source, target, sems):
        self.copies = []
        slot = target.at[place.column, place.core, place.z]
        for shift in itertools.product(range(2), repeat=4):
            column, low, half = place.shifted(*shift)
            block = self.pick(source, column * 2 + low)
            if any(shift):
                copy = remote(
                    block, slot, sems.at[0], sems.at[1], (column * 2 + place.core, half * 2 + low)
                )
                copy.start()
                self.copies.append(copy)
            else:
                pltpu.make_async_copy(block, slot, sems.at[1]).start()

    def relay(self, place, source, target, sems):
        mine = target.at[:, place.core]
        await_bytes(mine, sems.at[1])
        self.passed = remote(mine, mine, sems.at[2], sems.at[3], place.sibling())
        self.passed.start()

    def finish(self, place, source, target, sems):
        self.passed.wait()
        for copy in self.copies:
            copy.wait_send()


class RowSpread:
    def start(self, place, source, target, sems):
        self.copies = []
        slot = target.at[place.half, place.low]
        for half in range(2):
            copy = remote(
                source,
                slot,
                sems.at[0],
                sems.at[1],
                (place.column * 2 + place.low, half * 2 + place.core),
            )
            own = (place.low == place.core) & (place.half == half)

            @pl.when(own)
            def _():
                pltpu.make_async_copy(source, slot, sems.at[1]).start()

            @pl.when(jnp.logical_not(own))
            def _():
                copy.start()

            self.copies.append((own, copy))

    def relay(self, place, source, target, sems):
        mine = target.at[:, place.core]
        await_bytes(mine, sems.at[1])
        self.passed = remote(mine, mine, sems.at[2], sems.at[3], place.sibling())
        self.passed.start()

    def finish(self, place, source, target, sems):
        self.passed.wait()
        for own, copy in self.copies:

            @pl.when(jnp.logical_not(own))
            def _():
                copy.wait_send()


class Peers:
    def __init__(self, pick):
        self.pick = pick

    def start(self, place, source, target, sems):
        self.copies = []
        slot = target.at[place.part]
        for shift in itertools.product(range(2), repeat=3):
            column, low, half = place.shifted(*shift, 0)
            block = self.pick(source, column * 2 + low)
            if any(shift):
                copy = remote(
                    block, slot, sems.at[0], sems.at[1], (column * 2 + place.core, half * 2 + low)
                )
                copy.start()
                self.copies.append(copy)
            else:
                pltpu.make_async_copy(block, slot, sems.at[1]).start()

    def relay(self, place, source, target, sems):
        pass

    def finish(self, place, source, target, sems):
        await_bytes(target, sems.at[1])
        for copy in self.copies:
            copy.wait_send()


class Swap:
    def start(self, place, source, target, sems):
        self.copy = remote(
            source.at[:, 1 - place.core], target, sems.at[0], sems.at[1], place.sibling()
        )
        self.copy.start()

    def relay(self, place, source, target, sems):
        pass

    def finish(self, place, source, target, sems):
        self.copy.wait()


class Owners:
    def start(self, place, source, target, sems):
        self.copies = []
        slot = target.at[place.half, place.part]
        for shift in itertools.product(range(2), repeat=4):
            column, low, half = place.shifted(*shift)
            z = half * 2 + low
            block = source.at[column, z]
            if any(shift):
                copy = remote(
                    block, slot, sems.at[0], sems.at[1], (column * 2 + place.core, z)
                )
                copy.start()
                self.copies.append(copy)
            else:
                pltpu.make_async_copy(block, slot, sems.at[1]).start()

    def relay(self, place, source, target, sems):
        pass

    def finish(self, place, source, target, sems):
        await_bytes(target, sems.at[1])
        for copy in self.copies:
            copy.wait_send()


class RowOwners:
    def start(self, place, source, target, sems):
        self.copies = []
        slot = target.at[place.half]
        for half in range(2):
            block = source.at[half]
            copy = remote(
                block,
                slot,
                sems.at[0],
                sems.at[1],
                (place.column * 2 + place.low, half * 2 + place.core),
            )
            own = (place.low == place.core) & (place.half == half)

            @pl.when(own)
            def _():
                pltpu.make_async_copy(block, slot, sems.at[1]).start()

            @pl.when(jnp.logical_not(own))
            def _():
                copy.start()

            self.copies.append((own, copy))

    def relay(self, place, source, target, sems):
        pass

    def finish(self, place, source, target, sems):
        await_bytes(target, sems.at[1])
        for own, copy in self.copies:

            @pl.when(jnp.logical_not(own))
            def _():
                copy.wait_send()


class Semaphores:
    def __init__(self, array):
        self.array, self.used = array, 0

    def take(self, count):
        taken = self.array.at[pl.ds(self.used, count)]
        self.used += count
        return taken


ORDERS = ((2, 0, 1), (2, 1, 0), (0, 2, 1), (1, 2, 0))
ROUTES = len(ORDERS)


def cuts(width):
    part = width // ROUTES
    return [pl.ds(route * part, part) for route in range(ROUTES)]


class CubeGather:
    def __init__(self, place, buffer, semaphores):
        self.place, self.buffer, self.copies = place, buffer, []
        self.sems = semaphores.take(6 * ROUTES)

    def step(self, number):
        rows = pl.ds(0, self.buffer.shape[3])
        for order, cut in enumerate(cuts(self.buffer.shape[4])):
            axes = ORDERS[order]
            if number > 0:
                self.copies[ROUTES * (number - 1) + order].wait_recv()
            region = self.buffer.at[self.place.cube(axes[number:]) + (rows, cut)]
            index = ROUTES * number + order
            copy = remote(
                region,
                region,
                self.sems.at[index],
                self.sems.at[3 * ROUTES + index],
                self.place.neighbour(axes[number]),
            )
            copy.start()
            self.copies.append(copy)

    def finish(self):
        for copy in self.copies[2 * ROUTES :]:
            copy.wait_recv()
        for copy in self.copies:
            copy.wait_send()


class CubeSum:
    def __init__(self, place, blocks, landings, semaphores):
        self.place, self.blocks, self.landings, self.copies = place, blocks, landings, []
        self.sems = semaphores.take(6 * ROUTES)

    def send(self, number, order, cut):
        axes = ORDERS[order][::-1]
        index = ROUTES * number + order
        rows = pl.ds(0, TOK)
        landing = self.landings[number]
        copy = remote(
            self.blocks.at[self.place.cube(axes[:number], axes[number]) + (rows, cut)],
            landing.at[(slice(None),) * (2 - number) + (rows, cut)],
            self.sems.at[index],
            self.sems.at[3 * ROUTES + index],
            self.place.neighbour(axes[number]),
        )
        copy.start()
        self.copies.append(copy)

    def start(self):
        for order, cut in enumerate(cuts(self.blocks.shape[4])):
            self.send(0, order, cut)

    def step(self, number, result=None):
        for order, cut in enumerate(cuts(self.blocks.shape[4])):
            axes = ORDERS[order][::-1]
            self.copies[ROUTES * number + order].wait_recv()
            landing = self.landings[number]
            for picks in itertools.product(range(2), repeat=2 - number):
                chosen = iter(picks)
                index = tuple(
                    self.place.own[axis] if axis in axes[: number + 1] else next(chosen)
                    for axis in range(3)
                )

                @pl.loop(0, TOK // 32)
                def _(block):
                    rows = pl.ds(pl.multiple_of(block * 32, 32), 32)
                    total = self.blocks[index + (rows, cut)].astype(full_type) + landing[
                        picks + (rows, cut)
                    ].astype(full_type)
                    if number < 2:
                        self.blocks[index + (rows, cut)] = total.astype(low_type)
                    else:
                        result[rows, cut] = total

            if number < 2:
                self.send(number + 1, order, cut)

    def finish(self):
        for copy in self.copies:
            copy.wait_send()


class Move:
    def __init__(self, place, plan, source, target, semaphores):
        self.plan, self.arguments = plan, (place, source, target, semaphores.take(4))

    def start(self):
        self.plan.start(*self.arguments)

    def relay(self):
        self.plan.relay(*self.arguments)

    def finish(self):
        self.plan.finish(*self.arguments)


class Local:
    def __init__(self, semaphores):
        self.semaphores, self.copies = semaphores, []

    def start(self, source, target):
        copy = pltpu.make_async_copy(source, target, self.semaphores.take(1).at[0])
        copy.start()
        self.copies.append(copy)
        return copy

    def finish(self):
        for copy in self.copies:
            copy.wait()


def whole(source, part):
    return source


def by_part(source, part):
    return source.at[part]


def by_columns(source, part):
    width = source.shape[1] // PARTS
    return source.at[:, pl.ds(pl.multiple_of(part * width, 128), width)]


def exchange_kernel(plan, *refs):
    count = len(plan)
    sources, targets, sems = refs[:count], refs[count : 2 * count], refs[2 * count]
    place = Place()
    greet_all(place)
    for step in ("start", "relay", "finish"):
        for index, move in enumerate(plan):
            getattr(move, step)(place, sources[index], targets[index], sems.at[index])


def exchange(name, identity, moves):
    plan = [move for move, array, shape in moves]
    hbm = pl.BlockSpec(memory_space=pl.ANY)
    return pl.pallas_call(
        functools.partial(exchange_kernel, plan),
        out_shape=[jax.ShapeDtypeStruct(shape, array.dtype) for move, array, shape in moves],
        in_specs=[hbm] * len(moves),
        out_specs=[hbm] * len(moves),
        scratch_shapes=[pltpu.SemaphoreType.DMA((len(moves), 4))],
        compiler_params=pltpu.CompilerParams(collective_id=identity, has_side_effects=True),
        name=name,
    )(*[array for move, array, shape in moves])


def row_block(row):
    return pl.ds(pl.multiple_of(row * TOK, TOK), TOK)


def small_expm1(values):
    near = values * (
        1.0
        + values
        * (0.5 + values * (1 / 6 + values * (1 / 24 + values * (1 / 120 + values * (1 / 720)))))
    )
    return jnp.where(values > -0.25, near, jnp.exp(values) - 1.0)


def gelu_parts(values):
    scale = 0.7978845608028654
    bent = jnp.tanh(scale * (values + 0.044715 * values * values * values))
    slope = 0.5 * (1.0 + bent) + 0.5 * values * (1.0 - bent * bent) * scale * (
        1.0 + 3 * 0.044715 * values * values
    )
    return (0.5 * values * (1.0 + bent), slope)


def put(array, rows, values):
    for piece in range(WIDTH // 128):
        array[piece, rows, :] = values[:, piece * 128 : (piece + 1) * 128]


def take(array, rows):
    return jnp.concatenate([array[piece, rows, :] for piece in range(WIDTH // 128)], axis=1)


def taps_of(aux):
    return [aux[tap : tap + 1, :] for tap in range(4)]


def placed_sum(gathered, place, row):
    owners = [
        gathered[place.part // 2, place.part % 2, z, row : row + 1, :].astype(full_type)
        for z in range(4)
    ]
    return owners[0] + owners[1] + owners[2] + owners[3]


def placed_gain(gathered, row):
    pieces = []
    for column, core, pair in itertools.product(range(COLUMNS), range(2), range(2)):
        both = [
            gathered[column, core, 2 * pair + odd, row : row + 1, 0:128].astype(full_type)
            for odd in range(2)
        ]
        pieces.append(both[0] + both[1])
    return jnp.concatenate(pieces, axis=1)


def scaled_norm(values, gain):
    scale = lax.rsqrt(jnp.mean(values * values, axis=1, keepdims=True) + epsilon)
    return values * scale * gain


def forward_kernel(
    tokens,
    small,
    states,
    columns,
    gates,
    out_rows,
    mlp_gate,
    mlp_up,
    mlp_down,
    cotangent,
    normed_out,
    states_out,
    columns_out,
    gates_out,
    rows_out,
    gate_out,
    up_out,
    down_out,
    cot_out,
    pre_out,
    conv_out,
    logits_out,
    hidden_out,
    mixed_out,
    after_out,
    two_out,
    aux_out,
    gains_out,
    tokens_all,
    small_all,
    states_all,
    columns_all,
    gates_all,
    rows_all,
    normed,
    pre,
    conv,
    logits,
    hidden,
    mixed,
    decays,
    inputs,
    padded,
    blocks,
    landing_one,
    landing_two,
    landing_three,
    after,
    two_all,
    aux,
    gains,
    sems,
):
    place = Place()
    semaphores = Semaphores(sems)
    local = Local(semaphores)

    def move(plan, source, target):
        return Move(place, plan, source, target, semaphores)

    own_tokens = tokens_all.at[place.own]
    load = pltpu.make_async_copy(tokens, own_tokens, semaphores.take(1).at[0])
    load.start()
    greet_all(place)
    load.wait()
    tokens_gather = CubeGather(place, tokens_all, semaphores)
    tokens_gather.step(0)
    small_move = move(Spread(whole), small, small_all)
    small_move.start()
    states_move = move(Peers(by_part), states, states_all)
    states_move.start()
    columns_move = move(Spread(by_part), columns, columns_all)
    columns_move.start()
    gates_move = move(RowSpread(), gates, gates_all)
    gates_move.start()
    rows_move = move(RowSpread(), out_rows, rows_all)
    rows_move.start()
    local.start(cotangent, cot_out.at[place.own])
    tokens_gather.step(1)
    small_move.relay()
    tokens_gather.step(2)
    late = [
        move(Spread(by_columns), mlp_gate, gate_out),
        move(Spread(by_columns), mlp_up, up_out),
        move(RowSpread(), mlp_down, down_out),
    ]
    for item in late:
        item.start()
    small_move.finish()
    for tap in range(5):
        aux[tap : tap + 1, :] = placed_sum(small_all, place, tap)
    decay = aux[4:5, :]
    aux[4:5, :] = jnp.maximum(-decay, 0.0) + jnp.log1p(jnp.exp(-jnp.abs(decay)))
    aux[5:6, :] = jax.nn.sigmoid(-decay)
    aux[6:8, :] = jnp.zeros((2, WIDTH), full_type)
    gains[0:1, :] = placed_gain(small_all, 5)
    gains[1:2, :] = placed_gain(small_all, 6)
    tokens_gather.finish()

    @pl.loop(0, SPAN // 32)
    def _(step):
        part, piece = step // 4, step % 4
        rows = pl.ds(pl.multiple_of(piece * 32, 32), 32)
        values = tokens_all[part // 4, part // 2 % 2, part % 2, rows, :].astype(full_type)
        normed[pl.ds(pl.multiple_of(step * 32, 32), 32), :] = scaled_norm(
            values, gains[0:1, :]
        ).astype(low_type)

    local.start(normed, normed_out)
    local.start(aux, aux_out)
    local.start(gains, gains_out)
    columns_move.relay()
    gates_move.relay()
    rows_move.relay()
    columns_move.finish()
    local.start(columns_all, columns_out)

    @pl.loop(0, SPAN // 256)
    def _(step):
        rows = pl.ds(pl.multiple_of(step * 256, 256), 256)
        pre[rows, :] = jnp.dot(
            normed[rows, :],
            columns_all[...].reshape(-1, 2 * WIDTH),
            preferred_element_type=full_type,
        )

    local.start(pre, pre_out)
    gates_move.finish()
    states_move.finish()
    local.start(gates_all, gates_out)
    local.start(states_all, states_out)
    taps = taps_of(aux)
    soft = aux[4:5, :]

    @pl.loop(0, PARTS)
    def _(row):
        rows = row_block(row)
        padded[0:8, :] = states_all[row]
        padded[8 : 8 + TOK, :] = pre[rows, 0:WIDTH]
        total = taps[0] * padded[8 : 8 + TOK, :]
        for tap in range(1, 4):
            total = total + taps[tap] * padded[8 - tap : 8 - tap + TOK, :]
        low = total.astype(low_type)
        conv[rows, :] = low
        both = jnp.dot(
            low, gates_all[...].reshape(WIDTH, 2 * WIDTH), preferred_element_type=full_type
        )
        logits[rows, :] = both
        log_decay = -8.0 * jax.nn.sigmoid(both[:, 0:WIDTH]) * soft
        scale = jnp.sqrt(-small_expm1(2.0 * log_decay))
        put(inputs, rows, scale * jax.nn.sigmoid(both[:, WIDTH:]) * low.astype(full_type))
        put(decays, rows, jnp.exp(log_decay))

    local.start(conv, conv_out)
    local.start(logits, logits_out)

    def advance(time, carried):
        across = pl.ds(time, PARTS, stride=TOK)
        carried = [
            decays[piece, across, :] * before + inputs[piece, across, :]
            for piece, before in enumerate(carried)
        ]
        for piece, now in enumerate(carried):
            hidden[piece, across, :] = now
        return carried

    initial = states_all[:, 0, :]
    initial = [initial[:, piece * 128 : (piece + 1) * 128] for piece in range(WIDTH // 128)]
    lax.fori_loop(0, TOK, advance, initial, unroll=8)
    local.start(hidden, hidden_out)
    rows_move.finish()
    local.start(rows_all, rows_out)

    @pl.loop(0, PARTS)
    def _(row):
        rows = row_block(row)
        gated, _ = gelu_parts(pre[rows, WIDTH:])
        low = (take(hidden, rows) * gated).astype(low_type)
        mixed[rows, :] = low
        blocks[row // 4, row // 2 % 2, row % 2] = jnp.dot(
            low, rows_all[...].reshape(WIDTH, -1), preferred_element_type=full_type
        ).astype(low_type)

    local.start(mixed, mixed_out)
    mixer_sum = CubeSum(place, blocks, (landing_one, landing_two, landing_three), semaphores)
    mixer_sum.start()
    mixer_sum.step(0)
    mixer_sum.step(1)
    mixer_sum.step(2, after)

    @pl.loop(0, TOK // 32)
    def _(step):
        rows = pl.ds(pl.multiple_of(step * 32, 32), 32)
        total = after[rows, :] + tokens_all[place.own + (rows,)].astype(full_type)
        after[rows, :] = total
        two_all[place.own + (rows,)] = scaled_norm(total, gains[1:2, :]).astype(low_type)

    local.start(after, after_out)
    two_gather = CubeGather(place, two_all, semaphores)
    two_gather.step(0)
    cot_gather = CubeGather(place, cot_out, semaphores)
    local.copies[0].wait()
    cot_gather.step(0)
    two_gather.step(1)
    cot_gather.step(1)
    two_gather.step(2)
    cot_gather.step(2)
    two_gather.finish()
    local.start(two_all, two_out)
    mixer_sum.finish()
    for item in late:
        item.relay()
    cot_gather.finish()
    for item in late:
        item.finish()
    states_move_done = local.copies[1:]
    for copy in states_move_done:
        copy.wait()


def forward_mixer(arrays, rows, width, units):
    hbm = pl.BlockSpec(memory_space=pl.ANY)
    lanes = (WIDTH // 128, SPAN, 128)
    cube = (2, 2, 2, TOK, width)
    spread = (COLUMNS, 2, 4, rows)
    outputs = [
        ((SPAN, width), low_type),
        ((PARTS, 8, WIDTH), full_type),
        (spread + (2 * WIDTH,), low_type),
        ((2, 2, LANES, 2 * WIDTH), low_type),
        ((2, 2, LANES, width), low_type),
        (spread + (4 * units,), low_type),
        (spread + (4 * units,), low_type),
        ((2, 2, units, width), low_type),
        (cube, low_type),
        ((SPAN, 2 * WIDTH), full_type),
        ((SPAN, WIDTH), low_type),
        ((SPAN, 2 * WIDTH), full_type),
        (lanes, full_type),
        ((SPAN, WIDTH), low_type),
        ((TOK, width), full_type),
        (cube, low_type),
        ((8, WIDTH), full_type),
        ((2, width), full_type),
    ]
    scratch = [
        (cube, low_type),
        ((COLUMNS, 2, 4, 16, WIDTH), low_type),
        ((PARTS, 8, WIDTH), full_type),
        (spread + (2 * WIDTH,), low_type),
        ((2, 2, LANES, 2 * WIDTH), low_type),
        ((2, 2, LANES, width), low_type),
        ((SPAN, width), low_type),
        ((SPAN, 2 * WIDTH), full_type),
        ((SPAN, WIDTH), low_type),
        ((SPAN, 2 * WIDTH), full_type),
        (lanes, full_type),
        ((SPAN, WIDTH), low_type),
        (lanes, full_type),
        (lanes, full_type),
        ((TOK + 8, WIDTH), full_type),
        (cube, low_type),
        ((2, 2, TOK, width), low_type),
        ((2, TOK, width), low_type),
        ((TOK, width), low_type),
        ((TOK, width), full_type),
        (cube, low_type),
        ((8, WIDTH), full_type),
        ((2, width), full_type),
    ]
    return pl.pallas_call(
        forward_kernel,
        out_shape=[jax.ShapeDtypeStruct(shape, kind) for shape, kind in outputs],
        in_specs=[hbm] * len(arrays),
        out_specs=[hbm] * len(outputs),
        scratch_shapes=[pltpu.VMEM(shape, kind) for shape, kind in scratch]
        + [pltpu.SemaphoreType.DMA((192,))],
        compiler_params=pltpu.CompilerParams(
            collective_id=0, has_side_effects=True, vmem_limit_bytes=VMEM_BYTES
        ),
        name="forward_mixer",
    )(*arrays)


def mixer_backward_kernel(
    pre,
    states,
    aux,
    blocks,
    conv_out,
    logits,
    hidden,
    grad_branch,
    grad_pre,
    grad_blocks,
    grad_states,
    grad_aux,
    decays,
    carries,
    padded,
):
    taps = taps_of(aux)
    soft, slope = aux[4:5, :], aux[5:6, :]

    @pl.loop(0, PARTS)
    def _(row):
        rows = row_block(row)
        gated, bend = gelu_parts(pre[rows, WIDTH:])
        branch = grad_branch[rows, :]
        grad_pre[rows, WIDTH:] = (branch * take(hidden, rows) * bend).astype(low_type)
        put(carries, rows, branch * gated)
        put(decays, rows, jnp.exp(-8.0 * jax.nn.sigmoid(logits[rows, 0:WIDTH]) * soft))

    def advance(step, state):
        factors, carried = state
        across = pl.ds(TOK - 1 - step, PARTS, stride=TOK)
        carried = [
            carries[piece, across, :] + factors[piece] * before
            for piece, before in enumerate(carried)
        ]
        for piece, now in enumerate(carried):
            carries[piece, across, :] = now
        return ([decays[piece, across, :] for piece in range(WIDTH // 128)], carried)

    zeros = [jnp.zeros((PARTS, 128), full_type)] * (WIDTH // 128)
    lax.fori_loop(0, TOK, advance, (zeros, zeros), unroll=8)
    grad_aux[...] = jnp.zeros_like(grad_aux)
    grad_blocks[...] = jnp.zeros_like(grad_blocks)

    @pl.loop(0, PARTS)
    def _(row):
        rows = row_block(row)
        padded[0:8, :] = jnp.broadcast_to(states[row, 0:1, :], (8, WIDTH))
        padded[8 : 8 + TOK, :] = take(hidden, rows)
        recur = jax.nn.sigmoid(logits[rows, 0:WIDTH])
        gate = jax.nn.sigmoid(logits[rows, WIDTH:])
        log_decay = -8.0 * recur * soft
        decay = take(decays, rows)
        scale = jnp.sqrt(-small_expm1(2.0 * log_decay))
        low = conv_out[rows, :]
        conv = low.astype(full_type)
        carried = take(carries, rows)
        total = (
            carried * decay * padded[7 : 7 + TOK, :]
            - carried * gate * conv * (decay * decay) / scale
        )
        grad_aux[4:5, :] += jnp.sum(total * 8.0 * recur * slope, axis=0, keepdims=True)
        to_recur = (total * (-8.0 * soft) * recur * (1.0 - recur)).astype(low_type)
        to_input = (carried * scale * conv * gate * (1.0 - gate)).astype(low_type)
        both = jnp.concatenate([to_recur, to_input], axis=1)
        grad_blocks[...] += lax.dot_general(
            low, both, contract_rows, preferred_element_type=full_type
        )
        back = carried * scale * gate + lax.dot_general(
            both, blocks[...], contract_cols, preferred_element_type=full_type
        )
        first = decay[0:1, :] * carried[0:1, :]
        padded[0:8, :] = jnp.zeros((8, WIDTH), full_type)
        padded[8 : 8 + TOK, :] = back
        padded[8 + TOK :, :] = jnp.zeros((8, WIDTH), full_type)
        spread = taps[0] * padded[0 : 8 + TOK, :]
        for tap in range(1, 4):
            spread = spread + taps[tap] * padded[tap : tap + 8 + TOK, :]
        grad_pre[rows, 0:WIDTH] = spread[8:, :].astype(low_type)
        grad_states[row] = spread[0:8, :]
        grad_states[row, 0:1, :] = first
        padded[0:8, :] = states[row]
        padded[8 : 8 + TOK, :] = pre[rows, 0:WIDTH]
        for tap in range(4):
            grad_aux[tap : tap + 1, :] += jnp.sum(
                back * padded[8 - tap : 8 - tap + TOK, :], axis=0, keepdims=True
            )


def in_vmem(kernel, name, arrays, shapes, scratch):
    vmem = pl.BlockSpec(memory_space=pltpu.VMEM)
    return pl.pallas_call(
        kernel,
        out_shape=[jax.ShapeDtypeStruct(shape, kind) for shape, kind in shapes],
        in_specs=[vmem] * len(arrays),
        out_specs=[vmem] * len(shapes),
        scratch_shapes=[pltpu.VMEM(shape, kind) for shape, kind in scratch],
        compiler_params=pltpu.CompilerParams(vmem_limit_bytes=VMEM_BYTES),
        name=name,
    )(*arrays)


def to_lanes(array):
    chunks = array.reshape(array.shape[:-1] + (-1, CHUNK))
    pads = [(0, 0)] * (chunks.ndim - 1) + [(0, LANES - CHUNK)]
    return jnp.pad(chunks, pads).reshape(array.shape[:-1] + (-1,))


def from_lanes(array):
    chunks = array.reshape(array.shape[:-1] + (-1, LANES))
    return chunks[..., :CHUNK].reshape(array.shape[:-1] + (-1,))


def pad_rows(array, rows):
    return jnp.pad(array, ((0, rows - array.shape[0]), (0, 0)))


def from_dense(dense):
    pair = 2 * LANES
    return jnp.concatenate(
        [
            jnp.concatenate(
                [
                    dense[
                        block * pair : (block + 1) * pair,
                        kind * WIDTH + block * pair : kind * WIDTH + (block + 1) * pair,
                    ]
                    for kind in range(2)
                ],
                axis=1,
            )
            for block in range(2)
        ],
        axis=0,
    )


def halves(
    tokens,
    conv_state,
    recur_state,
    fresh_rows,
    gain_mixer,
    proj_input,
    proj_gate,
    conv_kernel,
    decay_param,
    gate_recur,
    gate_input,
    proj_output,
    gain_mlp,
    mlp_gate,
    mlp_up,
    mlp_down,
    cotangent,
):
    width = tokens.shape[2]
    rows = width // 32
    units = mlp_down.shape[0]
    core = lax.axis_index("wide") % 2
    part = lax.axis_index("wide") // 2 * 2 + lax.axis_index("narrow") % 2
    keep = (1 - fresh_rows).astype(full_type)[0]

    columns = jnp.concatenate(
        [
            to_lanes(proj).reshape(rows, PARTS, WIDTH).transpose(1, 0, 2)
            for proj in (proj_input, proj_gate)
        ],
        axis=2,
    )
    zeros = jnp.zeros((CHUNK, 2 * LANES), low_type)
    first = lax.axis_index("narrow") < 2
    gates = jnp.concatenate(
        [
            jnp.where(chosen, to_lanes(gate), zeros)
            for gate in (gate_recur, gate_input)
            for chosen in (first, jnp.logical_not(first))
        ],
        axis=1,
    )
    z = lax.axis_index("narrow")
    taps = pad_rows(jnp.concatenate([conv_kernel, decay_param[None]], axis=0), 16)
    taps = lax.dynamic_update_slice(jnp.zeros((16, WIDTH), low_type), taps, (0, z * LANES))
    gain_rows = jnp.stack([gain_mixer, gain_mlp])
    small = lax.dynamic_update_slice(taps, gain_rows, (5, z % 2 * rows))
    state_rows = jnp.concatenate(
        [recur_state, jnp.zeros((4, recur_state.shape[1]), full_type), conv_state[0]], axis=0
    )
    states = to_lanes(state_rows * keep).reshape(8, PARTS, WIDTH).transpose(1, 0, 2)
    (
        normed_all,
        states_all,
        columns,
        gates,
        out_rows,
        mlp_gate,
        mlp_up,
        down,
        cot_all,
        pre,
        conv_out,
        logits,
        hidden,
        mixed,
        after_mixer,
        normed_two_all,
        aux,
        gain_rows,
    ) = forward_mixer(
        (
            tokens[0],
            small,
            states,
            columns,
            pad_rows(gates, LANES),
            pad_rows(proj_output, LANES),
            mlp_gate,
            mlp_up,
            mlp_down,
            cotangent[0],
        ),
        rows,
        width,
        units,
    )
    gain_one, gain_two = gain_rows[0], gain_rows[1]
    values = tokens[0].astype(full_type)
    cot_all = cot_all.reshape(SPAN, width)
    columns = columns.reshape(width, 2 * WIDTH)
    blocks = gates.reshape(WIDTH, 2 * WIDTH)
    out_rows = out_rows.reshape(WIDTH, width)
    mlp_gate = mlp_gate.reshape(width, units * 4)
    mlp_up = mlp_up.reshape(width, units * 4)
    down = down.reshape(units * 4, width)

    normed_two_all = normed_two_all.reshape(SPAN, width)
    gate_part = plain_product(normed_two_all, mlp_gate)
    up_part = plain_product(normed_two_all, mlp_up)
    activated = mlp_apply(gate_part, up_part).astype(low_type)
    out_partial = plain_product(activated, down).astype(low_type).reshape(PARTS, TOK, width)
    grad_activated = cols_product(cot_all, down)
    grad_down = rows_product(activated, cot_all).astype(low_type)
    unused, mlp_pull = jax.vjp(mlp_apply, gate_part, up_part)
    grad_gate_part, grad_up_part = mlp_pull(grad_activated)
    grad_gate_part = grad_gate_part.astype(low_type)
    grad_up_part = grad_up_part.astype(low_type)
    grad_two = cols_product(grad_gate_part, mlp_gate) + cols_product(grad_up_part, mlp_up)
    grad_two = grad_two.astype(low_type).reshape(PARTS, TOK, width)
    grad_mlp_gate = rows_product(normed_two_all, grad_gate_part).astype(low_type)
    grad_mlp_up = rows_product(normed_two_all, grad_up_part).astype(low_type)
    grad_two, out_arrived = exchange(
        "sum_two",
        4,
        [
            (Peers(by_part), grad_two, (PARTS, TOK, width)),
            (Peers(by_part), out_partial, (PARTS, TOK, width)),
        ],
    )
    output = (after_mixer + jnp.sum(out_arrived.astype(full_type), axis=0)).astype(low_type)
    grad_two = jnp.sum(grad_two.astype(full_type), axis=0)
    unused, norm_pull = jax.vjp(norm_scale, after_mixer, gain_two)
    grad_values, grad_gain_two = norm_pull(grad_two)
    grad_after = cotangent[0].astype(full_type) + grad_values

    grad_mixed = grad_after.astype(low_type)
    (mixed_all,) = exchange("gather_mixed", 5, [(Peers(whole), grad_mixed, (PARTS, TOK, width))])
    mixed_all = mixed_all.reshape(SPAN, width)
    grad_branch = cols_product(mixed_all, out_rows)
    grad_out = rows_product(mixed, mixed_all).astype(low_type)
    grad_pre, grad_blocks, grad_states, grad_aux = in_vmem(
        mixer_backward_kernel,
        "mixer_backward",
        (pre, states_all, aux, blocks, conv_out, logits, hidden, grad_branch),
        [
            ((SPAN, 2 * WIDTH), low_type),
            ((WIDTH, 2 * WIDTH), full_type),
            ((PARTS, 8, WIDTH), full_type),
            ((8, WIDTH), full_type),
        ],
        [
            ((WIDTH // 128, SPAN, 128), full_type),
            ((WIDTH // 128, SPAN, 128), full_type),
            ((TOK + 16, WIDTH), full_type),
        ],
    )
    grad_one = cols_product(grad_pre, columns).astype(low_type).reshape(PARTS, TOK, width)
    grad_columns = rows_product(normed_all, grad_pre).astype(low_type)
    grad_one, grad_states = exchange(
        "sum_one",
        6,
        [
            (Peers(by_part), grad_one, (PARTS, TOK, width)),
            (Peers(by_part), grad_states, (PARTS, 8, WIDTH)),
        ],
    )
    grad_one = jnp.sum(grad_one.astype(full_type), axis=0)
    unused, norm_pull = jax.vjp(norm_scale, values, gain_one)
    grad_values, grad_gain_one = norm_pull(grad_one)
    grad_tokens = (grad_after + grad_values).astype(low_type)
    grad_states = grad_states.transpose(1, 0, 2).reshape(8, PARTS * WIDTH)
    grad_states = from_lanes(grad_states) * keep

    gains = jnp.stack([grad_gain_one.reshape(32, rows), grad_gain_two.reshape(32, rows)], axis=1)
    gains = jnp.pad(gains, ((0, 0), (0, 6), (0, 128 - rows)))
    own_aux = grad_aux.reshape(8, 4, LANES).transpose(1, 0, 2)[:, 0:5]
    own_aux = jnp.pad(own_aux, ((0, 0), (2, 1), (0, 128 - LANES)))
    own_aux = lax.dynamic_update_slice(jnp.zeros_like(gains), own_aux, (4 * part, 0, 0))
    small_terms = (gains + own_aux).reshape(COLUMNS, 2, 4, 8, 128)
    wide_terms = [
        array.reshape(COLUMNS, 2, 4, rows, -1) for array in (grad_columns, grad_mlp_gate, grad_mlp_up)
    ]
    row_terms = [
        from_dense(grad_blocks).astype(low_type).reshape(2, 2, LANES, WIDTH),
        grad_out.reshape(2, 2, LANES, width),
        grad_down.reshape(2, 2, units, width),
    ]
    terms = [small_terms] + wide_terms + row_terms
    swapped = exchange(
        "swap_cores",
        7,
        [(Swap(), term, term.shape[:1] + term.shape[2:]) for term in terms],
    )
    terms = [
        (
            lax.dynamic_index_in_dim(term, core, 1, keepdims=False).astype(full_type)
            + other.astype(full_type)
        ).astype(term.dtype)
        for term, other in zip(terms, swapped)
    ]
    arrived = exchange(
        "return_weights",
        8,
        [(Owners(), term, (2, PARTS) + term.shape[2:]) for term in terms[:4]]
        + [(RowOwners(), term, term.shape) for term in terms[4:]],
    )
    small_sum = jnp.sum(arrived[0], axis=(0, 1))
    column_sum, gate_sum, up_sum, block_sum, out_sum, down_sum = (
        jnp.sum(term.astype(full_type), axis=0) for term in arrived[1:]
    )
    column_sum = column_sum.transpose(1, 0, 2)
    block_sum = block_sum[:CHUNK]
    return (
        output[None],
        grad_tokens[None],
        grad_states[None, 5:8],
        grad_states[0:1],
        small_sum[0, :rows],
        from_lanes(column_sum[:, :, :WIDTH]).reshape(rows, -1),
        from_lanes(column_sum[:, :, WIDTH:]).reshape(rows, -1),
        small_sum[2:6, :CHUNK],
        small_sum[6, :CHUNK],
        from_lanes(block_sum[:, : 2 * LANES]),
        from_lanes(block_sum[:, 2 * LANES :]),
        out_sum[:CHUNK],
        small_sum[1, :rows],
        gate_sum.transpose(1, 0, 2).reshape(rows, -1),
        up_sum.transpose(1, 0, 2).reshape(rows, -1),
        down_sum,
    )


def solution(mesh):
    sizes = (mesh.shape["wide"], mesh.shape["narrow"])
    return jax.shard_map(
        halves if sizes == (2 * COLUMNS, 2 * LOWS) else shards,
        mesh=mesh,
        in_specs=(
            P(("wide", "narrow"), None, None),
            P(("wide", "narrow"), None, None),
            P(("wide", "narrow"), None),
            P(("wide", "narrow")),
            P(("wide", "narrow")),
            P(("wide", "narrow"), None),
            P(("wide", "narrow"), None),
            P(None, ("wide", "narrow")),
            P(("wide", "narrow")),
            P(("wide", "narrow"), None),
            P(("wide", "narrow"), None),
            P(("wide", "narrow"), None),
            P(("wide", "narrow")),
            P(("wide", "narrow"), None),
            P(("wide", "narrow"), None),
            P(("wide", "narrow"), None),
            P(("wide", "narrow"), None, None),
        ),
        out_specs=(
            P(("wide", "narrow"), None, None),
            P(("wide", "narrow"), None, None),
            P(("wide", "narrow"), None, None),
            P(("wide", "narrow"), None),
            P(("wide", "narrow")),
            P(("wide", "narrow"), None),
            P(("wide", "narrow"), None),
            P(None, ("wide", "narrow")),
            P(("wide", "narrow")),
            P(("wide", "narrow"), None),
            P(("wide", "narrow"), None),
            P(("wide", "narrow"), None),
            P(("wide", "narrow")),
            P(("wide", "narrow"), None),
            P(("wide", "narrow"), None),
            P(("wide", "narrow"), None),
        ),
        check_vma=False,
    )
```

```python
import functools
import itertools
from functools import reduce

import jax
import jax.numpy as jnp
from jax import lax
from jax.experimental import pallas as pl
from jax.experimental.pallas import tpu as pltpu
from jax.sharding import PartitionSpec as P

BLOCKS = 16
BLK = 176
SCAN_BLOCK = 16


epsilon = 1e-06
contract_rows = (((0,), (0,)), ((), ()))
contract_cols = (((1,), (1,)), ((), ()))


def plain_product(left_side, right_side):
    return jnp.dot(left_side, right_side, preferred_element_type=jnp.float32)


def rows_product(left_side, right_side):
    return lax.dot_general(left_side, right_side, contract_rows, preferred_element_type=jnp.float32)


def cols_product(left_side, right_side):
    return lax.dot_general(left_side, right_side, contract_cols, preferred_element_type=jnp.float32)


def norm_scale(values, gain_vec):
    return (
        values * lax.rsqrt(jnp.mean(values * values, axis=-1, keepdims=True) + epsilon) * gain_vec
    )


def conv_apply(values, history, kernel):
    joined = jnp.concatenate([history, values], axis=0)
    length = values.shape[0]
    kernel_taps = kernel.shape[0]
    result = jnp.zeros_like(values)
    for offset in range(kernel_taps):
        first_row = kernel_taps - 1 - offset
        result = result + kernel[offset] * joined[first_row : first_row + length]
    return result


def block_mix(values, matrix):
    length = values.shape[0]
    mixed_out = jnp.einsum(
        "tki,kij->tkj",
        values.reshape(length, BLOCKS, BLK),
        matrix.reshape(BLOCKS, BLK, BLK),
        preferred_element_type=jnp.float32,
    )
    return mixed_out.reshape(length, BLOCKS * BLK)


def block_back(grad_logits, matrix):
    length = grad_logits.shape[0]
    spread_back = jnp.einsum(
        "tkj,kij->tki",
        grad_logits.reshape(length, BLOCKS, BLK),
        matrix.reshape(BLOCKS, BLK, BLK),
        preferred_element_type=jnp.float32,
    )
    return spread_back.reshape(length, BLOCKS * BLK)


def block_grad(values, grad_logits):
    length = values.shape[0]
    summed = jnp.einsum(
        "tki,tkj->kij",
        values.reshape(length, BLOCKS, BLK),
        grad_logits.reshape(length, BLOCKS, BLK),
        preferred_element_type=jnp.float32,
    )
    return summed.reshape(BLOCKS * BLK, BLK)


def gate_apply(recur_logits, input_logits, conv_float, decay_float):
    log_decay = -8.0 * jax.nn.sigmoid(recur_logits) * jax.nn.softplus(-decay_float)
    scan_in = jnp.sqrt(-jnp.expm1(2.0 * log_decay)) * jax.nn.sigmoid(input_logits) * conv_float
    return (log_decay, scan_in)


def branch_apply(hidden, gate_logits):
    return hidden * jax.nn.gelu(gate_logits)


def mlp_apply(gate_part, up_part):
    return jax.nn.gelu(gate_part) * up_part


def block_scan(log_decay, scan_in, initial):
    length, channels = scan_in.shape
    block_count = length // SCAN_BLOCK
    positions = jnp.arange(SCAN_BLOCK)
    causal = (positions[:, None] >= positions[None, :])[:, :, None]

    def advance(carried, pieces):
        decay_piece, input_piece = pieces
        cumulative = jnp.cumsum(decay_piece, axis=0)
        spread = jnp.where(causal, cumulative[:, None, :] - cumulative[None, :, :], 0.0)
        factors = jnp.where(causal, jnp.exp(spread), 0.0)
        states = jnp.sum(factors * input_piece[None, :, :], axis=1) + jnp.exp(cumulative) * carried
        return (states[-1], states)

    last_state, states = lax.scan(
        advance,
        initial,
        (
            log_decay.reshape(block_count, SCAN_BLOCK, channels),
            scan_in.reshape(block_count, SCAN_BLOCK, channels),
        ),
    )
    return states.reshape(length, channels)


def scan_back(log_decay, hidden, initial, grad_hidden):
    following = jnp.concatenate([log_decay[1:], jnp.zeros_like(log_decay[:1])], axis=0)
    carried = block_scan(following[::-1], grad_hidden[::-1], jnp.zeros_like(initial))[::-1]
    previous = jnp.concatenate([initial[None], hidden[:-1]], axis=0)
    grad_log_decay = carried * jnp.exp(log_decay) * previous
    grad_initial = jnp.exp(log_decay[0]) * carried[0]
    return (grad_log_decay, carried, grad_initial)


def mixer_forward(tokens_row, history, initial, keep_row, mixer):
    (
        gain_vec,
        proj_input,
        proj_gate,
        conv_kernel,
        decay_param,
        gate_recur,
        gate_input,
        proj_output,
    ) = mixer
    values = tokens_row.astype(jnp.float32)
    normed_one = norm_scale(values, gain_vec.astype(jnp.float32)).astype(jnp.bfloat16)
    branch_in = plain_product(normed_one, proj_input)
    gate_logits = plain_product(normed_one, proj_gate)
    history_kept = history * keep_row
    kernel_float = conv_kernel.astype(jnp.float32)
    conv_out = conv_apply(branch_in, history_kept, kernel_float).astype(jnp.bfloat16)
    recur_logits = block_mix(conv_out, gate_recur)
    input_logits = block_mix(conv_out, gate_input)
    decay_float = decay_param.astype(jnp.float32)
    conv_float = conv_out.astype(jnp.float32)
    log_decay, scan_in = gate_apply(recur_logits, input_logits, conv_float, decay_float)
    initial_kept = initial * keep_row
    hidden = block_scan(log_decay, scan_in, initial_kept)
    mixed_out = branch_apply(hidden, gate_logits).astype(jnp.bfloat16)
    after_mixer = values + plain_product(mixed_out, proj_output)
    kept = (
        values,
        normed_one,
        branch_in,
        gate_logits,
        history_kept,
        kernel_float,
        conv_out,
        conv_float,
        recur_logits,
        input_logits,
        decay_float,
        log_decay,
        initial_kept,
        hidden,
        mixed_out,
    )
    return (after_mixer, kept)


def mlp_forward(after_mixer, mlp):
    gain_vec, mlp_gate, mlp_up, mlp_down = mlp
    normed_two = norm_scale(after_mixer, gain_vec.astype(jnp.float32)).astype(jnp.bfloat16)
    gate_part = plain_product(normed_two, mlp_gate)
    up_part = plain_product(normed_two, mlp_up)
    activated = mlp_apply(gate_part, up_part).astype(jnp.bfloat16)
    result = after_mixer + plain_product(activated, mlp_down)
    return (result, (after_mixer, normed_two, gate_part, up_part, activated))


def mlp_backward(grad_result, mlp, kept):
    gain_vec, mlp_gate, mlp_up, mlp_down = mlp
    after_mixer, normed_two, gate_part, up_part, activated = kept
    grad_activated = cols_product(grad_result, mlp_down)
    grad_down = rows_product(activated, grad_result)
    unused, mlp_pull = jax.vjp(mlp_apply, gate_part, up_part)
    grad_gate_part, grad_up_part = mlp_pull(grad_activated)
    grad_gate_part = grad_gate_part.astype(jnp.bfloat16)
    grad_up_part = grad_up_part.astype(jnp.bfloat16)
    grad_normed = cols_product(grad_gate_part, mlp_gate) + cols_product(grad_up_part, mlp_up)
    grad_mlp_gate = rows_product(normed_two, grad_gate_part)
    grad_mlp_up = rows_product(normed_two, grad_up_part)
    unused, norm_pull = jax.vjp(norm_scale, after_mixer, gain_vec.astype(jnp.float32))
    grad_values, grad_gain = norm_pull(grad_normed)
    grad_after = grad_result.astype(jnp.float32) + grad_values
    return (grad_after, (grad_gain, grad_mlp_gate, grad_mlp_up, grad_down))


def mixer_backward(grad_after, mixer, kept, keep_row):
    (
        gain_vec,
        proj_input,
        proj_gate,
        conv_kernel,
        decay_param,
        gate_recur,
        gate_input,
        proj_output,
    ) = mixer
    (
        values,
        normed_one,
        branch_in,
        gate_logits,
        history_kept,
        kernel_float,
        conv_out,
        conv_float,
        recur_logits,
        input_logits,
        decay_float,
        log_decay,
        initial_kept,
        hidden,
        mixed_out,
    ) = kept
    grad_mixed = grad_after.astype(jnp.bfloat16)
    grad_proj_output = rows_product(mixed_out, grad_mixed)
    grad_branch = cols_product(grad_mixed, proj_output)
    unused, branch_pull = jax.vjp(branch_apply, hidden, gate_logits)
    grad_hidden, grad_gate_logits = branch_pull(grad_branch)
    grad_gate_logits = grad_gate_logits.astype(jnp.bfloat16)
    grad_log_decay, grad_scan_in, grad_initial = scan_back(
        log_decay, hidden, initial_kept, grad_hidden
    )
    unused, gate_pull = jax.vjp(gate_apply, recur_logits, input_logits, conv_float, decay_float)
    grad_recur_logits, grad_input_logits, grad_conv, grad_decay = gate_pull(
        (grad_log_decay, grad_scan_in)
    )
    grad_recur_logits = grad_recur_logits.astype(jnp.bfloat16)
    grad_input_logits = grad_input_logits.astype(jnp.bfloat16)
    grad_gate_recur = block_grad(conv_out, grad_recur_logits)
    grad_gate_input = block_grad(conv_out, grad_input_logits)
    grad_conv = (
        grad_conv
        + block_back(grad_recur_logits, gate_recur)
        + block_back(grad_input_logits, gate_input)
    )
    unused, conv_pull = jax.vjp(conv_apply, branch_in, history_kept, kernel_float)
    grad_branch_in, grad_history, grad_kernel = conv_pull(grad_conv)
    grad_branch_low = grad_branch_in.astype(jnp.bfloat16)
    grad_proj_input = rows_product(normed_one, grad_branch_low)
    grad_proj_gate = rows_product(normed_one, grad_gate_logits)
    grad_normed = cols_product(grad_branch_low, proj_input) + cols_product(
        grad_gate_logits, proj_gate
    )
    unused, norm_pull = jax.vjp(norm_scale, values, gain_vec.astype(jnp.float32))
    grad_values, grad_gain = norm_pull(grad_normed)
    grad_tokens = (grad_after + grad_values).astype(jnp.bfloat16)
    weight_terms = (
        grad_gain,
        grad_proj_input,
        grad_proj_gate,
        grad_kernel,
        grad_decay,
        grad_gate_recur,
        grad_gate_input,
        grad_proj_output,
    )
    return (grad_tokens, grad_history * keep_row, grad_initial * keep_row, weight_terms)


def add_terms(first_terms, second_terms):
    return tuple(
        (left_side + right_side for left_side, right_side in zip(first_terms, second_terms))
    )


def shards(
    tokens,
    conv_state,
    recur_state,
    fresh_rows,
    gain_mixer,
    proj_input,
    proj_gate,
    conv_kernel,
    decay_param,
    gate_recur,
    gate_input,
    proj_output,
    gain_mlp,
    mlp_gate,
    mlp_up,
    mlp_down,
    cotangent,
):
    mixer_full = (
        lax.all_gather(gain_mixer, ("wide", "narrow"), axis=0, tiled=True),
        lax.all_gather(proj_input, ("wide", "narrow"), axis=0, tiled=True),
        lax.all_gather(proj_gate, ("wide", "narrow"), axis=0, tiled=True),
        lax.all_gather(conv_kernel, ("wide", "narrow"), axis=1, tiled=True),
        lax.all_gather(decay_param, ("wide", "narrow"), axis=0, tiled=True),
        lax.all_gather(gate_recur, ("wide", "narrow"), axis=0, tiled=True),
        lax.all_gather(gate_input, ("wide", "narrow"), axis=0, tiled=True),
        lax.all_gather(proj_output, ("wide", "narrow"), axis=0, tiled=True),
    )
    mlp_full = (
        lax.all_gather(gain_mlp, ("wide", "narrow"), axis=0, tiled=True),
        lax.all_gather(mlp_gate, ("wide", "narrow"), axis=0, tiled=True),
        lax.all_gather(mlp_up, ("wide", "narrow"), axis=0, tiled=True),
        lax.all_gather(mlp_down, ("wide", "narrow"), axis=0, tiled=True),
    )
    keep_rows = (1 - fresh_rows).astype(jnp.float32)
    stored = []
    row_index = 0
    after_mixer, mixer_kept = mixer_forward(
        tokens[row_index],
        conv_state[row_index],
        recur_state[row_index],
        keep_rows[row_index],
        mixer_full,
    )
    result, mlp_kept = mlp_forward(after_mixer, mlp_full)
    outputs = [result.astype(jnp.bfloat16)]
    stored.append((mixer_kept, mlp_kept))
    mixer_back = (
        lax.all_gather(gain_mixer, ("wide", "narrow"), axis=0, tiled=True),
        lax.all_gather(proj_input, ("wide", "narrow"), axis=0, tiled=True),
        lax.all_gather(proj_gate, ("wide", "narrow"), axis=0, tiled=True),
        lax.all_gather(conv_kernel, ("wide", "narrow"), axis=1, tiled=True),
        lax.all_gather(decay_param, ("wide", "narrow"), axis=0, tiled=True),
        lax.all_gather(gate_recur, ("wide", "narrow"), axis=0, tiled=True),
        lax.all_gather(gate_input, ("wide", "narrow"), axis=0, tiled=True),
        lax.all_gather(proj_output, ("wide", "narrow"), axis=0, tiled=True),
    )
    mlp_back = (
        lax.all_gather(gain_mlp, ("wide", "narrow"), axis=0, tiled=True),
        lax.all_gather(mlp_gate, ("wide", "narrow"), axis=0, tiled=True),
        lax.all_gather(mlp_up, ("wide", "narrow"), axis=0, tiled=True),
        lax.all_gather(mlp_down, ("wide", "narrow"), axis=0, tiled=True),
    )
    stored = []
    row_index = 0
    after_mixer, mixer_kept = mixer_forward(
        tokens[row_index],
        conv_state[row_index],
        recur_state[row_index],
        keep_rows[row_index],
        mixer_back,
    )
    unused, mlp_kept = mlp_forward(after_mixer, mlp_back)
    stored.append((mixer_kept, mlp_kept))
    row_index = 0
    grad_after, row_terms = mlp_backward(cotangent[row_index], mlp_back, stored[row_index][1])
    after_grads = [grad_after]
    mlp_terms = [row_terms]
    mlp_total = reduce(add_terms, mlp_terms)
    mlp_sums = (
        lax.psum_scatter(mlp_total[0], ("wide", "narrow"), scatter_dimension=0, tiled=True),
        lax.psum_scatter(mlp_total[1], ("wide", "narrow"), scatter_dimension=0, tiled=True),
        lax.psum_scatter(mlp_total[2], ("wide", "narrow"), scatter_dimension=0, tiled=True),
        lax.psum_scatter(mlp_total[3], ("wide", "narrow"), scatter_dimension=0, tiled=True),
    )
    row_index = 0
    grad_tokens, grad_history, grad_initial, row_terms = mixer_backward(
        after_grads[row_index], mixer_back, stored[row_index][0], keep_rows[row_index]
    )
    token_grads = [grad_tokens]
    history_grads = [grad_history]
    initial_grads = [grad_initial]
    mixer_terms = [row_terms]
    mixer_total = reduce(add_terms, mixer_terms)
    mixer_sums = (
        lax.psum_scatter(mixer_total[0], ("wide", "narrow"), scatter_dimension=0, tiled=True),
        lax.psum_scatter(mixer_total[1], ("wide", "narrow"), scatter_dimension=0, tiled=True),
        lax.psum_scatter(mixer_total[2], ("wide", "narrow"), scatter_dimension=0, tiled=True),
        lax.psum_scatter(mixer_total[3], ("wide", "narrow"), scatter_dimension=1, tiled=True),
        lax.psum_scatter(mixer_total[4], ("wide", "narrow"), scatter_dimension=0, tiled=True),
        lax.psum_scatter(mixer_total[5], ("wide", "narrow"), scatter_dimension=0, tiled=True),
        lax.psum_scatter(mixer_total[6], ("wide", "narrow"), scatter_dimension=0, tiled=True),
        lax.psum_scatter(mixer_total[7], ("wide", "narrow"), scatter_dimension=0, tiled=True),
    )
    return (
        jnp.stack(outputs),
        jnp.stack(token_grads),
        jnp.stack(history_grads),
        jnp.stack(initial_grads),
        mixer_sums[0],
        mixer_sums[1],
        mixer_sums[2],
        mixer_sums[3],
        mixer_sums[4],
        mixer_sums[5],
        mixer_sums[6],
        mixer_sums[7],
        mlp_sums[0],
        mlp_sums[1],
        mlp_sums[2],
        mlp_sums[3],
    )


COLUMNS = 4
LOWS = 2
PARTS = COLUMNS * LOWS
TOK = 128
CHUNK = 88
LANES = 96
WIDTH = 4 * LANES
SPAN = PARTS * TOK
MESH = pl.DeviceIdType.MESH
VMEM_BYTES = 63 * 1024 * 1024
low_type = jnp.bfloat16
full_type = jnp.float32


class Place:
    def __init__(self):
        wide = lax.axis_index("wide")
        self.z = lax.axis_index("narrow")
        self.column, self.core = wide // 2, wide % 2
        self.half, self.low = self.z // 2, self.z % 2
        self.part = self.column * 2 + self.low
        self.index = wide * 4 + self.z
        self.own = (self.column // 2, self.column % 2, self.low)

    def shifted(self, by_y, by_x, by_low, by_half):
        column = (self.column // 2 + by_y) % 2 * 2 + (self.column % 2 + by_x) % 2
        low, half = (self.low + by_low) % 2, (self.half + by_half) % 2
        return (column, low, half)

    def neighbour(self, axis):
        y, x, low = (1 - at if axis == here else at for here, at in enumerate(self.own))
        return (y * 4 + x * 2 + self.core, self.half * 2 + low)

    def cube(self, fixed, other=None):
        return tuple(
            1 - at if axis == other else at if axis in fixed else slice(None)
            for axis, at in enumerate(self.own)
        )

    def sibling(self):
        return (self.column * 2 + 1 - self.core, self.z)


def greet_all(place):
    barrier = pltpu.get_barrier_semaphore()

    @pl.loop(1, 32)
    def _(step):
        other = (place.index + step) % 32
        pl.semaphore_signal(
            barrier, inc=1, device_id=(other // 4, other % 4), device_id_type=MESH
        )

    pl.semaphore_wait(barrier, 31)


def remote(source, target, send, receive, device):
    return pltpu.make_async_remote_copy(
        src_ref=source,
        dst_ref=target,
        send_sem=send,
        recv_sem=receive,
        device_id=device,
        device_id_type=MESH,
    )


def await_bytes(view, semaphore):
    pltpu.make_async_copy(view, view, semaphore).wait()


class Spread:
    def __init__(self, pick):
        self.pick = pick

    def start(self, place, source, target, sems):
        self.copies = []
        slot = target.at[place.column, place.core, place.z]
        for shift in itertools.product(range(2), repeat=4):
            column, low, half = place.shifted(*shift)
            block = self.pick(source, column * 2 + low)
            if any(shift):
                copy = remote(
                    block, slot, sems.at[0], sems.at[1], (column * 2 + place.core, half * 2 + low)
                )
                copy.start()
                self.copies.append(copy)
            else:
                pltpu.make_async_copy(block, slot, sems.at[1]).start()

    def relay(self, place, source, target, sems):
        mine = target.at[:, place.core]
        await_bytes(mine, sems.at[1])
        self.passed = remote(mine, mine, sems.at[2], sems.at[3], place.sibling())
        self.passed.start()

    def finish(self, place, source, target, sems):
        self.passed.wait()
        for copy in self.copies:
            copy.wait_send()


class RowSpread:
    def start(self, place, source, target, sems):
        self.copies = []
        slot = target.at[place.half, place.low]
        for half in range(2):
            copy = remote(
                source,
                slot,
                sems.at[0],
                sems.at[1],
                (place.column * 2 + place.low, half * 2 + place.core),
            )
            own = (place.low == place.core) & (place.half == half)

            @pl.when(own)
            def _():
                pltpu.make_async_copy(source, slot, sems.at[1]).start()

            @pl.when(jnp.logical_not(own))
            def _():
                copy.start()

            self.copies.append((own, copy))

    def relay(self, place, source, target, sems):
        mine = target.at[:, place.core]
        await_bytes(mine, sems.at[1])
        self.passed = remote(mine, mine, sems.at[2], sems.at[3], place.sibling())
        self.passed.start()

    def finish(self, place, source, target, sems):
        self.passed.wait()
        for own, copy in self.copies:

            @pl.when(jnp.logical_not(own))
            def _():
                copy.wait_send()


class Peers:
    def __init__(self, pick):
        self.pick = pick

    def start(self, place, source, target, sems):
        self.copies = []
        slot = target.at[place.part]
        for shift in itertools.product(range(2), repeat=3):
            column, low, half = place.shifted(*shift, 0)
            block = self.pick(source, column * 2 + low)
            if any(shift):
                copy = remote(
                    block, slot, sems.at[0], sems.at[1], (column * 2 + place.core, half * 2 + low)
                )
                copy.start()
                self.copies.append(copy)
            else:
                pltpu.make_async_copy(block, slot, sems.at[1]).start()

    def relay(self, place, source, target, sems):
        pass

    def finish(self, place, source, target, sems):
        await_bytes(target, sems.at[1])
        for copy in self.copies:
            copy.wait_send()


class Swap:
    def start(self, place, source, target, sems):
        self.copy = remote(
            source.at[:, 1 - place.core], target, sems.at[0], sems.at[1], place.sibling()
        )
        self.copy.start()

    def relay(self, place, source, target, sems):
        pass

    def finish(self, place, source, target, sems):
        self.copy.wait()


class Owners:
    def start(self, place, source, target, sems):
        self.copies = []
        slot = target.at[place.half, place.part]
        for shift in itertools.product(range(2), repeat=4):
            column, low, half = place.shifted(*shift)
            z = half * 2 + low
            block = source.at[column, place.core, z]
            if any(shift):
                copy = remote(
                    block, slot, sems.at[0], sems.at[1], (column * 2 + place.core, z)
                )
                copy.start()
                self.copies.append(copy)
            else:
                pltpu.make_async_copy(block, slot, sems.at[1]).start()

    def relay(self, place, source, target, sems):
        pass

    def finish(self, place, source, target, sems):
        await_bytes(target, sems.at[1])
        for copy in self.copies:
            copy.wait_send()


class RowOwners:
    def start(self, place, source, target, sems):
        self.copies = []
        slot = target.at[place.half]
        for half in range(2):
            block = source.at[half, place.core]
            copy = remote(
                block,
                slot,
                sems.at[0],
                sems.at[1],
                (place.column * 2 + place.low, half * 2 + place.core),
            )
            own = (place.low == place.core) & (place.half == half)

            @pl.when(own)
            def _():
                pltpu.make_async_copy(block, slot, sems.at[1]).start()

            @pl.when(jnp.logical_not(own))
            def _():
                copy.start()

            self.copies.append((own, copy))

    def relay(self, place, source, target, sems):
        pass

    def finish(self, place, source, target, sems):
        await_bytes(target, sems.at[1])
        for own, copy in self.copies:

            @pl.when(jnp.logical_not(own))
            def _():
                copy.wait_send()


class Semaphores:
    def __init__(self, array):
        self.array, self.used = array, 0

    def take(self, count):
        taken = self.array.at[pl.ds(self.used, count)]
        self.used += count
        return taken


ORDERS = ((2, 0, 1), (2, 1, 0), (0, 2, 1), (1, 2, 0))
ROUTES = len(ORDERS)


def cuts(width):
    part = width // ROUTES
    return [pl.ds(route * part, part) for route in range(ROUTES)]


class CubeGather:
    def __init__(self, place, buffer, semaphores):
        self.place, self.buffer, self.copies = place, buffer, []
        self.sems = semaphores.take(6 * ROUTES)

    def step(self, number):
        rows = pl.ds(0, self.buffer.shape[3])
        for order, cut in enumerate(cuts(self.buffer.shape[4])):
            axes = ORDERS[order]
            if number > 0:
                self.copies[ROUTES * (number - 1) + order].wait_recv()
            region = self.buffer.at[self.place.cube(axes[number:]) + (rows, cut)]
            index = ROUTES * number + order
            copy = remote(
                region,
                region,
                self.sems.at[index],
                self.sems.at[3 * ROUTES + index],
                self.place.neighbour(axes[number]),
            )
            copy.start()
            self.copies.append(copy)

    def finish(self):
        for copy in self.copies[2 * ROUTES :]:
            copy.wait_recv()
        for copy in self.copies:
            copy.wait_send()


class CubeSum:
    def __init__(self, place, blocks, landings, semaphores):
        self.place, self.blocks, self.landings, self.copies = place, blocks, landings, []
        self.sems = semaphores.take(6 * ROUTES)

    def send(self, number, order, cut):
        axes = ORDERS[order][::-1]
        index = ROUTES * number + order
        rows = pl.ds(0, TOK)
        landing = self.landings[number]
        copy = remote(
            self.blocks.at[self.place.cube(axes[:number], axes[number]) + (rows, cut)],
            landing.at[(slice(None),) * (2 - number) + (rows, cut)],
            self.sems.at[index],
            self.sems.at[3 * ROUTES + index],
            self.place.neighbour(axes[number]),
        )
        copy.start()
        self.copies.append(copy)

    def start(self):
        for order, cut in enumerate(cuts(self.blocks.shape[4])):
            self.send(0, order, cut)

    def step(self, number, result=None):
        for order, cut in enumerate(cuts(self.blocks.shape[4])):
            axes = ORDERS[order][::-1]
            self.copies[ROUTES * number + order].wait_recv()
            landing = self.landings[number]
            for picks in itertools.product(range(2), repeat=2 - number):
                chosen = iter(picks)
                index = tuple(
                    self.place.own[axis] if axis in axes[: number + 1] else next(chosen)
                    for axis in range(3)
                )

                @pl.loop(0, TOK // 32)
                def _(block):
                    rows = pl.ds(pl.multiple_of(block * 32, 32), 32)
                    total = self.blocks[index + (rows, cut)].astype(full_type) + landing[
                        picks + (rows, cut)
                    ].astype(full_type)
                    if number < 2:
                        self.blocks[index + (rows, cut)] = total.astype(low_type)
                    else:
                        result[rows, cut] = total

            if number < 2:
                self.send(number + 1, order, cut)

    def finish(self):
        for copy in self.copies:
            copy.wait_send()


class Move:
    def __init__(self, place, plan, source, target, semaphores):
        self.plan, self.arguments = plan, (place, source, target, semaphores.take(4))

    def start(self):
        self.plan.start(*self.arguments)

    def relay(self):
        self.plan.relay(*self.arguments)

    def finish(self):
        self.plan.finish(*self.arguments)


class Local:
    def __init__(self, semaphores):
        self.semaphores, self.copies = semaphores, []

    def start(self, source, target):
        copy = pltpu.make_async_copy(source, target, self.semaphores.take(1).at[0])
        copy.start()
        self.copies.append(copy)
        return copy

    def finish(self):
        for copy in self.copies:
            copy.wait()


def whole(source, part):
    return source


def by_part(source, part):
    return source.at[part]


def by_columns(source, part):
    width = source.shape[1] // PARTS
    return source.at[:, pl.ds(pl.multiple_of(part * width, 128), width)]


def row_block(row):
    return pl.ds(pl.multiple_of(row * TOK, TOK), TOK)


def small_expm1(values):
    near = values * (
        1.0
        + values
        * (0.5 + values * (1 / 6 + values * (1 / 24 + values * (1 / 120 + values * (1 / 720)))))
    )
    return jnp.where(values > -0.25, near, jnp.exp(values) - 1.0)


def gelu_parts(values):
    scale = 0.7978845608028654
    bent = jnp.tanh(scale * (values + 0.044715 * values * values * values))
    slope = 0.5 * (1.0 + bent) + 0.5 * values * (1.0 - bent * bent) * scale * (
        1.0 + 3 * 0.044715 * values * values
    )
    return (0.5 * values * (1.0 + bent), slope)


def put(array, rows, values):
    for piece in range(WIDTH // 128):
        array[piece, rows, :] = values[:, piece * 128 : (piece + 1) * 128]


def take(array, rows):
    return jnp.concatenate([array[piece, rows, :] for piece in range(WIDTH // 128)], axis=1)


def taps_of(aux):
    return [aux[tap : tap + 1, :] for tap in range(4)]


def placed_sum(gathered, place, row):
    owners = [
        gathered[place.part // 2, place.part % 2, z, row : row + 1, :].astype(full_type)
        for z in range(4)
    ]
    return owners[0] + owners[1] + owners[2] + owners[3]


def placed_gain(gathered, row):
    pieces = []
    for column, core, pair in itertools.product(range(COLUMNS), range(2), range(2)):
        both = [
            gathered[column, core, 2 * pair + odd, row : row + 1, 0:128].astype(full_type)
            for odd in range(2)
        ]
        pieces.append(both[0] + both[1])
    return jnp.concatenate(pieces, axis=1)


def scaled_norm(values, gain):
    scale = lax.rsqrt(jnp.mean(values * values, axis=1, keepdims=True) + epsilon)
    return values * scale * gain


def whole_block(place, row):
    return (row // 4, row // 2 % 2, row % 2)


def add_swapped(array, landing, core):
    rows, columns = array.shape[-2:]
    inner = array.shape[2] if len(array.shape) == 5 else 1
    outer = array.shape[0]
    chunk = 32 if columns > 1024 and rows % 32 == 0 else 16 if rows % 16 == 0 else 8

    @pl.loop(0, outer * inner * (rows // chunk))
    def _(step):
        part = pl.ds(pl.multiple_of(step % (rows // chunk) * chunk, chunk), chunk)
        first = step // (rows // chunk)
        if len(array.shape) == 5:
            here, there = (first // inner, core, first % inner, part), (first // inner, first % inner, part)
        else:
            here, there = (first, core, part), (first, part)
        total = array[here].astype(full_type) + landing[there].astype(full_type)
        array[here] = total.astype(array.dtype)


def norm_back(values, gain, grad):
    scale = lax.rsqrt(jnp.mean(values * values, axis=1, keepdims=True) + epsilon)
    inner = grad * gain
    along = jnp.mean(inner * values, axis=1, keepdims=True)
    return (scale * inner - values * (scale * scale * scale * along), grad * values * scale)


def block_kernel(
    tokens,
    small,
    states,
    columns,
    gates,
    out_rows,
    mlp_gate,
    mlp_up,
    mlp_down,
    cotangent,
    output,
    grad_tokens,
    states_back,
    small_back,
    columns_back,
    gate_back,
    up_back,
    blocks_back,
    rows_back,
    down_back,
    normed_kept,
    cube_one,
    cube_two,
    cube_three,
    blocks,
    landing_one,
    landing_two,
    landing_three,
    small_all,
    states_all,
    columns_all,
    gates_all,
    rows_all,
    gate_all,
    up_all,
    down_all,
    pre,
    conv,
    hidden,
    mixed,
    decays,
    carries,
    padded,
    after,
    grad,
    summed,
    aux,
    gains,
    grad_gains,
    grad_aux,
    active,
    grad_gate,
    grad_up,
    down_landing,
    grad_pre,
    grad_blocks,
    blocks_low,
    blocks_landing,
    grad_states,
    small_terms,
    small_landing,
    sems,
    free,
):
    place = Place()
    semaphores = Semaphores(sems)
    local = Local(semaphores)
    width = tokens.shape[1]
    hidden_units = gate_all.shape[-1]
    tokens_all = cube_one
    normed = cube_two
    two_all = cube_three

    def move(plan, source, target):
        return Move(place, plan, source, target, semaphores)

    def whole_matrix(array):
        return array[...].reshape(-1, array.shape[-1])

    own_tokens = tokens_all.at[place.own]
    load = pltpu.make_async_copy(tokens, own_tokens, semaphores.take(1).at[0])
    load.start()
    greet_all(place)
    load.wait()
    tokens_gather = CubeGather(place, tokens_all, semaphores)
    tokens_gather.step(0)
    small_move = move(Spread(whole), small, small_all)
    small_move.start()
    states_move = move(Peers(by_part), states, states_all)
    states_move.start()
    columns_move = move(Spread(by_part), columns, columns_all)
    columns_move.start()
    gates_move = move(RowSpread(), gates, gates_all)
    gates_move.start()
    rows_move = move(RowSpread(), out_rows, rows_all)
    rows_move.start()
    tokens_gather.step(1)
    small_move.relay()
    tokens_gather.step(2)
    late = [
        move(Spread(by_columns), mlp_gate, gate_all),
        move(Spread(by_columns), mlp_up, up_all),
        move(RowSpread(), mlp_down, down_all),
    ]
    for item in late:
        item.start()
    small_move.finish()
    for tap in range(5):
        aux[tap : tap + 1, :] = placed_sum(small_all, place, tap)
    decay_row = aux[4:5, :]
    aux[4:5, :] = jnp.maximum(-decay_row, 0.0) + jnp.log1p(jnp.exp(-jnp.abs(decay_row)))
    aux[5:6, :] = jax.nn.sigmoid(-decay_row)
    aux[6:8, :] = jnp.zeros((2, WIDTH), full_type)
    gains[0:1, :] = placed_gain(small_all, 5)
    gains[1:2, :] = placed_gain(small_all, 6)
    tokens_gather.finish()

    @pl.loop(0, SPAN // 32)
    def _(step):
        rows = pl.ds(pl.multiple_of(step % 4 * 32, 32), 32)
        index = whole_block(place, step // 4) + (rows,)
        normed[index] = scaled_norm(tokens_all[index].astype(full_type), gains[0:1, :]).astype(
            low_type
        )

    keep_normed = local.start(normed, normed_kept)
    columns_move.relay()
    gates_move.relay()
    rows_move.relay()
    columns_move.finish()

    @pl.loop(0, 4)
    def _(step):
        rows = pl.ds(pl.multiple_of(step * 256, 256), 256)
        pre[rows, :] = jnp.dot(
            normed[step // 2, step % 2].reshape(256, width),
            whole_matrix(columns_all),
            preferred_element_type=full_type,
        )

    gates_move.finish()
    states_move.finish()
    taps = taps_of(aux)
    soft, slope = aux[4:5, :], aux[5:6, :]

    def gate_logits(low):
        both = jnp.dot(low, whole_matrix(gates_all), preferred_element_type=full_type)
        return (jax.nn.sigmoid(both[:, 0:WIDTH]), jax.nn.sigmoid(both[:, WIDTH:]))

    @pl.loop(0, PARTS)
    def _(row):
        rows = row_block(row)
        padded[0:8, :] = states_all[row]
        padded[8 : 8 + TOK, :] = pre[rows, 0:WIDTH]
        total = taps[0] * padded[8 : 8 + TOK, :]
        for tap in range(1, 4):
            total = total + taps[tap] * padded[8 - tap : 8 - tap + TOK, :]
        low = total.astype(low_type)
        conv[rows, :] = low
        recur, gate = gate_logits(low)
        log_decay = -8.0 * recur * soft
        scale = jnp.sqrt(-small_expm1(2.0 * log_decay))
        put(carries, rows, scale * gate * low.astype(full_type))
        put(decays, rows, jnp.exp(log_decay))

    def advance(time, carried):
        across = pl.ds(time, PARTS, stride=TOK)
        carried = [
            decays[piece, across, :] * before + carries[piece, across, :]
            for piece, before in enumerate(carried)
        ]
        for piece, now in enumerate(carried):
            hidden[piece, across, :] = now
        return carried

    initial = states_all[:, 0, :]
    initial = [initial[:, piece * 128 : (piece + 1) * 128] for piece in range(WIDTH // 128)]
    lax.fori_loop(0, TOK, advance, initial, unroll=8)
    rows_move.finish()

    @pl.loop(0, PARTS)
    def _(row):
        rows = row_block(row)
        gated, _ = gelu_parts(pre[rows, WIDTH:])
        low = (take(hidden, rows) * gated).astype(low_type)
        mixed[rows, :] = low
        blocks[whole_block(place, row)] = jnp.dot(
            low, whole_matrix(rows_all), preferred_element_type=full_type
        ).astype(low_type)

    landings = (landing_one, landing_two, landing_three)
    mixer_sum = CubeSum(place, blocks, landings, semaphores)
    mixer_sum.start()
    mixer_sum.step(0)
    mixer_sum.step(1)
    mixer_sum.step(2, after)

    @pl.loop(0, TOK // 32)
    def _(step):
        rows = pl.ds(pl.multiple_of(step * 32, 32), 32)
        total = after[rows, :] + tokens_all[place.own + (rows,)].astype(full_type)
        after[rows, :] = total
        two_all[place.own + (rows,)] = scaled_norm(total, gains[1:2, :]).astype(low_type)

    two_gather = CubeGather(place, two_all, semaphores)
    two_gather.step(0)
    cot_all = cube_one
    load_cot = pltpu.make_async_copy(
        cotangent, cot_all.at[place.own], semaphores.take(1).at[0]
    )
    load_cot.start()
    cot_gather = CubeGather(place, cot_all, semaphores)
    load_cot.wait()
    cot_gather.step(0)
    two_gather.step(1)
    cot_gather.step(1)
    two_gather.step(2)
    cot_gather.step(2)
    two_gather.finish()
    mixer_sum.finish()
    for item in late:
        item.relay()
    cot_gather.finish()
    keep_normed.wait()
    for item in late:
        item.finish()

    out_blocks = cube_two

    @pl.loop(0, 4)
    def _(step):
        at = (step // 2, step % 2)
        normed_two = two_all[at].reshape(256, width)
        cot = cot_all[at].reshape(256, width)
        gate_part = jnp.dot(normed_two, whole_matrix(gate_all), preferred_element_type=full_type)
        up_part = jnp.dot(normed_two, whole_matrix(up_all), preferred_element_type=full_type)
        gated, bend = gelu_parts(gate_part)
        low = (gated * up_part).astype(low_type)
        active[step] = low.reshape(4, 64, hidden_units)
        grad_active = cols_product(cot, whole_matrix(down_all))
        to_gate = (grad_active * up_part * bend).astype(low_type)
        to_up = (grad_active * gated).astype(low_type)
        grad_gate[step] = to_gate.reshape(4, 64, hidden_units)
        grad_up[step] = to_up.reshape(4, 64, hidden_units)
        for piece in range(4):
            cut = pl.ds(piece * (width // 4), width // 4)
            part = down_all[:, :, :, cut].reshape(hidden_units, width // 4)
            out_blocks[at + (slice(None), slice(None), cut)] = (
                jnp.dot(low, part, preferred_element_type=full_type)
                .astype(low_type)
                .reshape(2, TOK, width // 4)
            )
            back = cols_product(to_gate, whole_matrix(gate_all.at[piece])) + cols_product(
                to_up, whole_matrix(up_all.at[piece])
            )
            blocks[at + (slice(None), slice(None), cut)] = back.astype(low_type).reshape(
                2, TOK, width // 4
            )

    two_sum = CubeSum(place, blocks, landings, semaphores)
    two_sum.start()

    @pl.loop(0, 8)
    def _(step):
        cut = pl.ds(pl.multiple_of(step * 256, 256), 256)
        side = two_all[:, :, :, :, cut].reshape(SPAN, 256)
        for terms, sums in ((grad_gate, gate_all), (grad_up, up_all)):
            sums[step // 2, step % 2] = (
                rows_product(side, whole_matrix(terms))
                .astype(low_type)
                .reshape(4, 64, hidden_units)
            )

    two_sum.step(0)

    @pl.loop(0, 4)
    def _(step):
        cut = pl.ds(pl.multiple_of(step * 512, 512), 512)
        down_all[:, :, :, cut] = (
            rows_product(whole_matrix(active), cot_all[:, :, :, :, cut].reshape(SPAN, 512))
            .astype(low_type)
            .reshape(2, 2, hidden_units // 4, 512)
        )

    pl.semaphore_signal(
        free.at[0], inc=1, device_id=place.sibling(), device_id_type=MESH
    )
    two_sum.step(1)
    pl.semaphore_wait(free.at[0], 1)
    mlp_swaps = [
        move(Swap(), gate_all, active),
        move(Swap(), up_all, grad_gate),
        move(Swap(), down_all, down_landing),
    ]
    for item in mlp_swaps:
        item.start()
    two_sum.step(2, grad)
    grad_gains[...] = jnp.zeros_like(grad_gains)

    @pl.loop(0, TOK // 32)
    def _(step):
        rows = pl.ds(pl.multiple_of(step * 32, 32), 32)
        back, by_gain = norm_back(after[rows, :], gains[1:2, :], grad[rows, :])
        total = cot_all[place.own + (rows,)].astype(full_type) + back
        grad[rows, :] = total
        cot_all[place.own + (rows,)] = total.astype(low_type)
        grad_gains[1:2, :] += jnp.sum(by_gain, axis=0, keepdims=True)

    mixed_all = cube_one
    mixed_gather = CubeGather(place, mixed_all, semaphores)
    mixed_gather.step(0)
    mlp_swaps[0].finish()
    add_swapped(gate_all, active, place.core)
    mixed_gather.step(1)
    mlp_swaps[1].finish()
    add_swapped(up_all, grad_gate, place.core)
    mixed_gather.step(2)
    mlp_swaps[2].finish()
    add_swapped(down_all, down_landing, place.core)
    pl.semaphore_signal(
        free.at[1], inc=1, device_id=place.sibling(), device_id_type=MESH
    )
    returns = [
        move(Owners(), gate_all, gate_back),
        move(Owners(), up_all, up_back),
        move(RowOwners(), down_all, down_back),
    ]
    for item in returns:
        item.start()
    two_sum.finish()
    mixed_gather.finish()

    out_sum = CubeSum(
        place,
        out_blocks,
        (cube_three.at[0], cube_three.at[1, 0], cube_three.at[1, 1, 0]),
        semaphores,
    )
    out_sum.start()

    @pl.loop(0, PARTS)
    def _(row):
        rows = row_block(row)
        branch = cols_product(mixed_all[whole_block(place, row)], whole_matrix(rows_all))
        gated, bend = gelu_parts(pre[rows, WIDTH:])
        grad_pre[rows, WIDTH:] = (branch * take(hidden, rows) * bend).astype(low_type)
        put(carries, rows, branch * gated)

    @pl.loop(0, 4)
    def _(step):
        cut = pl.ds(pl.multiple_of(step * 512, 512), 512)
        rows_all[:, :, :, cut] = (
            rows_product(mixed[...], mixed_all[:, :, :, :, cut].reshape(SPAN, 512))
            .astype(low_type)
            .reshape(2, 2, LANES, 512)
        )

    normed_again = cube_one
    load_normed = pltpu.make_async_copy(normed_kept, normed_again, semaphores.take(1).at[0])
    load_normed.start()

    def advance_back(step, state):
        factors, carried = state
        across = pl.ds(TOK - 1 - step, PARTS, stride=TOK)
        carried = [
            carries[piece, across, :] + factors[piece] * before
            for piece, before in enumerate(carried)
        ]
        for piece, now in enumerate(carried):
            carries[piece, across, :] = now
        return ([decays[piece, across, :] for piece in range(WIDTH // 128)], carried)

    zeros = [jnp.zeros((PARTS, 128), full_type)] * (WIDTH // 128)
    lax.fori_loop(0, TOK, advance_back, (zeros, zeros), unroll=8)
    out_sum.step(0)
    grad_aux[...] = jnp.zeros_like(grad_aux)
    grad_blocks[...] = jnp.zeros_like(grad_blocks)

    @pl.loop(0, PARTS)
    def _(row):
        rows = row_block(row)
        padded[0:8, :] = jnp.broadcast_to(states_all[row, 0:1, :], (8, WIDTH))
        padded[8 : 8 + TOK, :] = take(hidden, rows)
        low = conv[rows, :]
        recur, gate = gate_logits(low)
        log_decay = -8.0 * recur * soft
        decay = take(decays, rows)
        scale = jnp.sqrt(-small_expm1(2.0 * log_decay))
        conv_full = low.astype(full_type)
        carried = take(carries, rows)
        total = (
            carried * decay * padded[7 : 7 + TOK, :]
            - carried * gate * conv_full * (decay * decay) / scale
        )
        grad_aux[4:5, :] += jnp.sum(total * 8.0 * recur * slope, axis=0, keepdims=True)
        to_recur = (total * (-8.0 * soft) * recur * (1.0 - recur)).astype(low_type)
        to_input = (carried * scale * conv_full * gate * (1.0 - gate)).astype(low_type)
        both = jnp.concatenate([to_recur, to_input], axis=1)
        grad_blocks[...] += rows_product(low, both)
        back = carried * scale * gate + cols_product(both, whole_matrix(gates_all))
        first = decay[0:1, :] * carried[0:1, :]
        padded[0:8, :] = jnp.zeros((8, WIDTH), full_type)
        padded[8 : 8 + TOK, :] = back
        padded[8 + TOK :, :] = jnp.zeros((8, WIDTH), full_type)
        spread = taps[0] * padded[0 : 8 + TOK, :]
        for tap in range(1, 4):
            spread = spread + taps[tap] * padded[tap : tap + 8 + TOK, :]
        grad_pre[rows, 0:WIDTH] = spread[8:, :].astype(low_type)
        grad_states[row] = spread[0:8, :]
        grad_states[row, 0:1, :] = first
        padded[0:8, :] = states_all[row]
        padded[8 : 8 + TOK, :] = pre[rows, 0:WIDTH]
        for tap in range(4):
            grad_aux[tap : tap + 1, :] += jnp.sum(
                back * padded[8 - tap : 8 - tap + TOK, :], axis=0, keepdims=True
            )

    states_return = move(Peers(by_part), grad_states, states_back)
    states_return.start()
    blocks_low[...] = grad_blocks[...].astype(low_type).reshape(2, 2, LANES, 2 * WIDTH)
    out_sum.step(1)

    @pl.loop(0, PARTS)
    def _(row):
        terms = grad_pre[row_block(row), :]
        for piece in range(COLUMNS):
            cut = pl.ds(piece * (width // 4), width // 4)
            blocks[whole_block(place, row) + (slice(None), cut)] = cols_product(
                terms, whole_matrix(columns_all.at[piece])
            ).astype(low_type)

    one_sum = CubeSum(place, blocks, landings, semaphores)
    one_sum.start()
    out_sum.step(2, summed)

    @pl.loop(0, TOK // 32)
    def _(step):
        rows = pl.ds(pl.multiple_of(step * 32, 32), 32)
        cube_three[1, 1, 1, rows, :] = (after[rows, :] + summed[rows, :]).astype(low_type)

    local.start(cube_three.at[1, 1, 1], output)
    one_sum.step(0)
    load_normed.wait()

    @pl.loop(0, 8)
    def _(step):
        cut = pl.ds(pl.multiple_of(step * 256, 256), 256)
        columns_all[step // 2, step % 2] = (
            rows_product(normed_again[:, :, :, :, cut].reshape(SPAN, 256), grad_pre[...])
            .astype(low_type)
            .reshape(4, 64, 2 * WIDTH)
        )

    pl.semaphore_wait(free.at[1], 1)
    mixer_swaps = [
        move(Swap(), columns_all, active),
        move(Swap(), rows_all, down_landing.at[:, pl.ds(0, LANES)]),
        move(Swap(), blocks_low, blocks_landing),
    ]
    for item in mixer_swaps:
        item.start()
    one_sum.step(1)
    mixer_swaps[0].finish()
    add_swapped(columns_all, active, place.core)
    columns_return = move(Owners(), columns_all, columns_back)
    columns_return.start()
    mixer_swaps[1].finish()
    add_swapped(rows_all, down_landing, place.core)
    rows_return = move(RowOwners(), rows_all, rows_back)
    rows_return.start()
    mixer_swaps[2].finish()
    add_swapped(blocks_low, blocks_landing, place.core)
    blocks_return = move(RowOwners(), blocks_low, blocks_back)
    blocks_return.start()
    one_sum.step(2, summed)
    load_tokens = pltpu.make_async_copy(
        tokens, cube_three.at[1, 0, 0], semaphores.take(1).at[0]
    )
    out_sum.finish()
    load_tokens.start()
    load_tokens.wait()

    @pl.loop(0, TOK // 32)
    def _(step):
        rows = pl.ds(pl.multiple_of(step * 32, 32), 32)
        values = cube_three[1, 0, 0, rows, :].astype(full_type)
        back, by_gain = norm_back(values, gains[0:1, :], summed[rows, :])
        cube_three[1, 0, 1, rows, :] = (grad[rows, :] + back).astype(low_type)
        grad_gains[0:1, :] += jnp.sum(by_gain, axis=0, keepdims=True)

    local.start(cube_three.at[1, 0, 1], grad_tokens)
    small_terms[...] = jnp.zeros_like(small_terms)
    for column, core, z in itertools.product(range(COLUMNS), range(2), range(4)):
        tile = (column * 8 + core * 4 + z) // 2
        small_terms[column, core, z, 0:2, 0:128] = grad_gains[:, tile * 128 : (tile + 1) * 128]
    for z in range(4):
        small_terms[place.part // 2, place.part % 2, z, 2:7, :] = grad_aux[0:5, :]
    small_swap = move(Swap(), small_terms, small_landing)
    small_swap.start()
    small_swap.finish()
    add_swapped(small_terms, small_landing, place.core)
    small_return = move(Owners(), small_terms, small_back)
    small_return.start()
    one_sum.finish()
    for item in [states_return, small_return, columns_return, rows_return, blocks_return] + returns:
        item.finish()
    for copy in local.copies[1:]:
        copy.wait()


def block_call(arrays, rows, width, units):
    hbm = pl.BlockSpec(memory_space=pl.ANY)
    lanes = (WIDTH // 128, SPAN, 128)
    cube = (2, 2, 2, TOK, width)
    spread = (COLUMNS, 2, 4, rows)
    hidden_units = 4 * units
    outputs = [
        ((TOK, width), low_type),
        ((TOK, width), low_type),
        ((PARTS, 8, WIDTH), full_type),
        ((2, PARTS, 8, WIDTH), full_type),
        ((2, PARTS, rows, 2 * WIDTH), low_type),
        ((2, PARTS, rows, hidden_units), low_type),
        ((2, PARTS, rows, hidden_units), low_type),
        ((2, LANES, 2 * WIDTH), low_type),
        ((2, LANES, width), low_type),
        ((2, units, width), low_type),
        (cube, low_type),
    ]
    scratch = [
        (cube, low_type),
        (cube, low_type),
        (cube, low_type),
        (cube, low_type),
        ((2, 2, TOK, width), low_type),
        ((2, TOK, width), low_type),
        ((TOK, width), low_type),
        ((COLUMNS, 2, 4, 16, WIDTH), low_type),
        ((PARTS, 8, WIDTH), full_type),
        (spread + (2 * WIDTH,), low_type),
        ((2, 2, LANES, 2 * WIDTH), low_type),
        ((2, 2, LANES, width), low_type),
        (spread + (hidden_units,), low_type),
        (spread + (hidden_units,), low_type),
        ((2, 2, units, width), low_type),
        ((SPAN, 2 * WIDTH), full_type),
        ((SPAN, WIDTH), low_type),
        (lanes, full_type),
        ((SPAN, WIDTH), low_type),
        (lanes, full_type),
        (lanes, full_type),
        ((TOK + 16, WIDTH), full_type),
        ((TOK, width), full_type),
        ((TOK, width), full_type),
        ((TOK, width), full_type),
        ((8, WIDTH), full_type),
        ((2, width), full_type),
        ((2, width), full_type),
        ((8, WIDTH), full_type),
        ((4, 4, 64, hidden_units), low_type),
        ((4, 4, 64, hidden_units), low_type),
        ((4, 4, 64, hidden_units), low_type),
        ((2, units, width), low_type),
        ((SPAN, 2 * WIDTH), low_type),
        ((WIDTH, 2 * WIDTH), full_type),
        ((2, 2, LANES, 2 * WIDTH), low_type),
        ((2, LANES, 2 * WIDTH), low_type),
        ((PARTS, 8, WIDTH), full_type),
        ((COLUMNS, 2, 4, 8, WIDTH), full_type),
        ((COLUMNS, 4, 8, WIDTH), full_type),
    ]
    return pl.pallas_call(
        block_kernel,
        out_shape=[jax.ShapeDtypeStruct(shape, kind) for shape, kind in outputs],
        in_specs=[hbm] * len(arrays),
        out_specs=[hbm] * len(outputs),
        scratch_shapes=[pltpu.VMEM(shape, kind) for shape, kind in scratch]
        + [pltpu.SemaphoreType.DMA((320,)), pltpu.SemaphoreType.REGULAR((2,))],
        compiler_params=pltpu.CompilerParams(
            collective_id=0, has_side_effects=True, vmem_limit_bytes=VMEM_BYTES
        ),
        name="hawk_block",
    )(*arrays)


def to_lanes(array):
    chunks = array.reshape(array.shape[:-1] + (-1, CHUNK))
    pads = [(0, 0)] * (chunks.ndim - 1) + [(0, LANES - CHUNK)]
    return jnp.pad(chunks, pads).reshape(array.shape[:-1] + (-1,))


def from_lanes(array):
    chunks = array.reshape(array.shape[:-1] + (-1, LANES))
    return chunks[..., :CHUNK].reshape(array.shape[:-1] + (-1,))


def pad_rows(array, rows):
    return jnp.pad(array, ((0, rows - array.shape[0]), (0, 0)))


def halves(
    tokens,
    conv_state,
    recur_state,
    fresh_rows,
    gain_mixer,
    proj_input,
    proj_gate,
    conv_kernel,
    decay_param,
    gate_recur,
    gate_input,
    proj_output,
    gain_mlp,
    mlp_gate,
    mlp_up,
    mlp_down,
    cotangent,
):
    width = tokens.shape[2]
    rows = width // 32
    units = mlp_down.shape[0]
    keep = (1 - fresh_rows).astype(full_type)[0]

    columns = jnp.concatenate(
        [
            to_lanes(proj).reshape(rows, PARTS, WIDTH).transpose(1, 0, 2)
            for proj in (proj_input, proj_gate)
        ],
        axis=2,
    )
    zeros = jnp.zeros((CHUNK, 2 * LANES), low_type)
    first = lax.axis_index("narrow") < 2
    gates = jnp.concatenate(
        [
            jnp.where(chosen, to_lanes(gate), zeros)
            for gate in (gate_recur, gate_input)
            for chosen in (first, jnp.logical_not(first))
        ],
        axis=1,
    )
    z = lax.axis_index("narrow")
    taps = pad_rows(jnp.concatenate([conv_kernel, decay_param[None]], axis=0), 16)
    taps = lax.dynamic_update_slice(jnp.zeros((16, WIDTH), low_type), taps, (0, z * LANES))
    gain_rows = jnp.stack([gain_mixer, gain_mlp])
    small = lax.dynamic_update_slice(taps, gain_rows, (5, z % 2 * rows))
    state_rows = jnp.concatenate(
        [recur_state, jnp.zeros((4, recur_state.shape[1]), full_type), conv_state[0]], axis=0
    )
    states = to_lanes(state_rows * keep).reshape(8, PARTS, WIDTH).transpose(1, 0, 2)
    (
        output,
        grad_tokens,
        grad_states,
        small_back,
        columns_back,
        gate_back,
        up_back,
        blocks_back,
        rows_back,
        down_back,
        _,
    ) = block_call(
        (
            tokens[0],
            small,
            states,
            columns,
            pad_rows(gates, LANES),
            pad_rows(proj_output, LANES),
            mlp_gate,
            mlp_up,
            mlp_down,
            cotangent[0],
        ),
        rows,
        width,
        units,
    )
    grad_states = grad_states.transpose(1, 0, 2).reshape(8, PARTS * WIDTH)
    grad_states = from_lanes(grad_states) * keep
    small_sum = jnp.sum(small_back, axis=(0, 1))
    gain_sums = lax.dynamic_slice(small_sum, (0, z % 2 * rows), (2, rows))
    tap_sums = lax.dynamic_slice(small_sum, (2, z * LANES), (5, CHUNK))
    column_sum, gate_sum, up_sum, block_sum, out_sum, down_sum = (
        jnp.sum(term.astype(full_type), axis=0)
        for term in (columns_back, gate_back, up_back, blocks_back, rows_back, down_back)
    )
    column_sum = column_sum.transpose(1, 0, 2)
    pair = 2 * LANES
    gate_sums = [
        from_lanes(
            jnp.where(
                first,
                block_sum[:CHUNK, start : start + pair],
                block_sum[:CHUNK, start + pair : start + 2 * pair],
            )
        )
        for start in (0, WIDTH)
    ]
    return (
        output[None],
        grad_tokens[None],
        grad_states[None, 5:8],
        grad_states[0:1],
        gain_sums[0],
        from_lanes(column_sum[:, :, :WIDTH]).reshape(rows, -1),
        from_lanes(column_sum[:, :, WIDTH:]).reshape(rows, -1),
        tap_sums[0:4],
        tap_sums[4],
        gate_sums[0],
        gate_sums[1],
        out_sum[:CHUNK],
        gain_sums[1],
        gate_sum.transpose(1, 0, 2).reshape(rows, -1),
        up_sum.transpose(1, 0, 2).reshape(rows, -1),
        down_sum,
    )


def solution(mesh):
    sizes = (mesh.shape["wide"], mesh.shape["narrow"])
    return jax.shard_map(
        halves if sizes == (2 * COLUMNS, 2 * LOWS) else shards,
        mesh=mesh,
        in_specs=(
            P(("wide", "narrow"), None, None),
            P(("wide", "narrow"), None, None),
            P(("wide", "narrow"), None),
            P(("wide", "narrow")),
            P(("wide", "narrow")),
            P(("wide", "narrow"), None),
            P(("wide", "narrow"), None),
            P(None, ("wide", "narrow")),
            P(("wide", "narrow")),
            P(("wide", "narrow"), None),
            P(("wide", "narrow"), None),
            P(("wide", "narrow"), None),
            P(("wide", "narrow")),
            P(("wide", "narrow"), None),
            P(("wide", "narrow"), None),
            P(("wide", "narrow"), None),
            P(("wide", "narrow"), None, None),
        ),
        out_specs=(
            P(("wide", "narrow"), None, None),
            P(("wide", "narrow"), None, None),
            P(("wide", "narrow"), None, None),
            P(("wide", "narrow"), None),
            P(("wide", "narrow")),
            P(("wide", "narrow"), None),
            P(("wide", "narrow"), None),
            P(None, ("wide", "narrow")),
            P(("wide", "narrow")),
            P(("wide", "narrow"), None),
            P(("wide", "narrow"), None),
            P(("wide", "narrow"), None),
            P(("wide", "narrow")),
            P(("wide", "narrow"), None),
            P(("wide", "narrow"), None),
            P(("wide", "narrow"), None),
        ),
        check_vma=False,
    )
```

```python
import functools
import itertools
from functools import reduce

import jax
import jax.numpy as jnp
from jax import lax
from jax.experimental import pallas as pl
from jax.experimental.pallas import tpu as pltpu
from jax.sharding import PartitionSpec as P

BLOCKS = 16
BLK = 176
SCAN_BLOCK = 16


epsilon = 1e-06
contract_rows = (((0,), (0,)), ((), ()))
contract_cols = (((1,), (1,)), ((), ()))


def plain_product(left_side, right_side):
    return jnp.dot(left_side, right_side, preferred_element_type=jnp.float32)


def rows_product(left_side, right_side):
    return lax.dot_general(left_side, right_side, contract_rows, preferred_element_type=jnp.float32)


def cols_product(left_side, right_side):
    return lax.dot_general(left_side, right_side, contract_cols, preferred_element_type=jnp.float32)


def norm_scale(values, gain_vec):
    return (
        values * lax.rsqrt(jnp.mean(values * values, axis=-1, keepdims=True) + epsilon) * gain_vec
    )


def conv_apply(values, history, kernel):
    joined = jnp.concatenate([history, values], axis=0)
    length = values.shape[0]
    kernel_taps = kernel.shape[0]
    result = jnp.zeros_like(values)
    for offset in range(kernel_taps):
        first_row = kernel_taps - 1 - offset
        result = result + kernel[offset] * joined[first_row : first_row + length]
    return result


def block_mix(values, matrix):
    length = values.shape[0]
    mixed_out = jnp.einsum(
        "tki,kij->tkj",
        values.reshape(length, BLOCKS, BLK),
        matrix.reshape(BLOCKS, BLK, BLK),
        preferred_element_type=jnp.float32,
    )
    return mixed_out.reshape(length, BLOCKS * BLK)


def block_back(grad_logits, matrix):
    length = grad_logits.shape[0]
    spread_back = jnp.einsum(
        "tkj,kij->tki",
        grad_logits.reshape(length, BLOCKS, BLK),
        matrix.reshape(BLOCKS, BLK, BLK),
        preferred_element_type=jnp.float32,
    )
    return spread_back.reshape(length, BLOCKS * BLK)


def block_grad(values, grad_logits):
    length = values.shape[0]
    summed = jnp.einsum(
        "tki,tkj->kij",
        values.reshape(length, BLOCKS, BLK),
        grad_logits.reshape(length, BLOCKS, BLK),
        preferred_element_type=jnp.float32,
    )
    return summed.reshape(BLOCKS * BLK, BLK)


def gate_apply(recur_logits, input_logits, conv_float, decay_float):
    log_decay = -8.0 * jax.nn.sigmoid(recur_logits) * jax.nn.softplus(-decay_float)
    scan_in = jnp.sqrt(-jnp.expm1(2.0 * log_decay)) * jax.nn.sigmoid(input_logits) * conv_float
    return (log_decay, scan_in)


def branch_apply(hidden, gate_logits):
    return hidden * jax.nn.gelu(gate_logits)


def mlp_apply(gate_part, up_part):
    return jax.nn.gelu(gate_part) * up_part


def block_scan(log_decay, scan_in, initial):
    length, channels = scan_in.shape
    block_count = length // SCAN_BLOCK
    positions = jnp.arange(SCAN_BLOCK)
    causal = (positions[:, None] >= positions[None, :])[:, :, None]

    def advance(carried, pieces):
        decay_piece, input_piece = pieces
        cumulative = jnp.cumsum(decay_piece, axis=0)
        spread = jnp.where(causal, cumulative[:, None, :] - cumulative[None, :, :], 0.0)
        factors = jnp.where(causal, jnp.exp(spread), 0.0)
        states = jnp.sum(factors * input_piece[None, :, :], axis=1) + jnp.exp(cumulative) * carried
        return (states[-1], states)

    last_state, states = lax.scan(
        advance,
        initial,
        (
            log_decay.reshape(block_count, SCAN_BLOCK, channels),
            scan_in.reshape(block_count, SCAN_BLOCK, channels),
        ),
    )
    return states.reshape(length, channels)


def scan_back(log_decay, hidden, initial, grad_hidden):
    following = jnp.concatenate([log_decay[1:], jnp.zeros_like(log_decay[:1])], axis=0)
    carried = block_scan(following[::-1], grad_hidden[::-1], jnp.zeros_like(initial))[::-1]
    previous = jnp.concatenate([initial[None], hidden[:-1]], axis=0)
    grad_log_decay = carried * jnp.exp(log_decay) * previous
    grad_initial = jnp.exp(log_decay[0]) * carried[0]
    return (grad_log_decay, carried, grad_initial)


def mixer_forward(tokens_row, history, initial, keep_row, mixer):
    (
        gain_vec,
        proj_input,
        proj_gate,
        conv_kernel,
        decay_param,
        gate_recur,
        gate_input,
        proj_output,
    ) = mixer
    values = tokens_row.astype(jnp.float32)
    normed_one = norm_scale(values, gain_vec.astype(jnp.float32)).astype(jnp.bfloat16)
    branch_in = plain_product(normed_one, proj_input)
    gate_logits = plain_product(normed_one, proj_gate)
    history_kept = history * keep_row
    kernel_float = conv_kernel.astype(jnp.float32)
    conv_out = conv_apply(branch_in, history_kept, kernel_float).astype(jnp.bfloat16)
    recur_logits = block_mix(conv_out, gate_recur)
    input_logits = block_mix(conv_out, gate_input)
    decay_float = decay_param.astype(jnp.float32)
    conv_float = conv_out.astype(jnp.float32)
    log_decay, scan_in = gate_apply(recur_logits, input_logits, conv_float, decay_float)
    initial_kept = initial * keep_row
    hidden = block_scan(log_decay, scan_in, initial_kept)
    mixed_out = branch_apply(hidden, gate_logits).astype(jnp.bfloat16)
    after_mixer = values + plain_product(mixed_out, proj_output)
    kept = (
        values,
        normed_one,
        branch_in,
        gate_logits,
        history_kept,
        kernel_float,
        conv_out,
        conv_float,
        recur_logits,
        input_logits,
        decay_float,
        log_decay,
        initial_kept,
        hidden,
        mixed_out,
    )
    return (after_mixer, kept)


def mlp_forward(after_mixer, mlp):
    gain_vec, mlp_gate, mlp_up, mlp_down = mlp
    normed_two = norm_scale(after_mixer, gain_vec.astype(jnp.float32)).astype(jnp.bfloat16)
    gate_part = plain_product(normed_two, mlp_gate)
    up_part = plain_product(normed_two, mlp_up)
    activated = mlp_apply(gate_part, up_part).astype(jnp.bfloat16)
    result = after_mixer + plain_product(activated, mlp_down)
    return (result, (after_mixer, normed_two, gate_part, up_part, activated))


def mlp_backward(grad_result, mlp, kept):
    gain_vec, mlp_gate, mlp_up, mlp_down = mlp
    after_mixer, normed_two, gate_part, up_part, activated = kept
    grad_activated = cols_product(grad_result, mlp_down)
    grad_down = rows_product(activated, grad_result)
    unused, mlp_pull = jax.vjp(mlp_apply, gate_part, up_part)
    grad_gate_part, grad_up_part = mlp_pull(grad_activated)
    grad_gate_part = grad_gate_part.astype(jnp.bfloat16)
    grad_up_part = grad_up_part.astype(jnp.bfloat16)
    grad_normed = cols_product(grad_gate_part, mlp_gate) + cols_product(grad_up_part, mlp_up)
    grad_mlp_gate = rows_product(normed_two, grad_gate_part)
    grad_mlp_up = rows_product(normed_two, grad_up_part)
    unused, norm_pull = jax.vjp(norm_scale, after_mixer, gain_vec.astype(jnp.float32))
    grad_values, grad_gain = norm_pull(grad_normed)
    grad_after = grad_result.astype(jnp.float32) + grad_values
    return (grad_after, (grad_gain, grad_mlp_gate, grad_mlp_up, grad_down))


def mixer_backward(grad_after, mixer, kept, keep_row):
    (
        gain_vec,
        proj_input,
        proj_gate,
        conv_kernel,
        decay_param,
        gate_recur,
        gate_input,
        proj_output,
    ) = mixer
    (
        values,
        normed_one,
        branch_in,
        gate_logits,
        history_kept,
        kernel_float,
        conv_out,
        conv_float,
        recur_logits,
        input_logits,
        decay_float,
        log_decay,
        initial_kept,
        hidden,
        mixed_out,
    ) = kept
    grad_mixed = grad_after.astype(jnp.bfloat16)
    grad_proj_output = rows_product(mixed_out, grad_mixed)
    grad_branch = cols_product(grad_mixed, proj_output)
    unused, branch_pull = jax.vjp(branch_apply, hidden, gate_logits)
    grad_hidden, grad_gate_logits = branch_pull(grad_branch)
    grad_gate_logits = grad_gate_logits.astype(jnp.bfloat16)
    grad_log_decay, grad_scan_in, grad_initial = scan_back(
        log_decay, hidden, initial_kept, grad_hidden
    )
    unused, gate_pull = jax.vjp(gate_apply, recur_logits, input_logits, conv_float, decay_float)
    grad_recur_logits, grad_input_logits, grad_conv, grad_decay = gate_pull(
        (grad_log_decay, grad_scan_in)
    )
    grad_recur_logits = grad_recur_logits.astype(jnp.bfloat16)
    grad_input_logits = grad_input_logits.astype(jnp.bfloat16)
    grad_gate_recur = block_grad(conv_out, grad_recur_logits)
    grad_gate_input = block_grad(conv_out, grad_input_logits)
    grad_conv = (
        grad_conv
        + block_back(grad_recur_logits, gate_recur)
        + block_back(grad_input_logits, gate_input)
    )
    unused, conv_pull = jax.vjp(conv_apply, branch_in, history_kept, kernel_float)
    grad_branch_in, grad_history, grad_kernel = conv_pull(grad_conv)
    grad_branch_low = grad_branch_in.astype(jnp.bfloat16)
    grad_proj_input = rows_product(normed_one, grad_branch_low)
    grad_proj_gate = rows_product(normed_one, grad_gate_logits)
    grad_normed = cols_product(grad_branch_low, proj_input) + cols_product(
        grad_gate_logits, proj_gate
    )
    unused, norm_pull = jax.vjp(norm_scale, values, gain_vec.astype(jnp.float32))
    grad_values, grad_gain = norm_pull(grad_normed)
    grad_tokens = (grad_after + grad_values).astype(jnp.bfloat16)
    weight_terms = (
        grad_gain,
        grad_proj_input,
        grad_proj_gate,
        grad_kernel,
        grad_decay,
        grad_gate_recur,
        grad_gate_input,
        grad_proj_output,
    )
    return (grad_tokens, grad_history * keep_row, grad_initial * keep_row, weight_terms)


def add_terms(first_terms, second_terms):
    return tuple(
        (left_side + right_side for left_side, right_side in zip(first_terms, second_terms))
    )


def shards(
    tokens,
    conv_state,
    recur_state,
    fresh_rows,
    gain_mixer,
    proj_input,
    proj_gate,
    conv_kernel,
    decay_param,
    gate_recur,
    gate_input,
    proj_output,
    gain_mlp,
    mlp_gate,
    mlp_up,
    mlp_down,
    cotangent,
):
    mixer_full = (
        lax.all_gather(gain_mixer, ("wide", "narrow"), axis=0, tiled=True),
        lax.all_gather(proj_input, ("wide", "narrow"), axis=0, tiled=True),
        lax.all_gather(proj_gate, ("wide", "narrow"), axis=0, tiled=True),
        lax.all_gather(conv_kernel, ("wide", "narrow"), axis=1, tiled=True),
        lax.all_gather(decay_param, ("wide", "narrow"), axis=0, tiled=True),
        lax.all_gather(gate_recur, ("wide", "narrow"), axis=0, tiled=True),
        lax.all_gather(gate_input, ("wide", "narrow"), axis=0, tiled=True),
        lax.all_gather(proj_output, ("wide", "narrow"), axis=0, tiled=True),
    )
    mlp_full = (
        lax.all_gather(gain_mlp, ("wide", "narrow"), axis=0, tiled=True),
        lax.all_gather(mlp_gate, ("wide", "narrow"), axis=0, tiled=True),
        lax.all_gather(mlp_up, ("wide", "narrow"), axis=0, tiled=True),
        lax.all_gather(mlp_down, ("wide", "narrow"), axis=0, tiled=True),
    )
    keep_rows = (1 - fresh_rows).astype(jnp.float32)
    stored = []
    row_index = 0
    after_mixer, mixer_kept = mixer_forward(
        tokens[row_index],
        conv_state[row_index],
        recur_state[row_index],
        keep_rows[row_index],
        mixer_full,
    )
    result, mlp_kept = mlp_forward(after_mixer, mlp_full)
    outputs = [result.astype(jnp.bfloat16)]
    stored.append((mixer_kept, mlp_kept))
    mixer_back = (
        lax.all_gather(gain_mixer, ("wide", "narrow"), axis=0, tiled=True),
        lax.all_gather(proj_input, ("wide", "narrow"), axis=0, tiled=True),
        lax.all_gather(proj_gate, ("wide", "narrow"), axis=0, tiled=True),
        lax.all_gather(conv_kernel, ("wide", "narrow"), axis=1, tiled=True),
        lax.all_gather(decay_param, ("wide", "narrow"), axis=0, tiled=True),
        lax.all_gather(gate_recur, ("wide", "narrow"), axis=0, tiled=True),
        lax.all_gather(gate_input, ("wide", "narrow"), axis=0, tiled=True),
        lax.all_gather(proj_output, ("wide", "narrow"), axis=0, tiled=True),
    )
    mlp_back = (
        lax.all_gather(gain_mlp, ("wide", "narrow"), axis=0, tiled=True),
        lax.all_gather(mlp_gate, ("wide", "narrow"), axis=0, tiled=True),
        lax.all_gather(mlp_up, ("wide", "narrow"), axis=0, tiled=True),
        lax.all_gather(mlp_down, ("wide", "narrow"), axis=0, tiled=True),
    )
    stored = []
    row_index = 0
    after_mixer, mixer_kept = mixer_forward(
        tokens[row_index],
        conv_state[row_index],
        recur_state[row_index],
        keep_rows[row_index],
        mixer_back,
    )
    unused, mlp_kept = mlp_forward(after_mixer, mlp_back)
    stored.append((mixer_kept, mlp_kept))
    row_index = 0
    grad_after, row_terms = mlp_backward(cotangent[row_index], mlp_back, stored[row_index][1])
    after_grads = [grad_after]
    mlp_terms = [row_terms]
    mlp_total = reduce(add_terms, mlp_terms)
    mlp_sums = (
        lax.psum_scatter(mlp_total[0], ("wide", "narrow"), scatter_dimension=0, tiled=True),
        lax.psum_scatter(mlp_total[1], ("wide", "narrow"), scatter_dimension=0, tiled=True),
        lax.psum_scatter(mlp_total[2], ("wide", "narrow"), scatter_dimension=0, tiled=True),
        lax.psum_scatter(mlp_total[3], ("wide", "narrow"), scatter_dimension=0, tiled=True),
    )
    row_index = 0
    grad_tokens, grad_history, grad_initial, row_terms = mixer_backward(
        after_grads[row_index], mixer_back, stored[row_index][0], keep_rows[row_index]
    )
    token_grads = [grad_tokens]
    history_grads = [grad_history]
    initial_grads = [grad_initial]
    mixer_terms = [row_terms]
    mixer_total = reduce(add_terms, mixer_terms)
    mixer_sums = (
        lax.psum_scatter(mixer_total[0], ("wide", "narrow"), scatter_dimension=0, tiled=True),
        lax.psum_scatter(mixer_total[1], ("wide", "narrow"), scatter_dimension=0, tiled=True),
        lax.psum_scatter(mixer_total[2], ("wide", "narrow"), scatter_dimension=0, tiled=True),
        lax.psum_scatter(mixer_total[3], ("wide", "narrow"), scatter_dimension=1, tiled=True),
        lax.psum_scatter(mixer_total[4], ("wide", "narrow"), scatter_dimension=0, tiled=True),
        lax.psum_scatter(mixer_total[5], ("wide", "narrow"), scatter_dimension=0, tiled=True),
        lax.psum_scatter(mixer_total[6], ("wide", "narrow"), scatter_dimension=0, tiled=True),
        lax.psum_scatter(mixer_total[7], ("wide", "narrow"), scatter_dimension=0, tiled=True),
    )
    return (
        jnp.stack(outputs),
        jnp.stack(token_grads),
        jnp.stack(history_grads),
        jnp.stack(initial_grads),
        mixer_sums[0],
        mixer_sums[1],
        mixer_sums[2],
        mixer_sums[3],
        mixer_sums[4],
        mixer_sums[5],
        mixer_sums[6],
        mixer_sums[7],
        mlp_sums[0],
        mlp_sums[1],
        mlp_sums[2],
        mlp_sums[3],
    )


COLUMNS = 4
LOWS = 2
PARTS = COLUMNS * LOWS
TOK = 128
CHUNK = 88
LANES = 96
WIDTH = 4 * LANES
SPAN = PARTS * TOK
MESH = pl.DeviceIdType.MESH
VMEM_BYTES = 63 * 1024 * 1024 + 896 * 1024
low_type = jnp.bfloat16
full_type = jnp.float32


class Place:
    def __init__(self):
        wide = lax.axis_index("wide")
        self.z = lax.axis_index("narrow")
        self.column, self.core = wide // 2, wide % 2
        self.half, self.low = self.z // 2, self.z % 2
        self.part = self.column * 2 + self.low
        self.index = wide * 4 + self.z
        self.own = (self.column // 2, self.column % 2, self.low)

    def shifted(self, by_y, by_x, by_low, by_half):
        column = (self.column // 2 + by_y) % 2 * 2 + (self.column % 2 + by_x) % 2
        low, half = (self.low + by_low) % 2, (self.half + by_half) % 2
        return (column, low, half)

    def neighbour(self, axis):
        y, x, low = (1 - at if axis == here else at for here, at in enumerate(self.own))
        return (y * 4 + x * 2 + self.core, self.half * 2 + low)

    def cube(self, fixed, other=None):
        return tuple(
            1 - at if axis == other else at if axis in fixed else slice(None)
            for axis, at in enumerate(self.own)
        )

    def sibling(self):
        return (self.column * 2 + 1 - self.core, self.z)


def greet_all(place):
    barrier = pltpu.get_barrier_semaphore()

    @pl.loop(1, 32)
    def _(step):
        other = (place.index + step) % 32
        pl.semaphore_signal(
            barrier, inc=1, device_id=(other // 4, other % 4), device_id_type=MESH
        )

    pl.semaphore_wait(barrier, 31)


def remote(source, target, send, receive, device):
    return pltpu.make_async_remote_copy(
        src_ref=source,
        dst_ref=target,
        send_sem=send,
        recv_sem=receive,
        device_id=device,
        device_id_type=MESH,
    )


def await_bytes(view, semaphore):
    pltpu.make_async_copy(view, view, semaphore).wait()


SHIFTS = tuple(
    near + (half,) for near in itertools.product(range(2), repeat=3) for half in (1, 0)
)


def row_pieces(place, source, slot_of, sems, copies, block_of=None):
    rows_all = source.shape[-2]
    step = rows_all // 3
    device = lambda half: (place.column * 2 + place.low, half * 2 + place.core)

    def piece(rows, half):
        block = source.at[rows] if block_of is None else block_of(half, rows)
        copy = remote(block, slot_of(half, rows), sems.at[0], sems.at[1], device(half))
        own = (place.low == place.core) & (place.half == half)

        @pl.when(own)
        def _():
            pltpu.make_async_copy(block, slot_of(half, rows), sems.at[1]).start()

        @pl.when(jnp.logical_not(own))
        def _():
            copy.start()

        copies.append((own, copy))

    return [
        functools.partial(piece, pl.ds(third * step, step), half)
        for third in range(3)
        for half in range(2)
    ]


def wait_pieces(copies):
    for own, copy in copies:

        @pl.when(jnp.logical_not(own))
        def _():
            copy.wait_send()


class Spread:
    def __init__(self, pick):
        self.pick = pick

    def pieces(self, place, source, target, sems):
        self.copies = []
        slot = target.at[place.column, place.core, place.z]

        def piece(shift):
            column, low, half = place.shifted(*shift)
            block = self.pick(source, column * 2 + low)
            if any(shift):
                copy = remote(
                    block, slot, sems.at[0], sems.at[1], (column * 2 + place.core, half * 2 + low)
                )
                copy.start()
                self.copies.append(copy)
            else:
                pltpu.make_async_copy(block, slot, sems.at[1]).start()

        return [functools.partial(piece, shift) for shift in SHIFTS]

    def relay(self, place, source, target, sems):
        mine = target.at[:, place.core]
        await_bytes(mine, sems.at[1])
        self.passed = remote(mine, mine, sems.at[2], sems.at[3], place.sibling())
        self.passed.start()

    def finish(self, place, source, target, sems):
        self.passed.wait()
        for copy in self.copies:
            copy.wait_send()


class RowSpread:
    def pieces(self, place, source, target, sems):
        self.copies = []
        slot = target.at[place.half, place.low]
        return row_pieces(place, source, lambda half, rows: slot.at[rows], sems, self.copies)

    def relay(self, place, source, target, sems):
        mine = target.at[:, place.core]
        await_bytes(mine, sems.at[1])
        self.passed = remote(mine, mine, sems.at[2], sems.at[3], place.sibling())
        self.passed.start()

    def finish(self, place, source, target, sems):
        self.passed.wait()
        wait_pieces(self.copies)


class Peers:
    def __init__(self, pick):
        self.pick = pick

    def start(self, place, source, target, sems):
        self.copies = []
        slot = target.at[place.part]
        for shift in itertools.product(range(2), repeat=3):
            column, low, half = place.shifted(*shift, 0)
            block = self.pick(source, column * 2 + low)
            if any(shift):
                copy = remote(
                    block, slot, sems.at[0], sems.at[1], (column * 2 + place.core, half * 2 + low)
                )
                copy.start()
                self.copies.append(copy)
            else:
                pltpu.make_async_copy(block, slot, sems.at[1]).start()

    def relay(self, place, source, target, sems):
        pass

    def finish(self, place, source, target, sems):
        await_bytes(target, sems.at[1])
        for copy in self.copies:
            copy.wait_send()


class Swap:
    def start(self, place, source, target, sems):
        self.copy = remote(
            source.at[:, 1 - place.core], target, sems.at[0], sems.at[1], place.sibling()
        )
        self.copy.start()

    def relay(self, place, source, target, sems):
        pass

    def finish(self, place, source, target, sems):
        self.copy.wait()


class Owners:
    def pieces(self, place, source, target, sems):
        self.copies = []
        if len(target.shape) == 3:
            width = source.shape[-1]
            cut = pl.ds(pl.multiple_of(place.part * width, 128), width)
            slot = target.at[place.half, :, cut]
        else:
            slot = target.at[place.half, place.part]

        def piece(shift):
            column, low, half = place.shifted(*shift)
            z = half * 2 + low
            block = source.at[column, place.core, z]
            if any(shift):
                copy = remote(
                    block, slot, sems.at[0], sems.at[1], (column * 2 + place.core, z)
                )
                copy.start()
                self.copies.append(copy)
            else:
                pltpu.make_async_copy(block, slot, sems.at[1]).start()

        return [functools.partial(piece, shift) for shift in SHIFTS]

    def finish(self, place, source, target, sems):
        await_bytes(target, sems.at[1])
        for copy in self.copies:
            copy.wait_send()


class RowOwners:
    def pieces(self, place, source, target, sems):
        self.copies = []
        slot = target.at[place.half]
        return row_pieces(
            place,
            source,
            lambda half, rows: slot.at[rows],
            sems,
            self.copies,
            lambda half, rows: source.at[half, place.core, rows],
        )

    def finish(self, place, source, target, sems):
        await_bytes(target, sems.at[1])
        wait_pieces(self.copies)


PACE = (6, 0, 0, 3, 1, 1)
PART = TOK // 2


class Semaphores:
    def __init__(self, array):
        self.array, self.used = array, 0

    def take(self, count):
        taken = self.array.at[pl.ds(self.used, count)]
        self.used += count
        return taken


LIGHT = ((2, 0, 1), (2, 1, 0), (0, 2, 1), (1, 2, 0))
EVEN = ((0, 1, 2), (1, 2, 0), (2, 0, 1))


def cuts(width, count):
    ends = [-(-(width // 128) * step // count) * 128 for step in range(count + 1)]
    return [pl.ds(start, end - start) for start, end in zip(ends, ends[1:])]


class CubeGather:
    def __init__(self, place, buffer, semaphores, rows, orders=LIGHT):
        self.place, self.buffer, self.copies = place, buffer, []
        self.rows, self.orders = rows, orders
        self.cuts = cuts(buffer.shape[4], len(orders))
        self.sems = semaphores.take(6 * len(orders))

    def step(self, number):
        routes = len(self.orders)
        for route, (axes, cut) in enumerate(zip(self.orders, self.cuts)):
            if number > 0:
                self.copies[routes * (number - 1) + route].wait_recv()
            region = self.buffer.at[self.place.cube(axes[number:]) + (self.rows, cut)]
            index = routes * number + route
            copy = remote(
                region,
                region,
                self.sems.at[index],
                self.sems.at[3 * routes + index],
                self.place.neighbour(axes[number]),
            )
            copy.start()
            self.copies.append(copy)

    def finish(self):
        for copy in self.copies[2 * len(self.orders) :]:
            copy.wait_recv()
        for copy in self.copies:
            copy.wait_send()


class CubeSum:
    def __init__(self, place, blocks, landings, semaphores, start, count, orders=LIGHT):
        self.place, self.blocks, self.landings, self.copies = place, blocks, landings, []
        self.first, self.count = start, count
        self.orders = [axes[::-1] for axes in orders]
        self.cuts = cuts(blocks.shape[4], len(orders))
        self.sems = semaphores.take(6 * len(orders))

    def send(self, number, route):
        axes, cut, routes = self.orders[route], self.cuts[route], len(self.orders)
        index = routes * number + route
        rows = pl.ds(self.first, self.count)
        landing = self.landings[number]
        copy = remote(
            self.blocks.at[self.place.cube(axes[:number], axes[number]) + (rows, cut)],
            landing.at[(slice(None),) * (2 - number) + (rows, cut)],
            self.sems.at[index],
            self.sems.at[3 * routes + index],
            self.place.neighbour(axes[number]),
        )
        copy.start()
        self.copies.append(copy)

    def start(self):
        for route in range(len(self.orders)):
            self.send(0, route)

    def step(self, number, result=None):
        for route, (axes, cut) in enumerate(zip(self.orders, self.cuts)):
            self.copies[len(self.orders) * number + route].wait_recv()
            landing = self.landings[number]
            for picks in itertools.product(range(2), repeat=2 - number):
                chosen = iter(picks)
                index = tuple(
                    self.place.own[axis] if axis in axes[: number + 1] else next(chosen)
                    for axis in range(3)
                )

                @pl.loop(0, self.count // 32)
                def _(block):
                    rows = pl.ds(pl.multiple_of(self.first + block * 32, 32), 32)
                    total = self.blocks[index + (rows, cut)].astype(full_type) + landing[
                        picks + (rows, cut)
                    ].astype(full_type)
                    if number < 2:
                        self.blocks[index + (rows, cut)] = total.astype(low_type)
                    else:
                        result[rows, cut] = total

            if number < 2:
                self.send(number + 1, route)

    def finish(self):
        for copy in self.copies:
            copy.wait_send()


class Move:
    def __init__(self, place, plan, source, target, semaphores):
        self.plan, self.arguments = plan, (place, source, target, semaphores.take(4))

    def pieces(self):
        return self.plan.pieces(*self.arguments)

    def start(self):
        if hasattr(self.plan, "start"):
            self.plan.start(*self.arguments)
        else:
            for piece in self.pieces():
                piece()

    def relay(self):
        self.plan.relay(*self.arguments)

    def finish(self):
        self.plan.finish(*self.arguments)


class Pump:
    def __init__(self, wide, tall):
        wide = [item.pieces() for item in wide]
        tall = [item.pieces() for item in tall]
        self.units = []
        for step in range(8):
            self.units.append([piece for each in wide for piece in each[2 * step : 2 * step + 2]])
            if step % 3 == 1:
                third = step // 3
                self.units.append(
                    [piece for each in tall for piece in each[2 * third : 2 * third + 2]]
                )

    def start(self, count):
        for _ in range(min(count, len(self.units))):
            for piece in self.units.pop(0):
                piece()


class Local:
    def __init__(self, semaphores):
        self.semaphores, self.copies = semaphores, []

    def start(self, source, target):
        copy = pltpu.make_async_copy(source, target, self.semaphores.take(1).at[0])
        copy.start()
        self.copies.append(copy)
        return copy

    def finish(self):
        for copy in self.copies:
            copy.wait()


def whole(source, part):
    return source


def by_part(source, part):
    return source.at[part]


def by_columns(source, part):
    width = source.shape[1] // PARTS
    return source.at[:, pl.ds(pl.multiple_of(part * width, 128), width)]


def row_block(row):
    return pl.ds(pl.multiple_of(row * TOK, TOK), TOK)


def small_expm1(values):
    near = values * (
        1.0
        + values
        * (0.5 + values * (1 / 6 + values * (1 / 24 + values * (1 / 120 + values * (1 / 720)))))
    )
    return jnp.where(values > -0.25, near, jnp.exp(values) - 1.0)


def gelu_parts(values):
    scale = 0.7978845608028654
    bent = jnp.tanh(scale * (values + 0.044715 * values * values * values))
    slope = 0.5 * (1.0 + bent) + 0.5 * values * (1.0 - bent * bent) * scale * (
        1.0 + 3 * 0.044715 * values * values
    )
    return (0.5 * values * (1.0 + bent), slope)


def put(array, rows, values):
    for piece in range(WIDTH // 128):
        array[piece, rows, :] = values[:, piece * 128 : (piece + 1) * 128]


def take(array, rows):
    return jnp.concatenate([array[piece, rows, :] for piece in range(WIDTH // 128)], axis=1)


def taps_of(aux):
    return [aux[tap : tap + 1, :] for tap in range(4)]


def placed_sum(gathered, place, row):
    owners = [
        gathered[place.part // 2, place.part % 2, z, row : row + 1, :].astype(full_type)
        for z in range(4)
    ]
    return owners[0] + owners[1] + owners[2] + owners[3]


def placed_gain(gathered, row):
    pieces = []
    for column, core, pair in itertools.product(range(COLUMNS), range(2), range(2)):
        both = [
            gathered[column, core, 2 * pair + odd, row : row + 1, 0:128].astype(full_type)
            for odd in range(2)
        ]
        pieces.append(both[0] + both[1])
    return jnp.concatenate(pieces, axis=1)


def scaled_norm(values, gain):
    scale = lax.rsqrt(jnp.mean(values * values, axis=1, keepdims=True) + epsilon)
    return values * scale * gain


def whole_block(place, row):
    return (row // 4, row // 2 % 2, row % 2)


def add_swapped(array, landing, core):
    rows, columns = array.shape[-2:]
    inner = array.shape[2] if len(array.shape) == 5 else 1
    outer = array.shape[0]
    chunk = 32 if columns > 1024 and rows % 32 == 0 else 16 if rows % 16 == 0 else 8

    @pl.loop(0, outer * inner * (rows // chunk))
    def _(step):
        part = pl.ds(pl.multiple_of(step % (rows // chunk) * chunk, chunk), chunk)
        first = step // (rows // chunk)
        if len(array.shape) == 5:
            here, there = (first // inner, core, first % inner, part), (first // inner, first % inner, part)
        else:
            here, there = (first, core, part), (first, part)
        total = array[here].astype(full_type) + landing[there].astype(full_type)
        array[here] = total.astype(array.dtype)


def norm_back(values, gain, grad):
    scale = lax.rsqrt(jnp.mean(values * values, axis=1, keepdims=True) + epsilon)
    inner = grad * gain
    along = jnp.mean(inner * values, axis=1, keepdims=True)
    return (scale * inner - values * (scale * scale * scale * along), grad * values * scale)


def block_kernel(
    tokens,
    small,
    states,
    columns,
    gates,
    out_rows,
    mlp_gate,
    mlp_up,
    mlp_down,
    cotangent,
    output,
    grad_tokens,
    states_back,
    small_back,
    columns_back,
    gate_back,
    up_back,
    blocks_back,
    rows_back,
    down_back,
    normed_kept,
    cot_kept,
    cube_one,
    cube_two,
    cube_three,
    blocks,
    landing_one,
    landing_two,
    landing_three,
    small_all,
    states_all,
    columns_all,
    gates_all,
    rows_all,
    gate_all,
    up_all,
    down_all,
    pre,
    conv,
    hidden,
    mixed,
    decays,
    carries,
    padded,
    after,
    grad,
    summed,
    aux,
    gains,
    grad_gains,
    grad_aux,
    active,
    grad_gate,
    grad_up,
    down_landing,
    grad_pre,
    grad_blocks,
    blocks_low,
    blocks_landing,
    grad_states,
    small_terms,
    small_landing,
    sems,
    free,
):
    place = Place()
    semaphores = Semaphores(sems)
    local = Local(semaphores)
    width = tokens.shape[1]
    hidden_units = gate_all.shape[-1]
    tokens_all = cube_one
    normed = cube_two
    two_all = cube_three

    def move(plan, source, target):
        return Move(place, plan, source, target, semaphores)

    def whole_matrix(array):
        return array[...].reshape(-1, array.shape[-1])

    own_tokens = tokens_all.at[place.own]
    load = pltpu.make_async_copy(tokens, own_tokens, semaphores.take(1).at[0])
    load.start()
    greet_all(place)
    load.wait()
    every = pl.ds(0, TOK)
    parts = (pl.ds(0, PART), pl.ds(PART, PART))
    tokens_gather = CubeGather(place, tokens_all, semaphores, every, EVEN)
    tokens_gather.step(0)
    load_own_cot = pltpu.make_async_copy(
        cotangent, cot_kept.at[place.own], semaphores.take(1).at[0]
    )
    load_own_cot.start()
    small_move = move(Spread(whole), small, small_all)
    small_move.start()
    states_move = move(Peers(by_part), states, states_all)
    states_move.start()
    columns_move = move(Spread(by_part), columns, columns_all)
    columns_move.start()
    gates_move = move(RowSpread(), gates, gates_all)
    gates_move.start()
    rows_move = move(RowSpread(), out_rows, rows_all)
    rows_move.start()
    tokens_gather.step(1)
    small_move.relay()
    tokens_gather.step(2)
    late = [
        move(Spread(by_columns), mlp_gate, gate_all),
        move(Spread(by_columns), mlp_up, up_all),
        move(RowSpread(), mlp_down, down_all),
    ]
    late_pump = Pump(late[:2], late[2:])
    late_pump.start(PACE[0])
    small_move.finish()
    for tap in range(5):
        aux[tap : tap + 1, :] = placed_sum(small_all, place, tap)
    decay_row = aux[4:5, :]
    aux[4:5, :] = jnp.maximum(-decay_row, 0.0) + jnp.log1p(jnp.exp(-jnp.abs(decay_row)))
    aux[5:6, :] = jax.nn.sigmoid(-decay_row)
    aux[6:8, :] = jnp.zeros((2, WIDTH), full_type)
    gains[0:1, :] = placed_gain(small_all, 5)
    gains[1:2, :] = placed_gain(small_all, 6)
    tokens_gather.finish()
    cot_gather = CubeGather(place, cot_kept, semaphores, every)
    load_own_cot.wait()

    @pl.loop(0, SPAN // 32)
    def _(step):
        rows = pl.ds(pl.multiple_of(step % 4 * 32, 32), 32)
        index = whole_block(place, step // 4) + (rows,)
        normed[index] = scaled_norm(tokens_all[index].astype(full_type), gains[0:1, :]).astype(
            low_type
        )

    keep_normed = local.start(normed, normed_kept)
    columns_move.relay()
    gates_move.relay()
    rows_move.relay()
    columns_move.finish()
    late_pump.start(PACE[1])

    @pl.loop(0, 4)
    def _(step):
        rows = pl.ds(pl.multiple_of(step * 256, 256), 256)
        pre[rows, :] = jnp.dot(
            normed[step // 2, step % 2].reshape(256, width),
            whole_matrix(columns_all),
            preferred_element_type=full_type,
        )

    late_pump.start(PACE[2])
    gates_move.finish()
    states_move.finish()
    taps = taps_of(aux)
    soft, slope = aux[4:5, :], aux[5:6, :]

    def gate_logits(low):
        both = jnp.dot(low, whole_matrix(gates_all), preferred_element_type=full_type)
        return (jax.nn.sigmoid(both[:, 0:WIDTH]), jax.nn.sigmoid(both[:, WIDTH:]))

    @pl.loop(0, PARTS)
    def _(row):
        rows = row_block(row)
        padded[0:8, :] = states_all[row]
        padded[8 : 8 + TOK, :] = pre[rows, 0:WIDTH]
        total = taps[0] * padded[8 : 8 + TOK, :]
        for tap in range(1, 4):
            total = total + taps[tap] * padded[8 - tap : 8 - tap + TOK, :]
        low = total.astype(low_type)
        conv[rows, :] = low
        recur, gate = gate_logits(low)
        log_decay = -8.0 * recur * soft
        scale = jnp.sqrt(-small_expm1(2.0 * log_decay))
        put(carries, rows, scale * gate * low.astype(full_type))
        put(decays, rows, jnp.exp(log_decay))

    def advance(time, carried):
        across = pl.ds(time, PARTS, stride=TOK)
        carried = [
            decays[piece, across, :] * before + carries[piece, across, :]
            for piece, before in enumerate(carried)
        ]
        for piece, now in enumerate(carried):
            hidden[piece, across, :] = now
        return carried

    late_pump.start(PACE[3])
    initial = states_all[:, 0, :]
    initial = [initial[:, piece * 128 : (piece + 1) * 128] for piece in range(WIDTH // 128)]
    lax.fori_loop(0, TOK, advance, initial, unroll=8)
    rows_move.finish()

    def project_out(part):
        @pl.loop(0, PARTS)
        def _(row):
            rows = pl.ds(pl.multiple_of(row * TOK + part * PART, PART), PART)
            gated, _ = gelu_parts(pre[rows, WIDTH:])
            low = (take(hidden, rows) * gated).astype(low_type)
            mixed[rows, :] = low
            blocks[whole_block(place, row) + (parts[part],)] = jnp.dot(
                low, whole_matrix(rows_all), preferred_element_type=full_type
            ).astype(low_type)

    def norm_two(part):
        @pl.loop(0, PART // 32)
        def _(step):
            rows = pl.ds(pl.multiple_of(part * PART + step * 32, 32), 32)
            total = after[rows, :] + tokens_all[place.own + (rows,)].astype(full_type)
            after[rows, :] = total
            two_all[place.own + (rows,)] = scaled_norm(total, gains[1:2, :]).astype(low_type)

    landings = (landing_one, landing_two, landing_three)

    def cube_sum(array, part):
        return CubeSum(place, array, landings, semaphores, part * PART, PART)

    mixer_sums = [cube_sum(blocks, part) for part in range(2)]
    two_gathers = [CubeGather(place, two_all, semaphores, rows) for rows in parts]
    for part in range(2):
        project_out(part)
        mixer_sums[part].start()
        late_pump.start(PACE[4 + part])
    cot_gather.step(0)
    for part in range(2):
        mixer_sums[part].step(0)
    cot_gather.step(1)
    for part in range(2):
        mixer_sums[part].step(1)
    for part in range(2):
        mixer_sums[part].step(2, after)
        norm_two(part)
        two_gathers[part].step(0)
    late_pump.start(20)
    cot_gather.step(2)
    for part in range(2):
        two_gathers[part].step(1)
    for part in range(2):
        two_gathers[part].step(2)
    cot_gather.finish()
    cot_all = cube_one
    load_cot = pltpu.make_async_copy(cot_kept, cot_all, semaphores.take(1).at[0])
    load_cot.start()
    for item in late:
        item.relay()
    for part in range(2):
        mixer_sums[part].finish()
    keep_normed.wait()
    load_cot.wait()
    for item in late:
        item.finish()

    out_blocks = cube_two

    def mlp(part, y):
        rows = parts[part]
        at = (y, slice(None), slice(None), rows)
        index = y * 2 + part
        normed_two = two_all[at].reshape(4 * PART, width)
        cot = cot_all[at].reshape(4 * PART, width)
        for piece in range(2):
            cut = pl.ds(piece * (hidden_units // 2), hidden_units // 2)
            gate_part, up_part = (
                jnp.dot(
                    normed_two,
                    array[:, :, :, :, cut].reshape(width, hidden_units // 2),
                    preferred_element_type=full_type,
                )
                for array in (gate_all, up_all)
            )
            gated, bend = gelu_parts(gate_part)
            matrix = down_all[piece].reshape(hidden_units // 2, width)
            grad_active = cols_product(cot, matrix)
            for array, values in (
                (active, gated * up_part),
                (grad_gate, grad_active * up_part * bend),
                (grad_up, grad_active * gated),
            ):
                array[index, :, :, cut] = values.astype(low_type).reshape(
                    4, PART, hidden_units // 2
                )
        low, to_gate, to_up = (whole_matrix(array.at[index]) for array in (active, grad_gate, grad_up))
        for piece in range(4):
            cut = pl.ds(piece * (width // 4), width // 4)
            matrix = down_all[:, :, :, cut].reshape(hidden_units, width // 4)
            out_blocks[at + (cut,)] = (
                jnp.dot(low, matrix, preferred_element_type=full_type)
                .astype(low_type)
                .reshape(2, 2, PART, width // 4)
            )
            back = cols_product(to_gate, whole_matrix(gate_all.at[piece])) + cols_product(
                to_up, whole_matrix(up_all.at[piece])
            )
            blocks[at + (cut,)] = back.astype(low_type).reshape(2, 2, PART, width // 4)

    def by_tokens(array, cut):
        return jnp.concatenate(
            [
                array[y, :, :, rows, cut].reshape(4 * PART, cut.size)
                for y in range(2)
                for rows in parts
            ],
            axis=0,
        )

    def grad_rows(terms, sums):
        @pl.loop(0, 8)
        def _(step):
            side = by_tokens(two_all, pl.ds(pl.multiple_of(step * 256, 256), 256))
            sums[step // 2, step % 2] = (
                rows_product(side, whole_matrix(terms))
                .astype(low_type)
                .reshape(4, 64, hidden_units)
            )

    def norm_two_back(part):
        @pl.loop(0, PART // 32)
        def _(step):
            rows = pl.ds(pl.multiple_of(part * PART + step * 32, 32), 32)
            back, by_gain = norm_back(after[rows, :], gains[1:2, :], grad[rows, :])
            total = cot_all[place.own + (rows,)].astype(full_type) + back
            grad[rows, :] = total
            cot_all[place.own + (rows,)] = total.astype(low_type)
            grad_gains[1:2, :] += jnp.sum(by_gain, axis=0, keepdims=True)

    mixed_all = cube_one
    two_sums = [cube_sum(blocks, part) for part in range(2)]
    mixed_gathers = [CubeGather(place, cube_one, semaphores, rows) for rows in parts]
    two_gathers[0].finish()

    @pl.loop(0, 2)
    def _(y):
        mlp(0, y)

    two_sums[0].start()
    two_gathers[1].finish()
    mlp(1, 0)
    two_sums[0].step(0)
    mlp(1, 1)
    two_sums[1].start()

    @pl.loop(0, 4)
    def _(step):
        cut = pl.ds(pl.multiple_of(step * 512, 512), 512)
        side = by_tokens(cot_all, cut)
        for piece in range(2):
            half = pl.ds(piece * (hidden_units // 2), hidden_units // 2)
            down_all[piece, :, :, cut] = (
                rows_product(active[:, :, :, half].reshape(SPAN, hidden_units // 2), side)
                .astype(low_type)
                .reshape(2, hidden_units // 4, 512)
            )

    def tell_sibling(number):
        pl.semaphore_signal(
            free.at[number], inc=1, device_id=place.sibling(), device_id_type=MESH
        )

    gate_swap = move(Swap(), gate_all, active)
    up_swap = move(Swap(), up_all, grad_gate)
    down_swap = move(Swap(), down_all, down_landing)
    gate_return = move(Owners(), gate_all, gate_back)
    up_return = move(Owners(), up_all, up_back)
    down_return = move(RowOwners(), down_all, down_back)
    returns = [gate_return, up_return, down_return]
    tell_sibling(0)
    down_swap.start()
    two_sums[0].step(1)
    two_sums[1].step(0)
    grad_rows(grad_gate, gate_all)
    tell_sibling(1)
    pl.semaphore_wait(free.at[0], 1)
    gate_swap.start()
    grad_gains[...] = jnp.zeros_like(grad_gains)
    two_sums[0].step(2, grad)
    norm_two_back(0)
    mixed_gathers[0].step(0)
    two_sums[1].step(1)
    down_swap.finish()
    add_swapped(down_all, down_landing, place.core)
    grad_rows(grad_up, up_all)
    pl.semaphore_wait(free.at[1], 1)
    up_swap.start()
    two_sums[1].step(2, grad)
    norm_two_back(1)
    mixed_gathers[1].step(0)
    gate_swap.finish()
    add_swapped(gate_all, active, place.core)
    mixed_gathers[0].step(1)
    mixed_gathers[1].step(1)
    up_swap.finish()
    add_swapped(up_all, grad_gate, place.core)
    tell_sibling(2)
    mixed_gathers[0].step(2)
    mixed_gathers[1].step(2)
    for item in returns:
        item.start()
    for part in range(2):
        two_sums[part].finish()
        mixed_gathers[part].finish()

    out_sum = CubeSum(
        place,
        out_blocks,
        (cube_three.at[0], cube_three.at[1, 0], cube_three.at[1, 1, 0]),
        semaphores,
        0,
        TOK,
    )
    out_sum.start()

    @pl.loop(0, PARTS)
    def _(row):
        rows = row_block(row)
        branch = cols_product(mixed_all[whole_block(place, row)], whole_matrix(rows_all))
        gated, bend = gelu_parts(pre[rows, WIDTH:])
        grad_pre[rows, WIDTH:] = (branch * take(hidden, rows) * bend).astype(low_type)
        put(carries, rows, branch * gated)

    @pl.loop(0, 4)
    def _(step):
        cut = pl.ds(pl.multiple_of(step * 512, 512), 512)
        rows_all[:, :, :, cut] = (
            rows_product(mixed[...], mixed_all[:, :, :, :, cut].reshape(SPAN, 512))
            .astype(low_type)
            .reshape(2, 2, LANES, 512)
        )

    pl.semaphore_wait(free.at[2], 1)
    rows_swap = move(Swap(), rows_all, down_landing.at[:, pl.ds(0, LANES)])
    rows_swap.start()
    normed_again = cube_one
    load_normed = pltpu.make_async_copy(normed_kept, normed_again, semaphores.take(1).at[0])
    load_normed.start()

    def advance_back(step, state):
        factors, carried = state
        across = pl.ds(TOK - 1 - step, PARTS, stride=TOK)
        carried = [
            carries[piece, across, :] + factors[piece] * before
            for piece, before in enumerate(carried)
        ]
        for piece, now in enumerate(carried):
            carries[piece, across, :] = now
        return ([decays[piece, across, :] for piece in range(WIDTH // 128)], carried)

    zeros = [jnp.zeros((PARTS, 128), full_type)] * (WIDTH // 128)
    lax.fori_loop(0, TOK, advance_back, (zeros, zeros), unroll=8)
    rows_swap.finish()
    add_swapped(rows_all, down_landing, place.core)
    rows_return = move(RowOwners(), rows_all, rows_back)
    rows_return.start()
    grad_aux[...] = jnp.zeros_like(grad_aux)
    grad_blocks[...] = jnp.zeros_like(grad_blocks)

    @pl.loop(0, PARTS)
    def _(row):
        rows = row_block(row)
        padded[0:8, :] = jnp.broadcast_to(states_all[row, 0:1, :], (8, WIDTH))
        padded[8 : 8 + TOK, :] = take(hidden, rows)
        low = conv[rows, :]
        recur, gate = gate_logits(low)
        log_decay = -8.0 * recur * soft
        decay = take(decays, rows)
        scale = jnp.sqrt(-small_expm1(2.0 * log_decay))
        conv_full = low.astype(full_type)
        carried = take(carries, rows)
        total = (
            carried * decay * padded[7 : 7 + TOK, :]
            - carried * gate * conv_full * (decay * decay) / scale
        )
        grad_aux[4:5, :] += jnp.sum(total * 8.0 * recur * slope, axis=0, keepdims=True)
        to_recur = (total * (-8.0 * soft) * recur * (1.0 - recur)).astype(low_type)
        to_input = (carried * scale * conv_full * gate * (1.0 - gate)).astype(low_type)
        both = jnp.concatenate([to_recur, to_input], axis=1)
        grad_blocks[...] += rows_product(low, both)
        back = carried * scale * gate + cols_product(both, whole_matrix(gates_all))
        first = decay[0:1, :] * carried[0:1, :]
        padded[0:8, :] = jnp.zeros((8, WIDTH), full_type)
        padded[8 : 8 + TOK, :] = back
        padded[8 + TOK :, :] = jnp.zeros((8, WIDTH), full_type)
        spread = taps[0] * padded[0 : 8 + TOK, :]
        for tap in range(1, 4):
            spread = spread + taps[tap] * padded[tap : tap + 8 + TOK, :]
        grad_pre[rows, 0:WIDTH] = spread[8:, :].astype(low_type)
        grad_states[row] = spread[0:8, :]
        grad_states[row, 0:1, :] = first
        padded[0:8, :] = states_all[row]
        padded[8 : 8 + TOK, :] = pre[rows, 0:WIDTH]
        for tap in range(4):
            grad_aux[tap : tap + 1, :] += jnp.sum(
                back * padded[8 - tap : 8 - tap + TOK, :], axis=0, keepdims=True
            )

    states_return = move(Peers(by_part), grad_states, states_back)
    states_return.start()
    blocks_low[...] = grad_blocks[...].astype(low_type).reshape(2, 2, LANES, 2 * WIDTH)
    out_sum.step(0)

    one_sums = [cube_sum(blocks, part) for part in range(2)]
    for part in range(2):

        @pl.loop(0, PARTS)
        def _(row):
            terms = grad_pre[pl.ds(pl.multiple_of(row * TOK + part * PART, PART), PART), :]
            for piece in range(COLUMNS):
                cut = pl.ds(piece * (width // 4), width // 4)
                blocks[whole_block(place, row) + (parts[part], cut)] = cols_product(
                    terms, whole_matrix(columns_all.at[piece])
                ).astype(low_type)

        one_sums[part].start()

    out_sum.step(1)
    one_sums[0].step(0)
    one_sums[1].step(0)
    out_sum.step(2, summed)

    @pl.loop(0, TOK // 32)
    def _(step):
        rows = pl.ds(pl.multiple_of(step * 32, 32), 32)
        cube_three[1, 1, 1, rows, :] = (after[rows, :] + summed[rows, :]).astype(low_type)

    local.start(cube_three.at[1, 1, 1], output)
    load_normed.wait()

    @pl.loop(0, 8)
    def _(step):
        cut = pl.ds(pl.multiple_of(step * 256, 256), 256)
        columns_all[step // 2, step % 2] = (
            rows_product(normed_again[:, :, :, :, cut].reshape(SPAN, 256), grad_pre[...])
            .astype(low_type)
            .reshape(4, 64, 2 * WIDTH)
        )

    mixer_swaps = [
        move(Swap(), columns_all, active),
        move(Swap(), blocks_low, blocks_landing),
    ]
    for item in mixer_swaps:
        item.start()
    one_sums[0].step(1)
    one_sums[1].step(1)
    mixer_swaps[0].finish()
    add_swapped(columns_all, active, place.core)
    columns_return = move(Owners(), columns_all, columns_back)
    columns_return.start()
    mixer_swaps[1].finish()
    add_swapped(blocks_low, blocks_landing, place.core)
    blocks_return = move(RowOwners(), blocks_low, blocks_back)
    blocks_return.start()
    one_sums[0].step(2, summed)
    one_sums[1].step(2, summed)
    load_tokens = pltpu.make_async_copy(
        tokens, cube_three.at[1, 0, 0], semaphores.take(1).at[0]
    )
    out_sum.finish()
    load_tokens.start()
    load_tokens.wait()

    @pl.loop(0, TOK // 32)
    def _(step):
        rows = pl.ds(pl.multiple_of(step * 32, 32), 32)
        values = cube_three[1, 0, 0, rows, :].astype(full_type)
        back, by_gain = norm_back(values, gains[0:1, :], summed[rows, :])
        cube_three[1, 0, 1, rows, :] = (grad[rows, :] + back).astype(low_type)
        grad_gains[0:1, :] += jnp.sum(by_gain, axis=0, keepdims=True)

    local.start(cube_three.at[1, 0, 1], grad_tokens)
    small_terms[...] = jnp.zeros_like(small_terms)
    for column, core, z in itertools.product(range(COLUMNS), range(2), range(4)):
        tile = (column * 8 + core * 4 + z) // 2
        small_terms[column, core, z, 0:2, 0:128] = grad_gains[:, tile * 128 : (tile + 1) * 128]
    for z in range(4):
        small_terms[place.part // 2, place.part % 2, z, 2:7, :] = grad_aux[0:5, :]
    small_swap = move(Swap(), small_terms, small_landing)
    small_swap.start()
    small_swap.finish()
    add_swapped(small_terms, small_landing, place.core)
    small_return = move(Owners(), small_terms, small_back)
    small_return.start()
    for part in range(2):
        one_sums[part].finish()
    for item in [states_return, small_return, columns_return, rows_return, blocks_return] + returns:
        item.finish()
    for copy in local.copies[1:]:
        copy.wait()


def block_call(arrays, rows, width, units):
    hbm = pl.BlockSpec(memory_space=pl.ANY)
    lanes = (WIDTH // 128, SPAN, 128)
    cube = (2, 2, 2, TOK, width)
    spread = (COLUMNS, 2, 4, rows)
    hidden_units = 4 * units
    outputs = [
        ((TOK, width), low_type),
        ((TOK, width), low_type),
        ((PARTS, 8, WIDTH), full_type),
        ((2, PARTS, 8, WIDTH), full_type),
        ((2, PARTS, rows, 2 * WIDTH), low_type),
        ((2, rows, PARTS * hidden_units), low_type),
        ((2, rows, PARTS * hidden_units), low_type),
        ((2, LANES, 2 * WIDTH), low_type),
        ((2, LANES, width), low_type),
        ((2, units, width), low_type),
        (cube, low_type),
        (cube, low_type),
    ]
    scratch = [
        (cube, low_type),
        (cube, low_type),
        (cube, low_type),
        (cube, low_type),
        ((2, 2, TOK, width), low_type),
        ((2, TOK, width), low_type),
        ((TOK, width), low_type),
        ((COLUMNS, 2, 4, 16, WIDTH), low_type),
        ((PARTS, 8, WIDTH), full_type),
        (spread + (2 * WIDTH,), low_type),
        ((2, 2, LANES, 2 * WIDTH), low_type),
        ((2, 2, LANES, width), low_type),
        (spread + (hidden_units,), low_type),
        (spread + (hidden_units,), low_type),
        ((2, 2, units, width), low_type),
        ((SPAN, 2 * WIDTH), full_type),
        ((SPAN, WIDTH), low_type),
        (lanes, full_type),
        ((SPAN, WIDTH), low_type),
        (lanes, full_type),
        (lanes, full_type),
        ((TOK + 16, WIDTH), full_type),
        ((TOK, width), full_type),
        ((TOK, width), full_type),
        ((TOK, width), full_type),
        ((8, WIDTH), full_type),
        ((2, width), full_type),
        ((2, width), full_type),
        ((8, WIDTH), full_type),
        ((4, 4, 64, hidden_units), low_type),
        ((4, 4, 64, hidden_units), low_type),
        ((4, 4, 64, hidden_units), low_type),
        ((2, units, width), low_type),
        ((SPAN, 2 * WIDTH), low_type),
        ((WIDTH, 2 * WIDTH), full_type),
        ((2, 2, LANES, 2 * WIDTH), low_type),
        ((2, LANES, 2 * WIDTH), low_type),
        ((PARTS, 8, WIDTH), full_type),
        ((COLUMNS, 2, 4, 8, WIDTH), full_type),
        ((COLUMNS, 4, 8, WIDTH), full_type),
    ]
    return pl.pallas_call(
        block_kernel,
        out_shape=[jax.ShapeDtypeStruct(shape, kind) for shape, kind in outputs],
        in_specs=[hbm] * len(arrays),
        out_specs=[hbm] * len(outputs),
        scratch_shapes=[pltpu.VMEM(shape, kind) for shape, kind in scratch]
        + [pltpu.SemaphoreType.DMA((480,)), pltpu.SemaphoreType.REGULAR((3,))],
        compiler_params=pltpu.CompilerParams(
            collective_id=0, has_side_effects=True, vmem_limit_bytes=VMEM_BYTES
        ),
        name="hawk_block",
    )(*arrays)


def to_lanes(array):
    chunks = array.reshape(array.shape[:-1] + (-1, CHUNK))
    pads = [(0, 0)] * (chunks.ndim - 1) + [(0, LANES - CHUNK)]
    return jnp.pad(chunks, pads).reshape(array.shape[:-1] + (-1,))


def from_lanes(array):
    chunks = array.reshape(array.shape[:-1] + (-1, LANES))
    return chunks[..., :CHUNK].reshape(array.shape[:-1] + (-1,))


def pad_rows(array, rows):
    return jnp.pad(array, ((0, rows - array.shape[0]), (0, 0)))


def halves(
    tokens,
    conv_state,
    recur_state,
    fresh_rows,
    gain_mixer,
    proj_input,
    proj_gate,
    conv_kernel,
    decay_param,
    gate_recur,
    gate_input,
    proj_output,
    gain_mlp,
    mlp_gate,
    mlp_up,
    mlp_down,
    cotangent,
):
    width = tokens.shape[2]
    rows = width // 32
    units = mlp_down.shape[0]
    keep = (1 - fresh_rows).astype(full_type)[0]

    columns = jnp.concatenate(
        [
            to_lanes(proj).reshape(rows, PARTS, WIDTH).transpose(1, 0, 2)
            for proj in (proj_input, proj_gate)
        ],
        axis=2,
    )
    zeros = jnp.zeros((CHUNK, 2 * LANES), low_type)
    first = lax.axis_index("narrow") < 2
    gates = jnp.concatenate(
        [
            jnp.where(chosen, to_lanes(gate), zeros)
            for gate in (gate_recur, gate_input)
            for chosen in (first, jnp.logical_not(first))
        ],
        axis=1,
    )
    z = lax.axis_index("narrow")
    taps = pad_rows(jnp.concatenate([conv_kernel, decay_param[None]], axis=0), 16)
    taps = lax.dynamic_update_slice(jnp.zeros((16, WIDTH), low_type), taps, (0, z * LANES))
    gain_rows = jnp.stack([gain_mixer, gain_mlp])
    small = lax.dynamic_update_slice(taps, gain_rows, (5, z % 2 * rows))
    state_rows = jnp.concatenate(
        [recur_state, jnp.zeros((4, recur_state.shape[1]), full_type), conv_state[0]], axis=0
    )
    states = to_lanes(state_rows * keep).reshape(8, PARTS, WIDTH).transpose(1, 0, 2)
    (
        output,
        grad_tokens,
        grad_states,
        small_back,
        columns_back,
        gate_back,
        up_back,
        blocks_back,
        rows_back,
        down_back,
        _,
        _,
    ) = block_call(
        (
            tokens[0],
            small,
            states,
            columns,
            pad_rows(gates, LANES),
            pad_rows(proj_output, LANES),
            mlp_gate,
            mlp_up,
            mlp_down,
            cotangent[0],
        ),
        rows,
        width,
        units,
    )
    grad_states = grad_states.transpose(1, 0, 2).reshape(8, PARTS * WIDTH)
    grad_states = from_lanes(grad_states) * keep
    small_sum = jnp.sum(small_back, axis=(0, 1))
    gain_sums = lax.dynamic_slice(small_sum, (0, z % 2 * rows), (2, rows))
    tap_sums = lax.dynamic_slice(small_sum, (2, z * LANES), (5, CHUNK))
    column_sum, gate_sum, up_sum, block_sum, out_sum, down_sum = (
        jnp.sum(term.astype(full_type), axis=0)
        for term in (columns_back, gate_back, up_back, blocks_back, rows_back, down_back)
    )
    column_sum = column_sum.transpose(1, 0, 2)
    pair = 2 * LANES
    gate_sums = [
        from_lanes(
            jnp.where(
                first,
                block_sum[:CHUNK, start : start + pair],
                block_sum[:CHUNK, start + pair : start + 2 * pair],
            )
        )
        for start in (0, WIDTH)
    ]
    return (
        output[None],
        grad_tokens[None],
        grad_states[None, 5:8],
        grad_states[0:1],
        gain_sums[0],
        from_lanes(column_sum[:, :, :WIDTH]).reshape(rows, -1),
        from_lanes(column_sum[:, :, WIDTH:]).reshape(rows, -1),
        tap_sums[0:4],
        tap_sums[4],
        gate_sums[0],
        gate_sums[1],
        out_sum[:CHUNK],
        gain_sums[1],
        gate_sum,
        up_sum,
        down_sum,
    )


def solution(mesh):
    sizes = (mesh.shape["wide"], mesh.shape["narrow"])
    return jax.shard_map(
        halves if sizes == (2 * COLUMNS, 2 * LOWS) else shards,
        mesh=mesh,
        in_specs=(
            P(("wide", "narrow"), None, None),
            P(("wide", "narrow"), None, None),
            P(("wide", "narrow"), None),
            P(("wide", "narrow")),
            P(("wide", "narrow")),
            P(("wide", "narrow"), None),
            P(("wide", "narrow"), None),
            P(None, ("wide", "narrow")),
            P(("wide", "narrow")),
            P(("wide", "narrow"), None),
            P(("wide", "narrow"), None),
            P(("wide", "narrow"), None),
            P(("wide", "narrow")),
            P(("wide", "narrow"), None),
            P(("wide", "narrow"), None),
            P(("wide", "narrow"), None),
            P(("wide", "narrow"), None, None),
        ),
        out_specs=(
            P(("wide", "narrow"), None, None),
            P(("wide", "narrow"), None, None),
            P(("wide", "narrow"), None, None),
            P(("wide", "narrow"), None),
            P(("wide", "narrow")),
            P(("wide", "narrow"), None),
            P(("wide", "narrow"), None),
            P(None, ("wide", "narrow")),
            P(("wide", "narrow")),
            P(("wide", "narrow"), None),
            P(("wide", "narrow"), None),
            P(("wide", "narrow"), None),
            P(("wide", "narrow")),
            P(("wide", "narrow"), None),
            P(("wide", "narrow"), None),
            P(("wide", "narrow"), None),
        ),
        check_vma=False,
    )
```

```python
import functools
import itertools
from functools import reduce

import jax
import jax.numpy as jnp
from jax import lax
from jax.experimental import pallas as pl
from jax.experimental.pallas import tpu as pltpu
from jax.sharding import PartitionSpec as P

BLOCKS = 16
BLK = 176
SCAN_BLOCK = 16


epsilon = 1e-06
contract_rows = (((0,), (0,)), ((), ()))
contract_cols = (((1,), (1,)), ((), ()))


def plain_product(left_side, right_side):
    return jnp.dot(left_side, right_side, preferred_element_type=jnp.float32)


def rows_product(left_side, right_side):
    return lax.dot_general(left_side, right_side, contract_rows, preferred_element_type=jnp.float32)


def cols_product(left_side, right_side):
    return lax.dot_general(left_side, right_side, contract_cols, preferred_element_type=jnp.float32)


def norm_scale(values, gain_vec):
    return (
        values * lax.rsqrt(jnp.mean(values * values, axis=-1, keepdims=True) + epsilon) * gain_vec
    )


def conv_apply(values, history, kernel):
    joined = jnp.concatenate([history, values], axis=0)
    length = values.shape[0]
    kernel_taps = kernel.shape[0]
    result = jnp.zeros_like(values)
    for offset in range(kernel_taps):
        first_row = kernel_taps - 1 - offset
        result = result + kernel[offset] * joined[first_row : first_row + length]
    return result


def block_mix(values, matrix):
    length = values.shape[0]
    mixed_out = jnp.einsum(
        "tki,kij->tkj",
        values.reshape(length, BLOCKS, BLK),
        matrix.reshape(BLOCKS, BLK, BLK),
        preferred_element_type=jnp.float32,
    )
    return mixed_out.reshape(length, BLOCKS * BLK)


def block_back(grad_logits, matrix):
    length = grad_logits.shape[0]
    spread_back = jnp.einsum(
        "tkj,kij->tki",
        grad_logits.reshape(length, BLOCKS, BLK),
        matrix.reshape(BLOCKS, BLK, BLK),
        preferred_element_type=jnp.float32,
    )
    return spread_back.reshape(length, BLOCKS * BLK)


def block_grad(values, grad_logits):
    length = values.shape[0]
    summed = jnp.einsum(
        "tki,tkj->kij",
        values.reshape(length, BLOCKS, BLK),
        grad_logits.reshape(length, BLOCKS, BLK),
        preferred_element_type=jnp.float32,
    )
    return summed.reshape(BLOCKS * BLK, BLK)


def gate_apply(recur_logits, input_logits, conv_float, decay_float):
    log_decay = -8.0 * jax.nn.sigmoid(recur_logits) * jax.nn.softplus(-decay_float)
    scan_in = jnp.sqrt(-jnp.expm1(2.0 * log_decay)) * jax.nn.sigmoid(input_logits) * conv_float
    return (log_decay, scan_in)


def branch_apply(hidden, gate_logits):
    return hidden * jax.nn.gelu(gate_logits)


def mlp_apply(gate_part, up_part):
    return jax.nn.gelu(gate_part) * up_part


def block_scan(log_decay, scan_in, initial):
    length, channels = scan_in.shape
    block_count = length // SCAN_BLOCK
    positions = jnp.arange(SCAN_BLOCK)
    causal = (positions[:, None] >= positions[None, :])[:, :, None]

    def advance(carried, pieces):
        decay_piece, input_piece = pieces
        cumulative = jnp.cumsum(decay_piece, axis=0)
        spread = jnp.where(causal, cumulative[:, None, :] - cumulative[None, :, :], 0.0)
        factors = jnp.where(causal, jnp.exp(spread), 0.0)
        states = jnp.sum(factors * input_piece[None, :, :], axis=1) + jnp.exp(cumulative) * carried
        return (states[-1], states)

    last_state, states = lax.scan(
        advance,
        initial,
        (
            log_decay.reshape(block_count, SCAN_BLOCK, channels),
            scan_in.reshape(block_count, SCAN_BLOCK, channels),
        ),
    )
    return states.reshape(length, channels)


def scan_back(log_decay, hidden, initial, grad_hidden):
    following = jnp.concatenate([log_decay[1:], jnp.zeros_like(log_decay[:1])], axis=0)
    carried = block_scan(following[::-1], grad_hidden[::-1], jnp.zeros_like(initial))[::-1]
    previous = jnp.concatenate([initial[None], hidden[:-1]], axis=0)
    grad_log_decay = carried * jnp.exp(log_decay) * previous
    grad_initial = jnp.exp(log_decay[0]) * carried[0]
    return (grad_log_decay, carried, grad_initial)


def mixer_forward(tokens_row, history, initial, keep_row, mixer):
    (
        gain_vec,
        proj_input,
        proj_gate,
        conv_kernel,
        decay_param,
        gate_recur,
        gate_input,
        proj_output,
    ) = mixer
    values = tokens_row.astype(jnp.float32)
    normed_one = norm_scale(values, gain_vec.astype(jnp.float32)).astype(jnp.bfloat16)
    branch_in = plain_product(normed_one, proj_input)
    gate_logits = plain_product(normed_one, proj_gate)
    history_kept = history * keep_row
    kernel_float = conv_kernel.astype(jnp.float32)
    conv_out = conv_apply(branch_in, history_kept, kernel_float).astype(jnp.bfloat16)
    recur_logits = block_mix(conv_out, gate_recur)
    input_logits = block_mix(conv_out, gate_input)
    decay_float = decay_param.astype(jnp.float32)
    conv_float = conv_out.astype(jnp.float32)
    log_decay, scan_in = gate_apply(recur_logits, input_logits, conv_float, decay_float)
    initial_kept = initial * keep_row
    hidden = block_scan(log_decay, scan_in, initial_kept)
    mixed_out = branch_apply(hidden, gate_logits).astype(jnp.bfloat16)
    after_mixer = values + plain_product(mixed_out, proj_output)
    kept = (
        values,
        normed_one,
        branch_in,
        gate_logits,
        history_kept,
        kernel_float,
        conv_out,
        conv_float,
        recur_logits,
        input_logits,
        decay_float,
        log_decay,
        initial_kept,
        hidden,
        mixed_out,
    )
    return (after_mixer, kept)


def mlp_forward(after_mixer, mlp):
    gain_vec, mlp_gate, mlp_up, mlp_down = mlp
    normed_two = norm_scale(after_mixer, gain_vec.astype(jnp.float32)).astype(jnp.bfloat16)
    gate_part = plain_product(normed_two, mlp_gate)
    up_part = plain_product(normed_two, mlp_up)
    activated = mlp_apply(gate_part, up_part).astype(jnp.bfloat16)
    result = after_mixer + plain_product(activated, mlp_down)
    return (result, (after_mixer, normed_two, gate_part, up_part, activated))


def mlp_backward(grad_result, mlp, kept):
    gain_vec, mlp_gate, mlp_up, mlp_down = mlp
    after_mixer, normed_two, gate_part, up_part, activated = kept
    grad_activated = cols_product(grad_result, mlp_down)
    grad_down = rows_product(activated, grad_result)
    unused, mlp_pull = jax.vjp(mlp_apply, gate_part, up_part)
    grad_gate_part, grad_up_part = mlp_pull(grad_activated)
    grad_gate_part = grad_gate_part.astype(jnp.bfloat16)
    grad_up_part = grad_up_part.astype(jnp.bfloat16)
    grad_normed = cols_product(grad_gate_part, mlp_gate) + cols_product(grad_up_part, mlp_up)
    grad_mlp_gate = rows_product(normed_two, grad_gate_part)
    grad_mlp_up = rows_product(normed_two, grad_up_part)
    unused, norm_pull = jax.vjp(norm_scale, after_mixer, gain_vec.astype(jnp.float32))
    grad_values, grad_gain = norm_pull(grad_normed)
    grad_after = grad_result.astype(jnp.float32) + grad_values
    return (grad_after, (grad_gain, grad_mlp_gate, grad_mlp_up, grad_down))


def mixer_backward(grad_after, mixer, kept, keep_row):
    (
        gain_vec,
        proj_input,
        proj_gate,
        conv_kernel,
        decay_param,
        gate_recur,
        gate_input,
        proj_output,
    ) = mixer
    (
        values,
        normed_one,
        branch_in,
        gate_logits,
        history_kept,
        kernel_float,
        conv_out,
        conv_float,
        recur_logits,
        input_logits,
        decay_float,
        log_decay,
        initial_kept,
        hidden,
        mixed_out,
    ) = kept
    grad_mixed = grad_after.astype(jnp.bfloat16)
    grad_proj_output = rows_product(mixed_out, grad_mixed)
    grad_branch = cols_product(grad_mixed, proj_output)
    unused, branch_pull = jax.vjp(branch_apply, hidden, gate_logits)
    grad_hidden, grad_gate_logits = branch_pull(grad_branch)
    grad_gate_logits = grad_gate_logits.astype(jnp.bfloat16)
    grad_log_decay, grad_scan_in, grad_initial = scan_back(
        log_decay, hidden, initial_kept, grad_hidden
    )
    unused, gate_pull = jax.vjp(gate_apply, recur_logits, input_logits, conv_float, decay_float)
    grad_recur_logits, grad_input_logits, grad_conv, grad_decay = gate_pull(
        (grad_log_decay, grad_scan_in)
    )
    grad_recur_logits = grad_recur_logits.astype(jnp.bfloat16)
    grad_input_logits = grad_input_logits.astype(jnp.bfloat16)
    grad_gate_recur = block_grad(conv_out, grad_recur_logits)
    grad_gate_input = block_grad(conv_out, grad_input_logits)
    grad_conv = (
        grad_conv
        + block_back(grad_recur_logits, gate_recur)
        + block_back(grad_input_logits, gate_input)
    )
    unused, conv_pull = jax.vjp(conv_apply, branch_in, history_kept, kernel_float)
    grad_branch_in, grad_history, grad_kernel = conv_pull(grad_conv)
    grad_branch_low = grad_branch_in.astype(jnp.bfloat16)
    grad_proj_input = rows_product(normed_one, grad_branch_low)
    grad_proj_gate = rows_product(normed_one, grad_gate_logits)
    grad_normed = cols_product(grad_branch_low, proj_input) + cols_product(
        grad_gate_logits, proj_gate
    )
    unused, norm_pull = jax.vjp(norm_scale, values, gain_vec.astype(jnp.float32))
    grad_values, grad_gain = norm_pull(grad_normed)
    grad_tokens = (grad_after + grad_values).astype(jnp.bfloat16)
    weight_terms = (
        grad_gain,
        grad_proj_input,
        grad_proj_gate,
        grad_kernel,
        grad_decay,
        grad_gate_recur,
        grad_gate_input,
        grad_proj_output,
    )
    return (grad_tokens, grad_history * keep_row, grad_initial * keep_row, weight_terms)


def add_terms(first_terms, second_terms):
    return tuple(
        (left_side + right_side for left_side, right_side in zip(first_terms, second_terms))
    )


def shards(
    tokens,
    conv_state,
    recur_state,
    fresh_rows,
    gain_mixer,
    proj_input,
    proj_gate,
    conv_kernel,
    decay_param,
    gate_recur,
    gate_input,
    proj_output,
    gain_mlp,
    mlp_gate,
    mlp_up,
    mlp_down,
    cotangent,
):
    mixer_full = (
        lax.all_gather(gain_mixer, ("wide", "narrow"), axis=0, tiled=True),
        lax.all_gather(proj_input, ("wide", "narrow"), axis=0, tiled=True),
        lax.all_gather(proj_gate, ("wide", "narrow"), axis=0, tiled=True),
        lax.all_gather(conv_kernel, ("wide", "narrow"), axis=1, tiled=True),
        lax.all_gather(decay_param, ("wide", "narrow"), axis=0, tiled=True),
        lax.all_gather(gate_recur, ("wide", "narrow"), axis=0, tiled=True),
        lax.all_gather(gate_input, ("wide", "narrow"), axis=0, tiled=True),
        lax.all_gather(proj_output, ("wide", "narrow"), axis=0, tiled=True),
    )
    mlp_full = (
        lax.all_gather(gain_mlp, ("wide", "narrow"), axis=0, tiled=True),
        lax.all_gather(mlp_gate, ("wide", "narrow"), axis=0, tiled=True),
        lax.all_gather(mlp_up, ("wide", "narrow"), axis=0, tiled=True),
        lax.all_gather(mlp_down, ("wide", "narrow"), axis=0, tiled=True),
    )
    keep_rows = (1 - fresh_rows).astype(jnp.float32)
    stored = []
    row_index = 0
    after_mixer, mixer_kept = mixer_forward(
        tokens[row_index],
        conv_state[row_index],
        recur_state[row_index],
        keep_rows[row_index],
        mixer_full,
    )
    result, mlp_kept = mlp_forward(after_mixer, mlp_full)
    outputs = [result.astype(jnp.bfloat16)]
    stored.append((mixer_kept, mlp_kept))
    mixer_back = (
        lax.all_gather(gain_mixer, ("wide", "narrow"), axis=0, tiled=True),
        lax.all_gather(proj_input, ("wide", "narrow"), axis=0, tiled=True),
        lax.all_gather(proj_gate, ("wide", "narrow"), axis=0, tiled=True),
        lax.all_gather(conv_kernel, ("wide", "narrow"), axis=1, tiled=True),
        lax.all_gather(decay_param, ("wide", "narrow"), axis=0, tiled=True),
        lax.all_gather(gate_recur, ("wide", "narrow"), axis=0, tiled=True),
        lax.all_gather(gate_input, ("wide", "narrow"), axis=0, tiled=True),
        lax.all_gather(proj_output, ("wide", "narrow"), axis=0, tiled=True),
    )
    mlp_back = (
        lax.all_gather(gain_mlp, ("wide", "narrow"), axis=0, tiled=True),
        lax.all_gather(mlp_gate, ("wide", "narrow"), axis=0, tiled=True),
        lax.all_gather(mlp_up, ("wide", "narrow"), axis=0, tiled=True),
        lax.all_gather(mlp_down, ("wide", "narrow"), axis=0, tiled=True),
    )
    stored = []
    row_index = 0
    after_mixer, mixer_kept = mixer_forward(
        tokens[row_index],
        conv_state[row_index],
        recur_state[row_index],
        keep_rows[row_index],
        mixer_back,
    )
    unused, mlp_kept = mlp_forward(after_mixer, mlp_back)
    stored.append((mixer_kept, mlp_kept))
    row_index = 0
    grad_after, row_terms = mlp_backward(cotangent[row_index], mlp_back, stored[row_index][1])
    after_grads = [grad_after]
    mlp_terms = [row_terms]
    mlp_total = reduce(add_terms, mlp_terms)
    mlp_sums = (
        lax.psum_scatter(mlp_total[0], ("wide", "narrow"), scatter_dimension=0, tiled=True),
        lax.psum_scatter(mlp_total[1], ("wide", "narrow"), scatter_dimension=0, tiled=True),
        lax.psum_scatter(mlp_total[2], ("wide", "narrow"), scatter_dimension=0, tiled=True),
        lax.psum_scatter(mlp_total[3], ("wide", "narrow"), scatter_dimension=0, tiled=True),
    )
    row_index = 0
    grad_tokens, grad_history, grad_initial, row_terms = mixer_backward(
        after_grads[row_index], mixer_back, stored[row_index][0], keep_rows[row_index]
    )
    token_grads = [grad_tokens]
    history_grads = [grad_history]
    initial_grads = [grad_initial]
    mixer_terms = [row_terms]
    mixer_total = reduce(add_terms, mixer_terms)
    mixer_sums = (
        lax.psum_scatter(mixer_total[0], ("wide", "narrow"), scatter_dimension=0, tiled=True),
        lax.psum_scatter(mixer_total[1], ("wide", "narrow"), scatter_dimension=0, tiled=True),
        lax.psum_scatter(mixer_total[2], ("wide", "narrow"), scatter_dimension=0, tiled=True),
        lax.psum_scatter(mixer_total[3], ("wide", "narrow"), scatter_dimension=1, tiled=True),
        lax.psum_scatter(mixer_total[4], ("wide", "narrow"), scatter_dimension=0, tiled=True),
        lax.psum_scatter(mixer_total[5], ("wide", "narrow"), scatter_dimension=0, tiled=True),
        lax.psum_scatter(mixer_total[6], ("wide", "narrow"), scatter_dimension=0, tiled=True),
        lax.psum_scatter(mixer_total[7], ("wide", "narrow"), scatter_dimension=0, tiled=True),
    )
    return (
        jnp.stack(outputs),
        jnp.stack(token_grads),
        jnp.stack(history_grads),
        jnp.stack(initial_grads),
        mixer_sums[0],
        mixer_sums[1],
        mixer_sums[2],
        mixer_sums[3],
        mixer_sums[4],
        mixer_sums[5],
        mixer_sums[6],
        mixer_sums[7],
        mlp_sums[0],
        mlp_sums[1],
        mlp_sums[2],
        mlp_sums[3],
    )


COLUMNS = 4
LOWS = 2
PARTS = COLUMNS * LOWS
TOK = 128
CHUNK = 88
LANES = 96
WIDTH = 4 * LANES
SPAN = PARTS * TOK
MESH = pl.DeviceIdType.MESH
VMEM_BYTES = 63 * 1024 * 1024 + 896 * 1024
low_type = jnp.bfloat16
full_type = jnp.float32


class Place:
    def __init__(self):
        wide = lax.axis_index("wide")
        self.z = lax.axis_index("narrow")
        self.column, self.core = wide // 2, wide % 2
        self.half, self.low = self.z // 2, self.z % 2
        self.part = self.column * 2 + self.low
        self.index = wide * 4 + self.z
        self.own = (self.column // 2, self.column % 2, self.low)

    def shifted(self, by_y, by_x, by_low, by_half):
        column = (self.column // 2 + by_y) % 2 * 2 + (self.column % 2 + by_x) % 2
        low, half = (self.low + by_low) % 2, (self.half + by_half) % 2
        return (column, low, half)

    def neighbour(self, axis):
        y, x, low = (1 - at if axis == here else at for here, at in enumerate(self.own))
        return (y * 4 + x * 2 + self.core, self.half * 2 + low)

    def cube(self, fixed, other=None):
        return tuple(
            1 - at if axis == other else at if axis in fixed else slice(None)
            for axis, at in enumerate(self.own)
        )

    def sibling(self):
        return (self.column * 2 + 1 - self.core, self.z)


def greet_all(place):
    barrier = pltpu.get_barrier_semaphore()

    @pl.loop(1, 32)
    def _(step):
        other = (place.index + step) % 32
        pl.semaphore_signal(
            barrier, inc=1, device_id=(other // 4, other % 4), device_id_type=MESH
        )

    pl.semaphore_wait(barrier, 31)


def remote(source, target, send, receive, device):
    return pltpu.make_async_remote_copy(
        src_ref=source,
        dst_ref=target,
        send_sem=send,
        recv_sem=receive,
        device_id=device,
        device_id_type=MESH,
    )


def await_bytes(view, semaphore):
    pltpu.make_async_copy(view, view, semaphore).wait()


SHIFTS = tuple(
    near + (half,) for near in itertools.product(range(2), repeat=3) for half in (1, 0)
)


def row_pieces(place, source, slot_of, sems, copies, block_of=None):
    rows_all = source.shape[-2]
    step = rows_all // 3
    device = lambda half: (place.column * 2 + place.low, half * 2 + place.core)

    def piece(rows, half):
        block = source.at[rows] if block_of is None else block_of(half, rows)
        copy = remote(block, slot_of(half, rows), sems.at[0], sems.at[1], device(half))
        own = (place.low == place.core) & (place.half == half)

        @pl.when(own)
        def _():
            pltpu.make_async_copy(block, slot_of(half, rows), sems.at[1]).start()

        @pl.when(jnp.logical_not(own))
        def _():
            copy.start()

        copies.append((own, copy))

    return [
        functools.partial(piece, pl.ds(third * step, step), half)
        for third in range(3)
        for half in range(2)
    ]


def wait_pieces(copies):
    for own, copy in copies:

        @pl.when(jnp.logical_not(own))
        def _():
            copy.wait_send()


class Spread:
    def __init__(self, pick):
        self.pick = pick

    def pieces(self, place, source, target, sems):
        self.copies = []
        slot = target.at[place.column, place.core, place.z]

        def piece(shift):
            column, low, half = place.shifted(*shift)
            block = self.pick(source, column * 2 + low)
            if any(shift):
                copy = remote(
                    block, slot, sems.at[0], sems.at[1], (column * 2 + place.core, half * 2 + low)
                )
                copy.start()
                self.copies.append(copy)
            else:
                pltpu.make_async_copy(block, slot, sems.at[1]).start()

        return [functools.partial(piece, shift) for shift in SHIFTS]

    def relay(self, place, source, target, sems):
        mine = target.at[:, place.core]
        await_bytes(mine, sems.at[1])
        self.passed = remote(mine, mine, sems.at[2], sems.at[3], place.sibling())
        self.passed.start()

    def finish(self, place, source, target, sems):
        self.passed.wait()
        for copy in self.copies:
            copy.wait_send()


class RowSpread:
    def pieces(self, place, source, target, sems):
        self.copies = []
        slot = target.at[place.half, place.low]
        return row_pieces(place, source, lambda half, rows: slot.at[rows], sems, self.copies)

    def relay(self, place, source, target, sems):
        mine = target.at[:, place.core]
        await_bytes(mine, sems.at[1])
        self.passed = remote(mine, mine, sems.at[2], sems.at[3], place.sibling())
        self.passed.start()

    def finish(self, place, source, target, sems):
        self.passed.wait()
        wait_pieces(self.copies)


class Peers:
    def __init__(self, pick):
        self.pick = pick

    def start(self, place, source, target, sems):
        self.copies = []
        slot = target.at[place.part]
        for shift in itertools.product(range(2), repeat=3):
            column, low, half = place.shifted(*shift, 0)
            block = self.pick(source, column * 2 + low)
            if any(shift):
                copy = remote(
                    block, slot, sems.at[0], sems.at[1], (column * 2 + place.core, half * 2 + low)
                )
                copy.start()
                self.copies.append(copy)
            else:
                pltpu.make_async_copy(block, slot, sems.at[1]).start()

    def relay(self, place, source, target, sems):
        pass

    def finish(self, place, source, target, sems):
        await_bytes(target, sems.at[1])
        for copy in self.copies:
            copy.wait_send()


class Swap:
    def start(self, place, source, target, sems):
        self.copy = remote(
            source.at[:, 1 - place.core], target, sems.at[0], sems.at[1], place.sibling()
        )
        self.copy.start()

    def relay(self, place, source, target, sems):
        pass

    def finish(self, place, source, target, sems):
        self.copy.wait()


class Owners:
    def pieces(self, place, source, target, sems):
        self.copies = []
        if len(target.shape) == 3:
            width = source.shape[-1]
            cut = pl.ds(pl.multiple_of(place.part * width, 128), width)
            slot = target.at[place.half, :, cut]
        else:
            slot = target.at[place.half, place.part]

        def piece(shift):
            column, low, half = place.shifted(*shift)
            z = half * 2 + low
            block = source.at[column, place.core, z]
            if any(shift):
                copy = remote(
                    block, slot, sems.at[0], sems.at[1], (column * 2 + place.core, z)
                )
                copy.start()
                self.copies.append(copy)
            else:
                pltpu.make_async_copy(block, slot, sems.at[1]).start()

        return [functools.partial(piece, shift) for shift in SHIFTS]

    def finish(self, place, source, target, sems):
        await_bytes(target, sems.at[1])
        for copy in self.copies:
            copy.wait_send()


class RowOwners:
    def pieces(self, place, source, target, sems):
        self.copies = []
        slot = target.at[place.half]
        return row_pieces(
            place,
            source,
            lambda half, rows: slot.at[rows],
            sems,
            self.copies,
            lambda half, rows: source.at[half, place.core, rows],
        )

    def finish(self, place, source, target, sems):
        await_bytes(target, sems.at[1])
        wait_pieces(self.copies)


PACE = (6, 0, 0, 3, 1, 1)
PART = TOK // 2


class Semaphores:
    def __init__(self, array):
        self.array, self.used = array, 0

    def take(self, count):
        taken = self.array.at[pl.ds(self.used, count)]
        self.used += count
        return taken


LIGHT = ((2, 0, 1), (2, 1, 0), (0, 2, 1), (1, 2, 0))
EVEN = ((0, 1, 2), (1, 2, 0), (2, 0, 1))


def cuts(width, count):
    ends = [-(-(width // 128) * step // count) * 128 for step in range(count + 1)]
    return [pl.ds(start, end - start) for start, end in zip(ends, ends[1:])]


class CubeGather:
    def __init__(self, place, buffer, semaphores, rows, orders=LIGHT):
        self.place, self.buffer, self.copies = place, buffer, []
        self.rows, self.orders = rows, orders
        self.cuts = cuts(buffer.shape[4], len(orders))
        self.sems = semaphores.take(6 * len(orders))

    def step(self, number):
        routes = len(self.orders)
        for route, (axes, cut) in enumerate(zip(self.orders, self.cuts)):
            if number > 0:
                self.copies[routes * (number - 1) + route].wait_recv()
            region = self.buffer.at[self.place.cube(axes[number:]) + (self.rows, cut)]
            index = routes * number + route
            copy = remote(
                region,
                region,
                self.sems.at[index],
                self.sems.at[3 * routes + index],
                self.place.neighbour(axes[number]),
            )
            copy.start()
            self.copies.append(copy)

    def finish(self):
        for copy in self.copies[2 * len(self.orders) :]:
            copy.wait_recv()
        for copy in self.copies:
            copy.wait_send()


class CubeSum:
    def __init__(self, place, blocks, landings, semaphores, start, count, orders=LIGHT):
        self.place, self.blocks, self.landings, self.copies = place, blocks, landings, []
        self.first, self.count = start, count
        self.orders = [axes[::-1] for axes in orders]
        self.cuts = cuts(blocks.shape[4], len(orders))
        self.sems = semaphores.take(6 * len(orders))

    def send(self, number, route):
        axes, cut, routes = self.orders[route], self.cuts[route], len(self.orders)
        index = routes * number + route
        rows = pl.ds(self.first, self.count)
        landing = self.landings[number]
        copy = remote(
            self.blocks.at[self.place.cube(axes[:number], axes[number]) + (rows, cut)],
            landing.at[(slice(None),) * (2 - number) + (rows, cut)],
            self.sems.at[index],
            self.sems.at[3 * routes + index],
            self.place.neighbour(axes[number]),
        )
        copy.start()
        self.copies.append(copy)

    def start(self):
        for route in range(len(self.orders)):
            self.send(0, route)

    def step(self, number, result=None):
        for route, (axes, cut) in enumerate(zip(self.orders, self.cuts)):
            self.copies[len(self.orders) * number + route].wait_recv()
            landing = self.landings[number]
            for picks in itertools.product(range(2), repeat=2 - number):
                chosen = iter(picks)
                index = tuple(
                    self.place.own[axis] if axis in axes[: number + 1] else next(chosen)
                    for axis in range(3)
                )

                @pl.loop(0, self.count // 32)
                def _(block):
                    rows = pl.ds(pl.multiple_of(self.first + block * 32, 32), 32)
                    total = self.blocks[index + (rows, cut)].astype(full_type) + landing[
                        picks + (rows, cut)
                    ].astype(full_type)
                    if number < 2:
                        self.blocks[index + (rows, cut)] = total.astype(low_type)
                    else:
                        result[rows, cut] = total

            if number < 2:
                self.send(number + 1, route)

    def finish(self):
        for copy in self.copies:
            copy.wait_send()


class Move:
    def __init__(self, place, plan, source, target, semaphores):
        self.plan, self.arguments = plan, (place, source, target, semaphores.take(4))

    def pieces(self):
        return self.plan.pieces(*self.arguments)

    def start(self):
        if hasattr(self.plan, "start"):
            self.plan.start(*self.arguments)
        else:
            for piece in self.pieces():
                piece()

    def relay(self):
        self.plan.relay(*self.arguments)

    def finish(self):
        self.plan.finish(*self.arguments)


class Pump:
    def __init__(self, wide, tall):
        wide = [item.pieces() for item in wide]
        tall = [item.pieces() for item in tall]
        self.units = []
        for step in range(8):
            self.units.append([piece for each in wide for piece in each[2 * step : 2 * step + 2]])
            if step % 3 == 1:
                third = step // 3
                self.units.append(
                    [piece for each in tall for piece in each[2 * third : 2 * third + 2]]
                )

    def start(self, count):
        for _ in range(min(count, len(self.units))):
            for piece in self.units.pop(0):
                piece()


class Local:
    def __init__(self, semaphores):
        self.semaphores, self.copies = semaphores, []

    def start(self, source, target):
        copy = pltpu.make_async_copy(source, target, self.semaphores.take(1).at[0])
        copy.start()
        self.copies.append(copy)
        return copy

    def finish(self):
        for copy in self.copies:
            copy.wait()


def whole(source, part):
    return source


def by_part(source, part):
    return source.at[part]


def by_columns(source, part):
    width = source.shape[1] // PARTS
    return source.at[:, pl.ds(pl.multiple_of(part * width, 128), width)]


def row_block(row):
    return pl.ds(pl.multiple_of(row * TOK, TOK), TOK)


def small_expm1(values):
    near = values * (
        1.0
        + values
        * (0.5 + values * (1 / 6 + values * (1 / 24 + values * (1 / 120 + values * (1 / 720)))))
    )
    return jnp.where(values > -0.25, near, jnp.exp(values) - 1.0)


def gelu_parts(values):
    scale = 0.7978845608028654
    bent = jnp.tanh(scale * (values + 0.044715 * values * values * values))
    slope = 0.5 * (1.0 + bent) + 0.5 * values * (1.0 - bent * bent) * scale * (
        1.0 + 3 * 0.044715 * values * values
    )
    return (0.5 * values * (1.0 + bent), slope)


def put(array, rows, values):
    for piece in range(WIDTH // 128):
        array[piece, rows, :] = values[:, piece * 128 : (piece + 1) * 128]


def take(array, rows):
    return jnp.concatenate([array[piece, rows, :] for piece in range(WIDTH // 128)], axis=1)


def taps_of(aux):
    return [aux[tap : tap + 1, :] for tap in range(4)]


def placed_sum(gathered, place, row):
    owners = [
        gathered[place.part // 2, place.part % 2, z, row : row + 1, :].astype(full_type)
        for z in range(4)
    ]
    return owners[0] + owners[1] + owners[2] + owners[3]


def placed_gain(gathered, row):
    pieces = []
    for column, core, pair in itertools.product(range(COLUMNS), range(2), range(2)):
        both = [
            gathered[column, core, 2 * pair + odd, row : row + 1, 0:128].astype(full_type)
            for odd in range(2)
        ]
        pieces.append(both[0] + both[1])
    return jnp.concatenate(pieces, axis=1)


def scaled_norm(values, gain):
    scale = lax.rsqrt(jnp.mean(values * values, axis=1, keepdims=True) + epsilon)
    return values * scale * gain


def whole_block(place, row):
    return (row // 4, row // 2 % 2, row % 2)


def add_swapped(array, landing, core):
    rows, columns = array.shape[-2:]
    inner = array.shape[2] if len(array.shape) == 5 else 1
    outer = array.shape[0]
    chunk = 32 if columns > 1024 and rows % 32 == 0 else 16 if rows % 16 == 0 else 8

    @pl.loop(0, outer * inner * (rows // chunk))
    def _(step):
        part = pl.ds(pl.multiple_of(step % (rows // chunk) * chunk, chunk), chunk)
        first = step // (rows // chunk)
        if len(array.shape) == 5:
            here, there = (first // inner, core, first % inner, part), (first // inner, first % inner, part)
        else:
            here, there = (first, core, part), (first, part)
        total = array[here].astype(full_type) + landing[there].astype(full_type)
        array[here] = total.astype(array.dtype)


def norm_back(values, gain, grad):
    scale = lax.rsqrt(jnp.mean(values * values, axis=1, keepdims=True) + epsilon)
    inner = grad * gain
    along = jnp.mean(inner * values, axis=1, keepdims=True)
    return (scale * inner - values * (scale * scale * scale * along), grad * values * scale)


def block_kernel(
    tokens,
    small,
    states,
    columns,
    gates,
    out_rows,
    mlp_gate,
    mlp_up,
    mlp_down,
    cotangent,
    output,
    grad_tokens,
    states_back,
    small_back,
    columns_back,
    gate_back,
    up_back,
    blocks_back,
    rows_back,
    down_back,
    normed_kept,
    cot_kept,
    cube_one,
    cube_two,
    cube_three,
    blocks,
    landing_one,
    landing_two,
    landing_three,
    small_all,
    states_all,
    columns_all,
    gates_all,
    rows_all,
    gate_all,
    up_all,
    down_all,
    pre,
    conv,
    hidden,
    mixed,
    decays,
    carries,
    padded,
    after,
    grad,
    summed,
    aux,
    gains,
    grad_gains,
    grad_aux,
    active,
    grad_gate,
    grad_up,
    down_landing,
    grad_pre,
    grad_blocks,
    blocks_low,
    blocks_landing,
    grad_states,
    small_terms,
    small_landing,
    sems,
    free,
):
    place = Place()
    semaphores = Semaphores(sems)
    local = Local(semaphores)
    width = tokens.shape[1]
    hidden_units = gate_all.shape[-1]
    tokens_all = cube_one
    normed = cube_two
    two_all = cube_three

    def move(plan, source, target):
        return Move(place, plan, source, target, semaphores)

    def whole_matrix(array):
        return array[...].reshape(-1, array.shape[-1])

    own_tokens = tokens_all.at[place.own]
    load = pltpu.make_async_copy(tokens, own_tokens, semaphores.take(1).at[0])
    load.start()
    greet_all(place)
    load.wait()
    every = pl.ds(0, TOK)
    parts = (pl.ds(0, PART), pl.ds(PART, PART))
    tokens_gather = CubeGather(place, tokens_all, semaphores, every, EVEN)
    tokens_gather.step(0)
    load_own_cot = pltpu.make_async_copy(
        cotangent, cot_kept.at[place.own], semaphores.take(1).at[0]
    )
    load_own_cot.start()
    small_move = move(Spread(whole), small, small_all)
    small_move.start()
    states_move = move(Peers(by_part), states, states_all)
    states_move.start()
    columns_move = move(Spread(by_part), columns, columns_all)
    columns_move.start()
    gates_move = move(RowSpread(), gates, gates_all)
    gates_move.start()
    rows_move = move(RowSpread(), out_rows, rows_all)
    rows_move.start()
    tokens_gather.step(1)
    small_move.relay()
    tokens_gather.step(2)
    late = [
        move(Spread(by_columns), mlp_gate, gate_all),
        move(Spread(by_columns), mlp_up, up_all),
        move(RowSpread(), mlp_down, down_all),
    ]
    late_pump = Pump(late[:2], late[2:])
    late_pump.start(PACE[0])
    small_move.finish()
    for tap in range(5):
        aux[tap : tap + 1, :] = placed_sum(small_all, place, tap)
    decay_row = aux[4:5, :]
    aux[4:5, :] = jnp.maximum(-decay_row, 0.0) + jnp.log1p(jnp.exp(-jnp.abs(decay_row)))
    aux[5:6, :] = jax.nn.sigmoid(-decay_row)
    aux[6:8, :] = jnp.zeros((2, WIDTH), full_type)
    gains[0:1, :] = placed_gain(small_all, 5)
    gains[1:2, :] = placed_gain(small_all, 6)
    tokens_gather.finish()
    cot_gather = CubeGather(place, cot_kept, semaphores, every)
    load_own_cot.wait()

    @pl.loop(0, SPAN // 32)
    def _(step):
        rows = pl.ds(pl.multiple_of(step % 4 * 32, 32), 32)
        index = whole_block(place, step // 4) + (rows,)
        normed[index] = scaled_norm(tokens_all[index].astype(full_type), gains[0:1, :]).astype(
            low_type
        )

    keep_normed = local.start(normed, normed_kept)
    columns_move.relay()
    gates_move.relay()
    rows_move.relay()
    columns_move.finish()
    late_pump.start(PACE[1])

    @pl.loop(0, 4)
    def _(step):
        rows = pl.ds(pl.multiple_of(step * 256, 256), 256)
        pre[rows, :] = jnp.dot(
            normed[step // 2, step % 2].reshape(256, width),
            whole_matrix(columns_all),
            preferred_element_type=full_type,
        )

    late_pump.start(PACE[2])
    gates_move.finish()
    states_move.finish()
    taps = taps_of(aux)
    soft, slope = aux[4:5, :], aux[5:6, :]

    def gate_logits(low):
        both = jnp.dot(low, whole_matrix(gates_all), preferred_element_type=full_type)
        return (jax.nn.sigmoid(both[:, 0:WIDTH]), jax.nn.sigmoid(both[:, WIDTH:]))

    @pl.loop(0, PARTS)
    def _(row):
        rows = row_block(row)
        padded[0:8, :] = states_all[row]
        padded[8 : 8 + TOK, :] = pre[rows, 0:WIDTH]
        total = taps[0] * padded[8 : 8 + TOK, :]
        for tap in range(1, 4):
            total = total + taps[tap] * padded[8 - tap : 8 - tap + TOK, :]
        low = total.astype(low_type)
        conv[rows, :] = low
        recur, gate = gate_logits(low)
        log_decay = -8.0 * recur * soft
        scale = jnp.sqrt(-small_expm1(2.0 * log_decay))
        put(carries, rows, scale * gate * low.astype(full_type))
        put(decays, rows, jnp.exp(log_decay))

    def advance(time, carried):
        across = pl.ds(time, PARTS, stride=TOK)
        carried = [
            decays[piece, across, :] * before + carries[piece, across, :]
            for piece, before in enumerate(carried)
        ]
        for piece, now in enumerate(carried):
            hidden[piece, across, :] = now
        return carried

    late_pump.start(PACE[3])
    initial = states_all[:, 0, :]
    initial = [initial[:, piece * 128 : (piece + 1) * 128] for piece in range(WIDTH // 128)]
    lax.fori_loop(0, TOK, advance, initial, unroll=8)
    rows_move.finish()

    def project_out(part):
        @pl.loop(0, PARTS)
        def _(row):
            rows = pl.ds(pl.multiple_of(row * TOK + part * PART, PART), PART)
            gated, _ = gelu_parts(pre[rows, WIDTH:])
            low = (take(hidden, rows) * gated).astype(low_type)
            mixed[rows, :] = low
            blocks[whole_block(place, row) + (parts[part],)] = jnp.dot(
                low, whole_matrix(rows_all), preferred_element_type=full_type
            ).astype(low_type)

    def norm_two(part):
        @pl.loop(0, PART // 32)
        def _(step):
            rows = pl.ds(pl.multiple_of(part * PART + step * 32, 32), 32)
            total = after[rows, :] + tokens_all[place.own + (rows,)].astype(full_type)
            after[rows, :] = total
            two_all[place.own + (rows,)] = scaled_norm(total, gains[1:2, :]).astype(low_type)

    landings = (landing_one, landing_two, landing_three)

    def cube_sum(array, part):
        return CubeSum(place, array, landings, semaphores, part * PART, PART)

    mixer_sums = [cube_sum(blocks, part) for part in range(2)]
    two_gathers = [CubeGather(place, two_all, semaphores, rows) for rows in parts]
    for part in range(2):
        project_out(part)
        mixer_sums[part].start()
        late_pump.start(PACE[4 + part])
    cot_gather.step(0)
    for part in range(2):
        mixer_sums[part].step(0)
    cot_gather.step(1)
    for part in range(2):
        mixer_sums[part].step(1)
    for part in range(2):
        mixer_sums[part].step(2, after)
        norm_two(part)
        two_gathers[part].step(0)
    late_pump.start(20)
    cot_gather.step(2)
    for part in range(2):
        two_gathers[part].step(1)
    for part in range(2):
        two_gathers[part].step(2)
    cot_gather.finish()
    cot_all = cube_one
    load_cot = pltpu.make_async_copy(cot_kept, cot_all, semaphores.take(1).at[0])
    load_cot.start()
    for item in late:
        item.relay()
    for part in range(2):
        mixer_sums[part].finish()
    keep_normed.wait()
    load_cot.wait()
    for item in late:
        item.finish()

    out_blocks = cube_two

    def mlp(part, y):
        rows = parts[part]
        at = (y, slice(None), slice(None), rows)
        index = y * 2 + part
        normed_two = two_all[at].reshape(4 * PART, width)
        cot = cot_all[at].reshape(4 * PART, width)
        for piece in range(2):
            cut = pl.ds(piece * (hidden_units // 2), hidden_units // 2)
            gate_part, up_part = (
                jnp.dot(
                    normed_two,
                    array[:, :, :, :, cut].reshape(width, hidden_units // 2),
                    preferred_element_type=full_type,
                )
                for array in (gate_all, up_all)
            )
            gated, bend = gelu_parts(gate_part)
            matrix = down_all[piece].reshape(hidden_units // 2, width)
            grad_active = cols_product(cot, matrix)
            for array, values in (
                (active, gated * up_part),
                (grad_gate, grad_active * up_part * bend),
                (grad_up, grad_active * gated),
            ):
                array[index, :, :, cut] = values.astype(low_type).reshape(
                    4, PART, hidden_units // 2
                )
        low, to_gate, to_up = (whole_matrix(array.at[index]) for array in (active, grad_gate, grad_up))
        for piece in range(4):
            cut = pl.ds(piece * (width // 4), width // 4)
            matrix = down_all[:, :, :, cut].reshape(hidden_units, width // 4)
            out_blocks[at + (cut,)] = (
                jnp.dot(low, matrix, preferred_element_type=full_type)
                .astype(low_type)
                .reshape(2, 2, PART, width // 4)
            )
            back = cols_product(to_gate, whole_matrix(gate_all.at[piece])) + cols_product(
                to_up, whole_matrix(up_all.at[piece])
            )
            blocks[at + (cut,)] = back.astype(low_type).reshape(2, 2, PART, width // 4)

    def by_tokens(array, cut):
        return jnp.concatenate(
            [
                array[y, :, :, rows, cut].reshape(4 * PART, cut.size)
                for y in range(2)
                for rows in parts
            ],
            axis=0,
        )

    def grad_rows(terms, sums):
        @pl.loop(0, 8)
        def _(step):
            side = by_tokens(two_all, pl.ds(pl.multiple_of(step * 256, 256), 256))
            sums[step // 2, step % 2] = (
                rows_product(side, whole_matrix(terms))
                .astype(low_type)
                .reshape(4, 64, hidden_units)
            )

    def norm_two_back(part):
        @pl.loop(0, PART // 32)
        def _(step):
            rows = pl.ds(pl.multiple_of(part * PART + step * 32, 32), 32)
            back, by_gain = norm_back(after[rows, :], gains[1:2, :], grad[rows, :])
            total = cot_all[place.own + (rows,)].astype(full_type) + back
            grad[rows, :] = total
            cot_all[place.own + (rows,)] = total.astype(low_type)
            grad_gains[1:2, :] += jnp.sum(by_gain, axis=0, keepdims=True)

    mixed_all = cube_one
    two_sums = [cube_sum(blocks, part) for part in range(2)]
    mixed_gathers = [CubeGather(place, cube_one, semaphores, rows) for rows in parts]
    two_gathers[0].finish()

    @pl.loop(0, 2)
    def _(y):
        mlp(0, y)

    two_sums[0].start()
    two_gathers[1].finish()
    mlp(1, 0)
    two_sums[0].step(0)
    mlp(1, 1)
    two_sums[1].start()

    @pl.loop(0, 4)
    def _(step):
        cut = pl.ds(pl.multiple_of(step * 512, 512), 512)
        side = by_tokens(cot_all, cut)
        for piece in range(2):
            half = pl.ds(piece * (hidden_units // 2), hidden_units // 2)
            down_all[piece, :, :, cut] = (
                rows_product(active[:, :, :, half].reshape(SPAN, hidden_units // 2), side)
                .astype(low_type)
                .reshape(2, hidden_units // 4, 512)
            )

    def tell_sibling(number):
        pl.semaphore_signal(
            free.at[number], inc=1, device_id=place.sibling(), device_id_type=MESH
        )

    gate_swap = move(Swap(), gate_all, active)
    up_swap = move(Swap(), up_all, grad_gate)
    down_swap = move(Swap(), down_all, down_landing)
    gate_return = move(Owners(), gate_all, gate_back)
    up_return = move(Owners(), up_all, up_back)
    down_return = move(RowOwners(), down_all, down_back)
    returns = [gate_return, up_return, down_return]
    tell_sibling(0)
    down_swap.start()
    two_sums[0].step(1)
    two_sums[1].step(0)
    grad_rows(grad_gate, gate_all)
    tell_sibling(1)
    pl.semaphore_wait(free.at[0], 1)
    gate_swap.start()
    grad_gains[...] = jnp.zeros_like(grad_gains)
    two_sums[0].step(2, grad)
    norm_two_back(0)
    mixed_gathers[0].step(0)
    two_sums[1].step(1)
    down_swap.finish()
    add_swapped(down_all, down_landing, place.core)
    grad_rows(grad_up, up_all)
    pl.semaphore_wait(free.at[1], 1)
    up_swap.start()
    two_sums[1].step(2, grad)
    norm_two_back(1)
    mixed_gathers[1].step(0)
    gate_swap.finish()
    add_swapped(gate_all, active, place.core)
    mixed_gathers[0].step(1)
    mixed_gathers[1].step(1)
    up_swap.finish()
    add_swapped(up_all, grad_gate, place.core)
    tell_sibling(2)
    mixed_gathers[0].step(2)
    mixed_gathers[1].step(2)
    for item in returns:
        item.start()
    for part in range(2):
        two_sums[part].finish()
        mixed_gathers[part].finish()

    out_sum = CubeSum(
        place,
        out_blocks,
        (cube_three.at[0], cube_three.at[1, 0], cube_three.at[1, 1, 0]),
        semaphores,
        0,
        TOK,
    )
    out_sum.start()

    @pl.loop(0, PARTS)
    def _(row):
        rows = row_block(row)
        branch = cols_product(mixed_all[whole_block(place, row)], whole_matrix(rows_all))
        gated, bend = gelu_parts(pre[rows, WIDTH:])
        grad_pre[rows, WIDTH:] = (branch * take(hidden, rows) * bend).astype(low_type)
        put(carries, rows, branch * gated)

    @pl.loop(0, 4)
    def _(step):
        cut = pl.ds(pl.multiple_of(step * 512, 512), 512)
        rows_all[:, :, :, cut] = (
            rows_product(mixed[...], mixed_all[:, :, :, :, cut].reshape(SPAN, 512))
            .astype(low_type)
            .reshape(2, 2, LANES, 512)
        )

    pl.semaphore_wait(free.at[2], 1)
    rows_swap = move(Swap(), rows_all, down_landing.at[:, pl.ds(0, LANES)])
    rows_swap.start()
    normed_again = cube_one
    load_normed = pltpu.make_async_copy(normed_kept, normed_again, semaphores.take(1).at[0])
    load_normed.start()

    def advance_back(step, state):
        factors, carried = state
        across = pl.ds(TOK - 1 - step, PARTS, stride=TOK)
        carried = [
            carries[piece, across, :] + factors[piece] * before
            for piece, before in enumerate(carried)
        ]
        for piece, now in enumerate(carried):
            carries[piece, across, :] = now
        return ([decays[piece, across, :] for piece in range(WIDTH // 128)], carried)

    zeros = [jnp.zeros((PARTS, 128), full_type)] * (WIDTH // 128)
    lax.fori_loop(0, TOK, advance_back, (zeros, zeros), unroll=8)
    rows_swap.finish()
    add_swapped(rows_all, down_landing, place.core)
    rows_return = move(RowOwners(), rows_all, rows_back)
    rows_return.start()
    grad_aux[...] = jnp.zeros_like(grad_aux)
    grad_blocks[...] = jnp.zeros_like(grad_blocks)

    @pl.loop(0, PARTS)
    def _(row):
        rows = row_block(row)
        padded[0:8, :] = jnp.broadcast_to(states_all[row, 0:1, :], (8, WIDTH))
        padded[8 : 8 + TOK, :] = take(hidden, rows)
        low = conv[rows, :]
        recur, gate = gate_logits(low)
        log_decay = -8.0 * recur * soft
        decay = take(decays, rows)
        scale = jnp.sqrt(-small_expm1(2.0 * log_decay))
        conv_full = low.astype(full_type)
        carried = take(carries, rows)
        total = (
            carried * decay * padded[7 : 7 + TOK, :]
            - carried * gate * conv_full * (decay * decay) / scale
        )
        grad_aux[4:5, :] += jnp.sum(total * 8.0 * recur * slope, axis=0, keepdims=True)
        to_recur = (total * (-8.0 * soft) * recur * (1.0 - recur)).astype(low_type)
        to_input = (carried * scale * conv_full * gate * (1.0 - gate)).astype(low_type)
        both = jnp.concatenate([to_recur, to_input], axis=1)
        grad_blocks[...] += rows_product(low, both)
        back = carried * scale * gate + cols_product(both, whole_matrix(gates_all))
        first = decay[0:1, :] * carried[0:1, :]
        padded[0:8, :] = jnp.zeros((8, WIDTH), full_type)
        padded[8 : 8 + TOK, :] = back
        padded[8 + TOK :, :] = jnp.zeros((8, WIDTH), full_type)
        spread = taps[0] * padded[0 : 8 + TOK, :]
        for tap in range(1, 4):
            spread = spread + taps[tap] * padded[tap : tap + 8 + TOK, :]
        grad_pre[rows, 0:WIDTH] = spread[8:, :].astype(low_type)
        grad_states[row] = spread[0:8, :]
        grad_states[row, 0:1, :] = first
        padded[0:8, :] = states_all[row]
        padded[8 : 8 + TOK, :] = pre[rows, 0:WIDTH]
        for tap in range(4):
            grad_aux[tap : tap + 1, :] += jnp.sum(
                back * padded[8 - tap : 8 - tap + TOK, :], axis=0, keepdims=True
            )

    states_return = move(Peers(by_part), grad_states, states_back)
    states_return.start()
    blocks_low[...] = grad_blocks[...].astype(low_type).reshape(2, 2, LANES, 2 * WIDTH)
    out_sum.step(0)

    one_sums = [cube_sum(blocks, part) for part in range(2)]
    for part in range(2):

        @pl.loop(0, PARTS)
        def _(row):
            terms = grad_pre[pl.ds(pl.multiple_of(row * TOK + part * PART, PART), PART), :]
            for piece in range(COLUMNS):
                cut = pl.ds(piece * (width // 4), width // 4)
                blocks[whole_block(place, row) + (parts[part], cut)] = cols_product(
                    terms, whole_matrix(columns_all.at[piece])
                ).astype(low_type)

        one_sums[part].start()

    out_sum.step(1)
    one_sums[0].step(0)
    one_sums[1].step(0)
    out_sum.step(2, summed)

    @pl.loop(0, TOK // 32)
    def _(step):
        rows = pl.ds(pl.multiple_of(step * 32, 32), 32)
        cube_three[1, 1, 1, rows, :] = (after[rows, :] + summed[rows, :]).astype(low_type)

    local.start(cube_three.at[1, 1, 1], output)
    load_normed.wait()

    @pl.loop(0, 8)
    def _(step):
        cut = pl.ds(pl.multiple_of(step * 256, 256), 256)
        columns_all[step // 2, step % 2] = (
            rows_product(normed_again[:, :, :, :, cut].reshape(SPAN, 256), grad_pre[...])
            .astype(low_type)
            .reshape(4, 64, 2 * WIDTH)
        )

    mixer_swaps = [
        move(Swap(), columns_all, active),
        move(Swap(), blocks_low, blocks_landing),
    ]
    for item in mixer_swaps:
        item.start()
    one_sums[0].step(1)
    one_sums[1].step(1)
    mixer_swaps[0].finish()
    add_swapped(columns_all, active, place.core)
    columns_return = move(Owners(), columns_all, columns_back)
    columns_return.start()
    mixer_swaps[1].finish()
    add_swapped(blocks_low, blocks_landing, place.core)
    blocks_return = move(RowOwners(), blocks_low, blocks_back)
    blocks_return.start()
    one_sums[0].step(2, summed)
    one_sums[1].step(2, summed)
    load_tokens = pltpu.make_async_copy(
        tokens, cube_three.at[1, 0, 0], semaphores.take(1).at[0]
    )
    out_sum.finish()
    load_tokens.start()
    load_tokens.wait()

    @pl.loop(0, TOK // 32)
    def _(step):
        rows = pl.ds(pl.multiple_of(step * 32, 32), 32)
        values = cube_three[1, 0, 0, rows, :].astype(full_type)
        back, by_gain = norm_back(values, gains[0:1, :], summed[rows, :])
        cube_three[1, 0, 1, rows, :] = (grad[rows, :] + back).astype(low_type)
        grad_gains[0:1, :] += jnp.sum(by_gain, axis=0, keepdims=True)

    local.start(cube_three.at[1, 0, 1], grad_tokens)
    small_terms[...] = jnp.zeros_like(small_terms)
    for column, core, z in itertools.product(range(COLUMNS), range(2), range(4)):
        tile = (column * 8 + core * 4 + z) // 2
        small_terms[column, core, z, 0:2, 0:128] = grad_gains[:, tile * 128 : (tile + 1) * 128]
    for z in range(4):
        small_terms[place.part // 2, place.part % 2, z, 2:7, :] = grad_aux[0:5, :]
    small_swap = move(Swap(), small_terms, small_landing)
    small_swap.start()
    small_swap.finish()
    add_swapped(small_terms, small_landing, place.core)
    small_return = move(Owners(), small_terms, small_back)
    small_return.start()
    for part in range(2):
        one_sums[part].finish()
    for item in [states_return, small_return, columns_return, rows_return, blocks_return] + returns:
        item.finish()
    for copy in local.copies[1:]:
        copy.wait()


def block_call(arrays, rows, width, units):
    hbm = pl.BlockSpec(memory_space=pl.ANY)
    lanes = (WIDTH // 128, SPAN, 128)
    cube = (2, 2, 2, TOK, width)
    spread = (COLUMNS, 2, 4, rows)
    hidden_units = 4 * units
    outputs = [
        ((TOK, width), low_type),
        ((TOK, width), low_type),
        ((PARTS, 8, WIDTH), full_type),
        ((2, PARTS, 8, WIDTH), full_type),
        ((2, PARTS, rows, 2 * WIDTH), low_type),
        ((2, rows, PARTS * hidden_units), low_type),
        ((2, rows, PARTS * hidden_units), low_type),
        ((2, LANES, 2 * WIDTH), low_type),
        ((2, LANES, width), low_type),
        ((2, units, width), low_type),
        (cube, low_type),
        (cube, low_type),
    ]
    scratch = [
        (cube, low_type),
        (cube, low_type),
        (cube, low_type),
        (cube, low_type),
        ((2, 2, TOK, width), low_type),
        ((2, TOK, width), low_type),
        ((TOK, width), low_type),
        ((COLUMNS, 2, 4, 16, WIDTH), low_type),
        ((PARTS, 8, WIDTH), full_type),
        (spread + (2 * WIDTH,), low_type),
        ((2, 2, LANES, 2 * WIDTH), low_type),
        ((2, 2, LANES, width), low_type),
        (spread + (hidden_units,), low_type),
        (spread + (hidden_units,), low_type),
        ((2, 2, units, width), low_type),
        ((SPAN, 2 * WIDTH), full_type),
        ((SPAN, WIDTH), low_type),
        (lanes, full_type),
        ((SPAN, WIDTH), low_type),
        (lanes, full_type),
        (lanes, full_type),
        ((TOK + 16, WIDTH), full_type),
        ((TOK, width), full_type),
        ((TOK, width), full_type),
        ((TOK, width), full_type),
        ((8, WIDTH), full_type),
        ((2, width), full_type),
        ((2, width), full_type),
        ((8, WIDTH), full_type),
        ((4, 4, 64, hidden_units), low_type),
        ((4, 4, 64, hidden_units), low_type),
        ((4, 4, 64, hidden_units), low_type),
        ((2, units, width), low_type),
        ((SPAN, 2 * WIDTH), low_type),
        ((WIDTH, 2 * WIDTH), full_type),
        ((2, 2, LANES, 2 * WIDTH), low_type),
        ((2, LANES, 2 * WIDTH), low_type),
        ((PARTS, 8, WIDTH), full_type),
        ((COLUMNS, 2, 4, 8, WIDTH), full_type),
        ((COLUMNS, 4, 8, WIDTH), full_type),
    ]
    return pl.pallas_call(
        block_kernel,
        out_shape=[jax.ShapeDtypeStruct(shape, kind) for shape, kind in outputs],
        in_specs=[hbm] * len(arrays),
        out_specs=[hbm] * len(outputs),
        scratch_shapes=[pltpu.VMEM(shape, kind) for shape, kind in scratch]
        + [pltpu.SemaphoreType.DMA((480,)), pltpu.SemaphoreType.REGULAR((3,))],
        compiler_params=pltpu.CompilerParams(
            collective_id=0, has_side_effects=True, vmem_limit_bytes=VMEM_BYTES
        ),
        name="hawk_block",
    )(*arrays)


def spread_lanes(values):
    gap = jnp.zeros((values.shape[0], LANES - CHUNK), values.dtype)
    pieces = []
    for start in range(0, values.shape[1], CHUNK):
        pieces += [values[:, start : start + CHUNK], gap]
    return jnp.concatenate(pieces, axis=1)


def joined_lanes(values):
    return [values[:, start : start + CHUNK] for start in range(0, values.shape[1], LANES)]


def prepare_kernel(
    fresh,
    gain_mixer,
    gain_mlp,
    conv_kernel,
    decay_param,
    proj_input,
    proj_gate,
    gate_recur,
    gate_input,
    proj_output,
    conv_state,
    recur_state,
    small,
    states,
    columns,
    gates,
    out_rows,
):
    z = lax.axis_index("narrow")
    keep = (1 - fresh[0]).astype(full_type)
    for kind, proj in enumerate((proj_input, proj_gate)):
        for part in range(PARTS):
            piece = proj[:, part * 4 * CHUNK : (part + 1) * 4 * CHUNK].astype(full_type)
            columns[part, :, kind * WIDTH : (kind + 1) * WIDTH] = spread_lanes(piece).astype(
                low_type
            )
    pair = 2 * LANES
    gates[CHUNK:, :] = jnp.zeros((LANES - CHUNK, 2 * WIDTH), low_type)
    for kind, gate in enumerate((gate_recur, gate_input)):
        values = spread_lanes(gate[...].astype(full_type))
        for block in range(2):
            start = kind * WIDTH + block * pair
            gates[0:CHUNK, start : start + pair] = jnp.where(
                z // 2 == block, values, jnp.zeros_like(values)
            ).astype(low_type)
    out_rows[0:CHUNK, :] = proj_output[...]
    out_rows[CHUNK:, :] = jnp.zeros((LANES - CHUNK, out_rows.shape[1]), low_type)
    taps = jnp.concatenate([conv_kernel[...], decay_param[...]], axis=0).astype(full_type)
    taps = spread_lanes(taps)
    taps = jnp.concatenate(
        [jnp.where(z == place, taps, jnp.zeros_like(taps)) for place in range(4)], axis=1
    )
    gains = jnp.concatenate([gain_mixer[...], gain_mlp[...]], axis=0).astype(full_type)
    gains = [jnp.where(z % 2 == odd, gains, jnp.zeros_like(gains)) for odd in range(2)]
    gains = jnp.concatenate(gains + [jnp.zeros((2, WIDTH - 128), full_type)], axis=1)
    rest = jnp.zeros((9, WIDTH), full_type)
    small[...] = jnp.concatenate([taps, gains, rest], axis=0).astype(low_type)
    states[...] = jnp.zeros_like(states)
    for part in range(PARTS):
        cut = slice(part * 4 * CHUNK, (part + 1) * 4 * CHUNK)
        states[part, 0:1, :] = spread_lanes(recur_state[:, cut]) * keep
        states[part, 5:8, :] = spread_lanes(conv_state[0, :, cut]) * keep


def finish_kernel(
    fresh,
    output,
    grad_tokens,
    states_back,
    small_back,
    columns_back,
    gate_back,
    up_back,
    blocks_back,
    rows_back,
    down_back,
    output_out,
    tokens_out,
    conv_out,
    recur_out,
    gain_one_out,
    input_out,
    gate_out,
    taps_out,
    decay_out,
    gate_recur_out,
    gate_input_out,
    rows_out,
    gain_two_out,
    mlp_gate_out,
    mlp_up_out,
    down_out,
):
    z = lax.axis_index("narrow")
    keep = (1 - fresh[0]).astype(full_type)
    output_out[0] = output[...]
    tokens_out[0] = grad_tokens[...]
    states = jnp.concatenate(
        [piece for part in range(PARTS) for piece in joined_lanes(states_back[part])], axis=1
    )
    recur_out[...] = states[0:1, :] * keep
    conv_out[0] = states[5:8, :] * keep

    def both(array, *index):
        return array[(0,) + index].astype(full_type) + array[(1,) + index].astype(full_type)

    for kind, target in enumerate((input_out, gate_out)):
        pieces = []
        for part in range(PARTS):
            cut = slice(kind * WIDTH, (kind + 1) * WIDTH)
            pieces += joined_lanes(both(columns_back, part, slice(None), cut))
        target[...] = jnp.concatenate(pieces, axis=1)
    pair = 2 * LANES
    for kind, target in enumerate((gate_recur_out, gate_input_out)):
        start = kind * WIDTH
        first = both(blocks_back, slice(0, CHUNK), slice(start, start + pair))
        second = both(blocks_back, slice(0, CHUNK), slice(start + pair, start + 2 * pair))
        target[...] = jnp.concatenate(joined_lanes(jnp.where(z < 2, first, second)), axis=1)
    total = jnp.zeros((8, WIDTH), full_type)
    for half, part in itertools.product(range(2), range(PARTS)):
        total = total + small_back[half, part]
    rows = gain_one_out.shape[1]
    gains = jnp.where(z % 2 == 0, total[0:2, 0:rows], total[0:2, rows : 2 * rows])
    gain_one_out[...] = gains[0:1, :]
    gain_two_out[...] = gains[1:2, :]
    taps = total[2:7, 0:CHUNK]
    for place in range(1, 4):
        taps = jnp.where(z == place, total[2:7, place * LANES : place * LANES + CHUNK], taps)
    taps_out[...] = taps[0:4, :]
    decay_out[...] = taps[4:5, :]
    rows_out[...] = both(rows_back, slice(0, CHUNK))
    for source, target in ((gate_back, mlp_gate_out), (up_back, mlp_up_out), (down_back, down_out)):

        @pl.loop(0, target.shape[0] // 8)
        def _(step):
            part = pl.ds(pl.multiple_of(step * 8, 8), 8)
            target[part, :] = both(source, part)


def plain_call(kernel, name, flags, arrays, outputs):
    vmem = pl.BlockSpec(memory_space=pltpu.VMEM)
    return pl.pallas_call(
        kernel,
        out_shape=[jax.ShapeDtypeStruct(shape, kind) for shape, kind in outputs],
        in_specs=[pl.BlockSpec(memory_space=pltpu.SMEM)] + [vmem] * len(arrays),
        out_specs=[vmem] * len(outputs),
        compiler_params=pltpu.CompilerParams(vmem_limit_bytes=VMEM_BYTES),
        name=name,
    )(flags, *arrays)


def halves(
    tokens,
    conv_state,
    recur_state,
    fresh_rows,
    gain_mixer,
    proj_input,
    proj_gate,
    conv_kernel,
    decay_param,
    gate_recur,
    gate_input,
    proj_output,
    gain_mlp,
    mlp_gate,
    mlp_up,
    mlp_down,
    cotangent,
):
    width = tokens.shape[2]
    rows = width // 32
    units = mlp_down.shape[0]
    small, states, columns, gates, out_rows = plain_call(
        prepare_kernel,
        "prepare",
        fresh_rows,
        (
            gain_mixer[None],
            gain_mlp[None],
            conv_kernel,
            decay_param[None],
            proj_input,
            proj_gate,
            gate_recur,
            gate_input,
            proj_output,
            conv_state,
            recur_state,
        ),
        [
            ((16, WIDTH), low_type),
            ((PARTS, 8, WIDTH), full_type),
            ((PARTS, rows, 2 * WIDTH), low_type),
            ((LANES, 2 * WIDTH), low_type),
            ((LANES, width), low_type),
        ],
    )
    results = block_call(
        (
            tokens[0],
            small,
            states,
            columns,
            gates,
            out_rows,
            mlp_gate,
            mlp_up,
            mlp_down,
            cotangent[0],
        ),
        rows,
        width,
        units,
    )
    results = plain_call(
        finish_kernel,
        "finish",
        fresh_rows,
        results[:10],
        [
            (tokens.shape, low_type),
            (tokens.shape, low_type),
            (conv_state.shape, full_type),
            (recur_state.shape, full_type),
            ((1, rows), full_type),
            (proj_input.shape, full_type),
            (proj_gate.shape, full_type),
            (conv_kernel.shape, full_type),
            ((1, CHUNK), full_type),
            (gate_recur.shape, full_type),
            (gate_input.shape, full_type),
            (proj_output.shape, full_type),
            ((1, rows), full_type),
            (mlp_gate.shape, full_type),
            (mlp_up.shape, full_type),
            (mlp_down.shape, full_type),
        ],
    )
    return tuple(
        result[0] if place in (4, 8, 12) else result for place, result in enumerate(results)
    )


def solution(mesh):
    sizes = (mesh.shape["wide"], mesh.shape["narrow"])
    return jax.shard_map(
        halves if sizes == (2 * COLUMNS, 2 * LOWS) else shards,
        mesh=mesh,
        in_specs=(
            P(("wide", "narrow"), None, None),
            P(("wide", "narrow"), None, None),
            P(("wide", "narrow"), None),
            P(("wide", "narrow")),
            P(("wide", "narrow")),
            P(("wide", "narrow"), None),
            P(("wide", "narrow"), None),
            P(None, ("wide", "narrow")),
            P(("wide", "narrow")),
            P(("wide", "narrow"), None),
            P(("wide", "narrow"), None),
            P(("wide", "narrow"), None),
            P(("wide", "narrow")),
            P(("wide", "narrow"), None),
            P(("wide", "narrow"), None),
            P(("wide", "narrow"), None),
            P(("wide", "narrow"), None, None),
        ),
        out_specs=(
            P(("wide", "narrow"), None, None),
            P(("wide", "narrow"), None, None),
            P(("wide", "narrow"), None, None),
            P(("wide", "narrow"), None),
            P(("wide", "narrow")),
            P(("wide", "narrow"), None),
            P(("wide", "narrow"), None),
            P(None, ("wide", "narrow")),
            P(("wide", "narrow")),
            P(("wide", "narrow"), None),
            P(("wide", "narrow"), None),
            P(("wide", "narrow"), None),
            P(("wide", "narrow")),
            P(("wide", "narrow"), None),
            P(("wide", "narrow"), None),
            P(("wide", "narrow"), None),
        ),
        check_vma=False,
    )
```

```python
import functools
import itertools
from functools import reduce

import jax
import jax.numpy as jnp
from jax import lax
from jax.experimental import pallas as pl
from jax.experimental.pallas import tpu as pltpu
from jax.sharding import PartitionSpec as P

BLOCKS = 16
BLK = 176
SCAN_BLOCK = 16


epsilon = 1e-06
contract_rows = (((0,), (0,)), ((), ()))
contract_cols = (((1,), (1,)), ((), ()))


def plain_product(left_side, right_side):
    return jnp.dot(left_side, right_side, preferred_element_type=jnp.float32)


def rows_product(left_side, right_side):
    return lax.dot_general(left_side, right_side, contract_rows, preferred_element_type=jnp.float32)


def cols_product(left_side, right_side):
    return lax.dot_general(left_side, right_side, contract_cols, preferred_element_type=jnp.float32)


def norm_scale(values, gain_vec):
    return (
        values * lax.rsqrt(jnp.mean(values * values, axis=-1, keepdims=True) + epsilon) * gain_vec
    )


def conv_apply(values, history, kernel):
    joined = jnp.concatenate([history, values], axis=0)
    length = values.shape[0]
    kernel_taps = kernel.shape[0]
    result = jnp.zeros_like(values)
    for offset in range(kernel_taps):
        first_row = kernel_taps - 1 - offset
        result = result + kernel[offset] * joined[first_row : first_row + length]
    return result


def block_mix(values, matrix):
    length = values.shape[0]
    mixed_out = jnp.einsum(
        "tki,kij->tkj",
        values.reshape(length, BLOCKS, BLK),
        matrix.reshape(BLOCKS, BLK, BLK),
        preferred_element_type=jnp.float32,
    )
    return mixed_out.reshape(length, BLOCKS * BLK)


def block_back(grad_logits, matrix):
    length = grad_logits.shape[0]
    spread_back = jnp.einsum(
        "tkj,kij->tki",
        grad_logits.reshape(length, BLOCKS, BLK),
        matrix.reshape(BLOCKS, BLK, BLK),
        preferred_element_type=jnp.float32,
    )
    return spread_back.reshape(length, BLOCKS * BLK)


def block_grad(values, grad_logits):
    length = values.shape[0]
    summed = jnp.einsum(
        "tki,tkj->kij",
        values.reshape(length, BLOCKS, BLK),
        grad_logits.reshape(length, BLOCKS, BLK),
        preferred_element_type=jnp.float32,
    )
    return summed.reshape(BLOCKS * BLK, BLK)


def gate_apply(recur_logits, input_logits, conv_float, decay_float):
    log_decay = -8.0 * jax.nn.sigmoid(recur_logits) * jax.nn.softplus(-decay_float)
    scan_in = jnp.sqrt(-jnp.expm1(2.0 * log_decay)) * jax.nn.sigmoid(input_logits) * conv_float
    return (log_decay, scan_in)


def branch_apply(hidden, gate_logits):
    return hidden * jax.nn.gelu(gate_logits)


def mlp_apply(gate_part, up_part):
    return jax.nn.gelu(gate_part) * up_part


def block_scan(log_decay, scan_in, initial):
    length, channels = scan_in.shape
    block_count = length // SCAN_BLOCK
    positions = jnp.arange(SCAN_BLOCK)
    causal = (positions[:, None] >= positions[None, :])[:, :, None]

    def advance(carried, pieces):
        decay_piece, input_piece = pieces
        cumulative = jnp.cumsum(decay_piece, axis=0)
        spread = jnp.where(causal, cumulative[:, None, :] - cumulative[None, :, :], 0.0)
        factors = jnp.where(causal, jnp.exp(spread), 0.0)
        states = jnp.sum(factors * input_piece[None, :, :], axis=1) + jnp.exp(cumulative) * carried
        return (states[-1], states)

    last_state, states = lax.scan(
        advance,
        initial,
        (
            log_decay.reshape(block_count, SCAN_BLOCK, channels),
            scan_in.reshape(block_count, SCAN_BLOCK, channels),
        ),
    )
    return states.reshape(length, channels)


def scan_back(log_decay, hidden, initial, grad_hidden):
    following = jnp.concatenate([log_decay[1:], jnp.zeros_like(log_decay[:1])], axis=0)
    carried = block_scan(following[::-1], grad_hidden[::-1], jnp.zeros_like(initial))[::-1]
    previous = jnp.concatenate([initial[None], hidden[:-1]], axis=0)
    grad_log_decay = carried * jnp.exp(log_decay) * previous
    grad_initial = jnp.exp(log_decay[0]) * carried[0]
    return (grad_log_decay, carried, grad_initial)


def mixer_forward(tokens_row, history, initial, keep_row, mixer):
    (
        gain_vec,
        proj_input,
        proj_gate,
        conv_kernel,
        decay_param,
        gate_recur,
        gate_input,
        proj_output,
    ) = mixer
    values = tokens_row.astype(jnp.float32)
    normed_one = norm_scale(values, gain_vec.astype(jnp.float32)).astype(jnp.bfloat16)
    branch_in = plain_product(normed_one, proj_input)
    gate_logits = plain_product(normed_one, proj_gate)
    history_kept = history * keep_row
    kernel_float = conv_kernel.astype(jnp.float32)
    conv_out = conv_apply(branch_in, history_kept, kernel_float).astype(jnp.bfloat16)
    recur_logits = block_mix(conv_out, gate_recur)
    input_logits = block_mix(conv_out, gate_input)
    decay_float = decay_param.astype(jnp.float32)
    conv_float = conv_out.astype(jnp.float32)
    log_decay, scan_in = gate_apply(recur_logits, input_logits, conv_float, decay_float)
    initial_kept = initial * keep_row
    hidden = block_scan(log_decay, scan_in, initial_kept)
    mixed_out = branch_apply(hidden, gate_logits).astype(jnp.bfloat16)
    after_mixer = values + plain_product(mixed_out, proj_output)
    kept = (
        values,
        normed_one,
        branch_in,
        gate_logits,
        history_kept,
        kernel_float,
        conv_out,
        conv_float,
        recur_logits,
        input_logits,
        decay_float,
        log_decay,
        initial_kept,
        hidden,
        mixed_out,
    )
    return (after_mixer, kept)


def mlp_forward(after_mixer, mlp):
    gain_vec, mlp_gate, mlp_up, mlp_down = mlp
    normed_two = norm_scale(after_mixer, gain_vec.astype(jnp.float32)).astype(jnp.bfloat16)
    gate_part = plain_product(normed_two, mlp_gate)
    up_part = plain_product(normed_two, mlp_up)
    activated = mlp_apply(gate_part, up_part).astype(jnp.bfloat16)
    result = after_mixer + plain_product(activated, mlp_down)
    return (result, (after_mixer, normed_two, gate_part, up_part, activated))


def mlp_backward(grad_result, mlp, kept):
    gain_vec, mlp_gate, mlp_up, mlp_down = mlp
    after_mixer, normed_two, gate_part, up_part, activated = kept
    grad_activated = cols_product(grad_result, mlp_down)
    grad_down = rows_product(activated, grad_result)
    unused, mlp_pull = jax.vjp(mlp_apply, gate_part, up_part)
    grad_gate_part, grad_up_part = mlp_pull(grad_activated)
    grad_gate_part = grad_gate_part.astype(jnp.bfloat16)
    grad_up_part = grad_up_part.astype(jnp.bfloat16)
    grad_normed = cols_product(grad_gate_part, mlp_gate) + cols_product(grad_up_part, mlp_up)
    grad_mlp_gate = rows_product(normed_two, grad_gate_part)
    grad_mlp_up = rows_product(normed_two, grad_up_part)
    unused, norm_pull = jax.vjp(norm_scale, after_mixer, gain_vec.astype(jnp.float32))
    grad_values, grad_gain = norm_pull(grad_normed)
    grad_after = grad_result.astype(jnp.float32) + grad_values
    return (grad_after, (grad_gain, grad_mlp_gate, grad_mlp_up, grad_down))


def mixer_backward(grad_after, mixer, kept, keep_row):
    (
        gain_vec,
        proj_input,
        proj_gate,
        conv_kernel,
        decay_param,
        gate_recur,
        gate_input,
        proj_output,
    ) = mixer
    (
        values,
        normed_one,
        branch_in,
        gate_logits,
        history_kept,
        kernel_float,
        conv_out,
        conv_float,
        recur_logits,
        input_logits,
        decay_float,
        log_decay,
        initial_kept,
        hidden,
        mixed_out,
    ) = kept
    grad_mixed = grad_after.astype(jnp.bfloat16)
    grad_proj_output = rows_product(mixed_out, grad_mixed)
    grad_branch = cols_product(grad_mixed, proj_output)
    unused, branch_pull = jax.vjp(branch_apply, hidden, gate_logits)
    grad_hidden, grad_gate_logits = branch_pull(grad_branch)
    grad_gate_logits = grad_gate_logits.astype(jnp.bfloat16)
    grad_log_decay, grad_scan_in, grad_initial = scan_back(
        log_decay, hidden, initial_kept, grad_hidden
    )
    unused, gate_pull = jax.vjp(gate_apply, recur_logits, input_logits, conv_float, decay_float)
    grad_recur_logits, grad_input_logits, grad_conv, grad_decay = gate_pull(
        (grad_log_decay, grad_scan_in)
    )
    grad_recur_logits = grad_recur_logits.astype(jnp.bfloat16)
    grad_input_logits = grad_input_logits.astype(jnp.bfloat16)
    grad_gate_recur = block_grad(conv_out, grad_recur_logits)
    grad_gate_input = block_grad(conv_out, grad_input_logits)
    grad_conv = (
        grad_conv
        + block_back(grad_recur_logits, gate_recur)
        + block_back(grad_input_logits, gate_input)
    )
    unused, conv_pull = jax.vjp(conv_apply, branch_in, history_kept, kernel_float)
    grad_branch_in, grad_history, grad_kernel = conv_pull(grad_conv)
    grad_branch_low = grad_branch_in.astype(jnp.bfloat16)
    grad_proj_input = rows_product(normed_one, grad_branch_low)
    grad_proj_gate = rows_product(normed_one, grad_gate_logits)
    grad_normed = cols_product(grad_branch_low, proj_input) + cols_product(
        grad_gate_logits, proj_gate
    )
    unused, norm_pull = jax.vjp(norm_scale, values, gain_vec.astype(jnp.float32))
    grad_values, grad_gain = norm_pull(grad_normed)
    grad_tokens = (grad_after + grad_values).astype(jnp.bfloat16)
    weight_terms = (
        grad_gain,
        grad_proj_input,
        grad_proj_gate,
        grad_kernel,
        grad_decay,
        grad_gate_recur,
        grad_gate_input,
        grad_proj_output,
    )
    return (grad_tokens, grad_history * keep_row, grad_initial * keep_row, weight_terms)


def add_terms(first_terms, second_terms):
    return tuple(
        (left_side + right_side for left_side, right_side in zip(first_terms, second_terms))
    )


def shards(
    tokens,
    conv_state,
    recur_state,
    fresh_rows,
    gain_mixer,
    proj_input,
    proj_gate,
    conv_kernel,
    decay_param,
    gate_recur,
    gate_input,
    proj_output,
    gain_mlp,
    mlp_gate,
    mlp_up,
    mlp_down,
    cotangent,
):
    mixer_full = (
        lax.all_gather(gain_mixer, ("wide", "narrow"), axis=0, tiled=True),
        lax.all_gather(proj_input, ("wide", "narrow"), axis=0, tiled=True),
        lax.all_gather(proj_gate, ("wide", "narrow"), axis=0, tiled=True),
        lax.all_gather(conv_kernel, ("wide", "narrow"), axis=1, tiled=True),
        lax.all_gather(decay_param, ("wide", "narrow"), axis=0, tiled=True),
        lax.all_gather(gate_recur, ("wide", "narrow"), axis=0, tiled=True),
        lax.all_gather(gate_input, ("wide", "narrow"), axis=0, tiled=True),
        lax.all_gather(proj_output, ("wide", "narrow"), axis=0, tiled=True),
    )
    mlp_full = (
        lax.all_gather(gain_mlp, ("wide", "narrow"), axis=0, tiled=True),
        lax.all_gather(mlp_gate, ("wide", "narrow"), axis=0, tiled=True),
        lax.all_gather(mlp_up, ("wide", "narrow"), axis=0, tiled=True),
        lax.all_gather(mlp_down, ("wide", "narrow"), axis=0, tiled=True),
    )
    keep_rows = (1 - fresh_rows).astype(jnp.float32)
    stored = []
    row_index = 0
    after_mixer, mixer_kept = mixer_forward(
        tokens[row_index],
        conv_state[row_index],
        recur_state[row_index],
        keep_rows[row_index],
        mixer_full,
    )
    result, mlp_kept = mlp_forward(after_mixer, mlp_full)
    outputs = [result.astype(jnp.bfloat16)]
    stored.append((mixer_kept, mlp_kept))
    mixer_back = (
        lax.all_gather(gain_mixer, ("wide", "narrow"), axis=0, tiled=True),
        lax.all_gather(proj_input, ("wide", "narrow"), axis=0, tiled=True),
        lax.all_gather(proj_gate, ("wide", "narrow"), axis=0, tiled=True),
        lax.all_gather(conv_kernel, ("wide", "narrow"), axis=1, tiled=True),
        lax.all_gather(decay_param, ("wide", "narrow"), axis=0, tiled=True),
        lax.all_gather(gate_recur, ("wide", "narrow"), axis=0, tiled=True),
        lax.all_gather(gate_input, ("wide", "narrow"), axis=0, tiled=True),
        lax.all_gather(proj_output, ("wide", "narrow"), axis=0, tiled=True),
    )
    mlp_back = (
        lax.all_gather(gain_mlp, ("wide", "narrow"), axis=0, tiled=True),
        lax.all_gather(mlp_gate, ("wide", "narrow"), axis=0, tiled=True),
        lax.all_gather(mlp_up, ("wide", "narrow"), axis=0, tiled=True),
        lax.all_gather(mlp_down, ("wide", "narrow"), axis=0, tiled=True),
    )
    stored = []
    row_index = 0
    after_mixer, mixer_kept = mixer_forward(
        tokens[row_index],
        conv_state[row_index],
        recur_state[row_index],
        keep_rows[row_index],
        mixer_back,
    )
    unused, mlp_kept = mlp_forward(after_mixer, mlp_back)
    stored.append((mixer_kept, mlp_kept))
    row_index = 0
    grad_after, row_terms = mlp_backward(cotangent[row_index], mlp_back, stored[row_index][1])
    after_grads = [grad_after]
    mlp_terms = [row_terms]
    mlp_total = reduce(add_terms, mlp_terms)
    mlp_sums = (
        lax.psum_scatter(mlp_total[0], ("wide", "narrow"), scatter_dimension=0, tiled=True),
        lax.psum_scatter(mlp_total[1], ("wide", "narrow"), scatter_dimension=0, tiled=True),
        lax.psum_scatter(mlp_total[2], ("wide", "narrow"), scatter_dimension=0, tiled=True),
        lax.psum_scatter(mlp_total[3], ("wide", "narrow"), scatter_dimension=0, tiled=True),
    )
    row_index = 0
    grad_tokens, grad_history, grad_initial, row_terms = mixer_backward(
        after_grads[row_index], mixer_back, stored[row_index][0], keep_rows[row_index]
    )
    token_grads = [grad_tokens]
    history_grads = [grad_history]
    initial_grads = [grad_initial]
    mixer_terms = [row_terms]
    mixer_total = reduce(add_terms, mixer_terms)
    mixer_sums = (
        lax.psum_scatter(mixer_total[0], ("wide", "narrow"), scatter_dimension=0, tiled=True),
        lax.psum_scatter(mixer_total[1], ("wide", "narrow"), scatter_dimension=0, tiled=True),
        lax.psum_scatter(mixer_total[2], ("wide", "narrow"), scatter_dimension=0, tiled=True),
        lax.psum_scatter(mixer_total[3], ("wide", "narrow"), scatter_dimension=1, tiled=True),
        lax.psum_scatter(mixer_total[4], ("wide", "narrow"), scatter_dimension=0, tiled=True),
        lax.psum_scatter(mixer_total[5], ("wide", "narrow"), scatter_dimension=0, tiled=True),
        lax.psum_scatter(mixer_total[6], ("wide", "narrow"), scatter_dimension=0, tiled=True),
        lax.psum_scatter(mixer_total[7], ("wide", "narrow"), scatter_dimension=0, tiled=True),
    )
    return (
        jnp.stack(outputs),
        jnp.stack(token_grads),
        jnp.stack(history_grads),
        jnp.stack(initial_grads),
        mixer_sums[0],
        mixer_sums[1],
        mixer_sums[2],
        mixer_sums[3],
        mixer_sums[4],
        mixer_sums[5],
        mixer_sums[6],
        mixer_sums[7],
        mlp_sums[0],
        mlp_sums[1],
        mlp_sums[2],
        mlp_sums[3],
    )


COLUMNS = 4
LOWS = 2
PARTS = COLUMNS * LOWS
TOK = 128
CHUNK = 88
LANES = 96
WIDTH = 4 * LANES
SPAN = PARTS * TOK
MESH = pl.DeviceIdType.MESH
VMEM_BYTES = 63 * 1024 * 1024 + 896 * 1024
low_type = jnp.bfloat16
full_type = jnp.float32


class Place:
    def __init__(self):
        wide = lax.axis_index("wide")
        self.z = lax.axis_index("narrow")
        self.column, self.core = wide // 2, wide % 2
        self.half, self.low = self.z // 2, self.z % 2
        self.part = self.column * 2 + self.low
        self.index = wide * 4 + self.z
        self.own = (self.column // 2, self.column % 2, self.low)

    def shifted(self, by_y, by_x, by_low, by_half):
        column = (self.column // 2 + by_y) % 2 * 2 + (self.column % 2 + by_x) % 2
        low, half = (self.low + by_low) % 2, (self.half + by_half) % 2
        return (column, low, half)

    def neighbour(self, axis):
        y, x, low = (1 - at if axis == here else at for here, at in enumerate(self.own))
        return (y * 4 + x * 2 + self.core, self.half * 2 + low)

    def cube(self, fixed, other=None):
        return tuple(
            1 - at if axis == other else at if axis in fixed else slice(None)
            for axis, at in enumerate(self.own)
        )

    def sibling(self):
        return (self.column * 2 + 1 - self.core, self.z)


def greet_all(place):
    barrier = pltpu.get_barrier_semaphore()

    @pl.loop(1, 32)
    def _(step):
        other = (place.index + step) % 32
        pl.semaphore_signal(
            barrier, inc=1, device_id=(other // 4, other % 4), device_id_type=MESH
        )

    pl.semaphore_wait(barrier, 31)


def remote(source, target, send, receive, device):
    return pltpu.make_async_remote_copy(
        src_ref=source,
        dst_ref=target,
        send_sem=send,
        recv_sem=receive,
        device_id=device,
        device_id_type=MESH,
    )


def await_bytes(view, semaphore):
    pltpu.make_async_copy(view, view, semaphore).wait()


SHIFTS = tuple(
    near + (half,) for near in itertools.product(range(2), repeat=3) for half in (1, 0)
)


def row_pieces(place, source, slot_of, sems, copies, block_of=None):
    rows_all = source.shape[-2]
    step = rows_all // 3
    device = lambda half: (place.column * 2 + place.low, half * 2 + place.core)

    def piece(rows, half):
        block = source.at[rows] if block_of is None else block_of(half, rows)
        copy = remote(block, slot_of(half, rows), sems.at[0], sems.at[1], device(half))
        own = (place.low == place.core) & (place.half == half)

        @pl.when(own)
        def _():
            pltpu.make_async_copy(block, slot_of(half, rows), sems.at[1]).start()

        @pl.when(jnp.logical_not(own))
        def _():
            copy.start()

        copies.append((own, copy))

    return [
        functools.partial(piece, pl.ds(third * step, step), half)
        for third in range(3)
        for half in range(2)
    ]


def wait_pieces(copies):
    for own, copy in copies:

        @pl.when(jnp.logical_not(own))
        def _():
            copy.wait_send()


class Spread:
    def __init__(self, pick):
        self.pick = pick

    def pieces(self, place, source, target, sems):
        self.copies = []
        slot = target.at[place.column, place.core, place.z]

        def piece(shift):
            column, low, half = place.shifted(*shift)
            block = self.pick(source, column * 2 + low)
            if any(shift):
                copy = remote(
                    block, slot, sems.at[0], sems.at[1], (column * 2 + place.core, half * 2 + low)
                )
                copy.start()
                self.copies.append(copy)
            else:
                pltpu.make_async_copy(block, slot, sems.at[1]).start()

        return [functools.partial(piece, shift) for shift in SHIFTS]

    def relay(self, place, source, target, sems):
        mine = target.at[:, place.core]
        await_bytes(mine, sems.at[1])
        self.passed = remote(mine, mine, sems.at[2], sems.at[3], place.sibling())
        self.passed.start()

    def finish(self, place, source, target, sems):
        self.passed.wait()
        for copy in self.copies:
            copy.wait_send()


class RowSpread:
    def pieces(self, place, source, target, sems):
        self.copies = []
        slot = target.at[place.half, place.low]
        return row_pieces(place, source, lambda half, rows: slot.at[rows], sems, self.copies)

    def relay(self, place, source, target, sems):
        mine = target.at[:, place.core]
        await_bytes(mine, sems.at[1])
        self.passed = remote(mine, mine, sems.at[2], sems.at[3], place.sibling())
        self.passed.start()

    def finish(self, place, source, target, sems):
        self.passed.wait()
        wait_pieces(self.copies)


class Peers:
    def __init__(self, pick):
        self.pick = pick

    def start(self, place, source, target, sems):
        self.copies = []
        slot = target.at[place.part]
        for shift in itertools.product(range(2), repeat=3):
            column, low, half = place.shifted(*shift, 0)
            block = self.pick(source, column * 2 + low)
            if any(shift):
                copy = remote(
                    block, slot, sems.at[0], sems.at[1], (column * 2 + place.core, half * 2 + low)
                )
                copy.start()
                self.copies.append(copy)
            else:
                pltpu.make_async_copy(block, slot, sems.at[1]).start()

    def relay(self, place, source, target, sems):
        pass

    def finish(self, place, source, target, sems):
        await_bytes(target, sems.at[1])
        for copy in self.copies:
            copy.wait_send()


class Swap:
    def start(self, place, source, target, sems):
        self.copy = remote(
            source.at[:, 1 - place.core], target, sems.at[0], sems.at[1], place.sibling()
        )
        self.copy.start()

    def relay(self, place, source, target, sems):
        pass

    def finish(self, place, source, target, sems):
        self.copy.wait()


class Owners:
    def pieces(self, place, source, target, sems):
        self.copies = []
        if len(target.shape) == 3:
            width = source.shape[-1]
            cut = pl.ds(pl.multiple_of(place.part * width, 128), width)
            slot = target.at[place.half, :, cut]
        else:
            slot = target.at[place.half, place.part]

        def piece(shift):
            column, low, half = place.shifted(*shift)
            z = half * 2 + low
            block = source.at[column, place.core, z]
            if any(shift):
                copy = remote(
                    block, slot, sems.at[0], sems.at[1], (column * 2 + place.core, z)
                )
                copy.start()
                self.copies.append(copy)
            else:
                pltpu.make_async_copy(block, slot, sems.at[1]).start()

        return [functools.partial(piece, shift) for shift in SHIFTS]

    def finish(self, place, source, target, sems):
        await_bytes(target, sems.at[1])
        for copy in self.copies:
            copy.wait_send()


class RowOwners:
    def pieces(self, place, source, target, sems):
        self.copies = []
        slot = target.at[place.half]
        return row_pieces(
            place,
            source,
            lambda half, rows: slot.at[rows],
            sems,
            self.copies,
            lambda half, rows: source.at[half, place.core, rows],
        )

    def finish(self, place, source, target, sems):
        await_bytes(target, sems.at[1])
        wait_pieces(self.copies)


PACE = (6, 0, 0, 3, 1, 1)
PART = TOK // 2


class Semaphores:
    def __init__(self, array):
        self.array, self.used = array, 0

    def take(self, count):
        taken = self.array.at[pl.ds(self.used, count)]
        self.used += count
        return taken


LIGHT = ((2, 0, 1), (2, 1, 0), (0, 2, 1), (1, 2, 0))
EVEN = ((0, 1, 2), (1, 2, 0), (2, 0, 1))


def cuts(width, count):
    ends = [-(-(width // 128) * step // count) * 128 for step in range(count + 1)]
    return [pl.ds(start, end - start) for start, end in zip(ends, ends[1:])]


class CubeGather:
    def __init__(self, place, buffer, semaphores, rows, orders=LIGHT):
        self.place, self.buffer, self.copies = place, buffer, []
        self.rows, self.orders = rows, orders
        self.cuts = cuts(buffer.shape[4], len(orders))
        self.sems = semaphores.take(6 * len(orders))

    def step(self, number):
        routes = len(self.orders)
        for route, (axes, cut) in enumerate(zip(self.orders, self.cuts)):
            if number > 0:
                self.copies[routes * (number - 1) + route].wait_recv()
            region = self.buffer.at[self.place.cube(axes[number:]) + (self.rows, cut)]
            index = routes * number + route
            copy = remote(
                region,
                region,
                self.sems.at[index],
                self.sems.at[3 * routes + index],
                self.place.neighbour(axes[number]),
            )
            copy.start()
            self.copies.append(copy)

    def finish(self):
        for copy in self.copies[2 * len(self.orders) :]:
            copy.wait_recv()
        for copy in self.copies:
            copy.wait_send()


class CubeSum:
    def __init__(self, place, blocks, landings, semaphores, start, count, orders=LIGHT):
        self.place, self.blocks, self.landings, self.copies = place, blocks, landings, []
        self.first, self.count = start, count
        self.orders = [axes[::-1] for axes in orders]
        self.cuts = cuts(blocks.shape[4], len(orders))
        self.sems = semaphores.take(6 * len(orders))

    def send(self, number, route):
        axes, cut, routes = self.orders[route], self.cuts[route], len(self.orders)
        index = routes * number + route
        rows = pl.ds(self.first, self.count)
        landing = self.landings[number]
        copy = remote(
            self.blocks.at[self.place.cube(axes[:number], axes[number]) + (rows, cut)],
            landing.at[(slice(None),) * (2 - number) + (rows, cut)],
            self.sems.at[index],
            self.sems.at[3 * routes + index],
            self.place.neighbour(axes[number]),
        )
        copy.start()
        self.copies.append(copy)

    def start(self):
        for route in range(len(self.orders)):
            self.send(0, route)

    def step(self, number, result=None):
        for route, (axes, cut) in enumerate(zip(self.orders, self.cuts)):
            self.copies[len(self.orders) * number + route].wait_recv()
            landing = self.landings[number]
            for picks in itertools.product(range(2), repeat=2 - number):
                chosen = iter(picks)
                index = tuple(
                    self.place.own[axis] if axis in axes[: number + 1] else next(chosen)
                    for axis in range(3)
                )

                @pl.loop(0, self.count // 32)
                def _(block):
                    rows = pl.ds(pl.multiple_of(self.first + block * 32, 32), 32)
                    total = self.blocks[index + (rows, cut)].astype(full_type) + landing[
                        picks + (rows, cut)
                    ].astype(full_type)
                    if number < 2:
                        self.blocks[index + (rows, cut)] = total.astype(low_type)
                    else:
                        result[rows, cut] = total

            if number < 2:
                self.send(number + 1, route)

    def finish(self):
        for copy in self.copies:
            copy.wait_send()


class Move:
    def __init__(self, place, plan, source, target, semaphores):
        self.plan, self.arguments = plan, (place, source, target, semaphores.take(4))

    def pieces(self):
        return self.plan.pieces(*self.arguments)

    def start(self):
        if hasattr(self.plan, "start"):
            self.plan.start(*self.arguments)
        else:
            for piece in self.pieces():
                piece()

    def relay(self):
        self.plan.relay(*self.arguments)

    def finish(self):
        self.plan.finish(*self.arguments)


class Pump:
    def __init__(self, wide, tall):
        wide = [item.pieces() for item in wide]
        tall = [item.pieces() for item in tall]
        self.units = []
        for step in range(8):
            self.units.append([piece for each in wide for piece in each[2 * step : 2 * step + 2]])
            if step % 3 == 1:
                third = step // 3
                self.units.append(
                    [piece for each in tall for piece in each[2 * third : 2 * third + 2]]
                )

    def start(self, count):
        for _ in range(min(count, len(self.units))):
            for piece in self.units.pop(0):
                piece()


class Local:
    def __init__(self, semaphores):
        self.semaphores, self.copies = semaphores, []

    def start(self, source, target):
        copy = pltpu.make_async_copy(source, target, self.semaphores.take(1).at[0])
        copy.start()
        self.copies.append(copy)
        return copy

    def finish(self):
        for copy in self.copies:
            copy.wait()


def whole(source, part):
    return source


def by_part(source, part):
    return source.at[part]


def by_columns(source, part):
    width = source.shape[1] // PARTS
    return source.at[:, pl.ds(pl.multiple_of(part * width, 128), width)]


def row_block(row):
    return pl.ds(pl.multiple_of(row * TOK, TOK), TOK)


def small_expm1(values):
    near = values * (
        1.0
        + values
        * (0.5 + values * (1 / 6 + values * (1 / 24 + values * (1 / 120 + values * (1 / 720)))))
    )
    return jnp.where(values > -0.25, near, jnp.exp(values) - 1.0)


def gelu_parts(values):
    scale = 0.7978845608028654
    bent = jnp.tanh(scale * (values + 0.044715 * values * values * values))
    slope = 0.5 * (1.0 + bent) + 0.5 * values * (1.0 - bent * bent) * scale * (
        1.0 + 3 * 0.044715 * values * values
    )
    return (0.5 * values * (1.0 + bent), slope)


def put(array, rows, values):
    for piece in range(WIDTH // 128):
        array[piece, rows, :] = values[:, piece * 128 : (piece + 1) * 128]


def take(array, rows):
    return jnp.concatenate([array[piece, rows, :] for piece in range(WIDTH // 128)], axis=1)


def taps_of(aux):
    return [aux[tap : tap + 1, :] for tap in range(4)]


def placed_sum(gathered, place, row):
    owners = [
        gathered[place.part // 2, place.part % 2, z, row : row + 1, :].astype(full_type)
        for z in range(4)
    ]
    return owners[0] + owners[1] + owners[2] + owners[3]


def placed_gain(gathered, row):
    pieces = []
    for column, core, pair in itertools.product(range(COLUMNS), range(2), range(2)):
        both = [
            gathered[column, core, 2 * pair + odd, row : row + 1, 0:128].astype(full_type)
            for odd in range(2)
        ]
        pieces.append(both[0] + both[1])
    return jnp.concatenate(pieces, axis=1)


def scaled_norm(values, gain):
    scale = lax.rsqrt(jnp.mean(values * values, axis=1, keepdims=True) + epsilon)
    return values * scale * gain


def whole_block(place, row):
    return (row // 4, row // 2 % 2, row % 2)


def add_swapped(array, landing, core):
    rows, columns = array.shape[-2:]
    inner = array.shape[2] if len(array.shape) == 5 else 1
    outer = array.shape[0]
    chunk = 32 if columns > 1024 and rows % 32 == 0 else 16 if rows % 16 == 0 else 8

    @pl.loop(0, outer * inner * (rows // chunk))
    def _(step):
        part = pl.ds(pl.multiple_of(step % (rows // chunk) * chunk, chunk), chunk)
        first = step // (rows // chunk)
        if len(array.shape) == 5:
            here, there = (first // inner, core, first % inner, part), (first // inner, first % inner, part)
        else:
            here, there = (first, core, part), (first, part)
        total = array[here].astype(full_type) + landing[there].astype(full_type)
        array[here] = total.astype(array.dtype)


def norm_back(values, gain, grad):
    scale = lax.rsqrt(jnp.mean(values * values, axis=1, keepdims=True) + epsilon)
    inner = grad * gain
    along = jnp.mean(inner * values, axis=1, keepdims=True)
    return (scale * inner - values * (scale * scale * scale * along), grad * values * scale)


def block_kernel(
    tokens,
    small,
    states,
    columns,
    gates,
    out_rows,
    mlp_gate,
    mlp_up,
    mlp_down,
    cotangent,
    output,
    grad_tokens,
    states_back,
    small_back,
    columns_back,
    gate_back,
    up_back,
    blocks_back,
    rows_back,
    down_back,
    normed_kept,
    cot_kept,
    cube_one,
    cube_two,
    cube_three,
    blocks,
    landing_one,
    landing_two,
    landing_three,
    small_all,
    states_all,
    columns_all,
    gates_sent,
    gates_all,
    rows_all,
    gate_all,
    up_all,
    down_all,
    pre,
    conv,
    hidden,
    mixed,
    decays,
    carries,
    padded,
    after,
    grad,
    summed,
    aux,
    gains,
    grad_gains,
    grad_aux,
    active,
    grad_gate,
    grad_up,
    down_landing,
    grad_pre,
    grad_blocks,
    blocks_low,
    blocks_landing,
    grad_states,
    small_terms,
    small_landing,
    sems,
    free,
):
    place = Place()
    semaphores = Semaphores(sems)
    local = Local(semaphores)
    width = tokens.shape[1]
    hidden_units = gate_all.shape[-1]
    tokens_all = cube_one
    normed = cube_two
    two_all = cube_three

    def move(plan, source, target):
        return Move(place, plan, source, target, semaphores)

    def whole_matrix(array):
        return array[...].reshape(-1, array.shape[-1])

    own_tokens = tokens_all.at[place.own]
    load = pltpu.make_async_copy(tokens, own_tokens, semaphores.take(1).at[0])
    load.start()
    greet_all(place)
    load.wait()
    every = pl.ds(0, TOK)
    parts = (pl.ds(0, PART), pl.ds(PART, PART))
    tokens_gather = CubeGather(place, tokens_all, semaphores, every, EVEN)
    tokens_gather.step(0)
    load_own_cot = pltpu.make_async_copy(
        cotangent, cot_kept.at[place.own], semaphores.take(1).at[0]
    )
    load_own_cot.start()
    small_move = move(Spread(whole), small, small_all)
    small_move.start()
    states_move = move(Peers(by_part), states, states_all)
    states_move.start()
    columns_move = move(Spread(by_part), columns, columns_all)
    columns_move.start()
    gates_move = move(RowSpread(), gates, gates_sent)
    gates_move.start()
    rows_move = move(RowSpread(), out_rows, rows_all)
    rows_move.start()
    tokens_gather.step(1)
    small_move.relay()
    tokens_gather.step(2)
    late = [
        move(Spread(by_columns), mlp_gate, gate_all),
        move(Spread(by_columns), mlp_up, up_all),
        move(RowSpread(), mlp_down, down_all),
    ]
    late_pump = Pump(late[:2], late[2:])
    late_pump.start(PACE[0])
    small_move.finish()
    for tap in range(5):
        aux[tap : tap + 1, :] = placed_sum(small_all, place, tap)
    decay_row = aux[4:5, :]
    aux[4:5, :] = jnp.maximum(-decay_row, 0.0) + jnp.log1p(jnp.exp(-jnp.abs(decay_row)))
    aux[5:6, :] = jax.nn.sigmoid(-decay_row)
    aux[6:8, :] = jnp.zeros((2, WIDTH), full_type)
    gains[0:1, :] = placed_gain(small_all, 5)
    gains[1:2, :] = placed_gain(small_all, 6)
    tokens_gather.finish()
    cot_gather = CubeGather(place, cot_kept, semaphores, every)
    load_own_cot.wait()

    @pl.loop(0, SPAN // 32)
    def _(step):
        rows = pl.ds(pl.multiple_of(step % 4 * 32, 32), 32)
        index = whole_block(place, step // 4) + (rows,)
        normed[index] = scaled_norm(tokens_all[index].astype(full_type), gains[0:1, :]).astype(
            low_type
        )

    keep_normed = local.start(normed, normed_kept)
    columns_move.relay()
    gates_move.relay()
    rows_move.relay()
    columns_move.finish()
    late_pump.start(PACE[1])

    @pl.loop(0, 4)
    def _(step):
        rows = pl.ds(pl.multiple_of(step * 256, 256), 256)
        pre[rows, :] = jnp.dot(
            normed[step // 2, step % 2].reshape(256, width),
            whole_matrix(columns_all),
            preferred_element_type=full_type,
        )

    late_pump.start(PACE[2])
    gates_move.finish()
    states_move.finish()
    pair = 2 * LANES
    for block, odd in itertools.product(range(2), range(2)):
        sent = gates_sent[block, odd].astype(full_type)
        empty = jnp.zeros((LANES, pair), full_type)
        pieces = []
        for kind in range(2):
            piece = sent[:, kind * pair : (kind + 1) * pair]
            pieces += [piece, empty] if block == 0 else [empty, piece]
        gates_all[block, odd] = jnp.concatenate(pieces, axis=1).astype(low_type)

    taps = taps_of(aux)
    soft, slope = aux[4:5, :], aux[5:6, :]

    def gate_logits(low):
        both = jnp.dot(low, whole_matrix(gates_all), preferred_element_type=full_type)
        return (jax.nn.sigmoid(both[:, 0:WIDTH]), jax.nn.sigmoid(both[:, WIDTH:]))

    @pl.loop(0, PARTS)
    def _(row):
        rows = row_block(row)
        padded[0:8, :] = states_all[row]
        padded[8 : 8 + TOK, :] = pre[rows, 0:WIDTH]
        total = taps[0] * padded[8 : 8 + TOK, :]
        for tap in range(1, 4):
            total = total + taps[tap] * padded[8 - tap : 8 - tap + TOK, :]
        low = total.astype(low_type)
        conv[rows, :] = low
        recur, gate = gate_logits(low)
        log_decay = -8.0 * recur * soft
        scale = jnp.sqrt(-small_expm1(2.0 * log_decay))
        put(carries, rows, scale * gate * low.astype(full_type))
        put(decays, rows, jnp.exp(log_decay))

    def advance(time, carried):
        across = pl.ds(time, PARTS, stride=TOK)
        carried = [
            decays[piece, across, :] * before + carries[piece, across, :]
            for piece, before in enumerate(carried)
        ]
        for piece, now in enumerate(carried):
            hidden[piece, across, :] = now
        return carried

    late_pump.start(PACE[3])
    initial = states_all[:, 0, :]
    initial = [initial[:, piece * 128 : (piece + 1) * 128] for piece in range(WIDTH // 128)]
    lax.fori_loop(0, TOK, advance, initial, unroll=8)
    rows_move.finish()

    def project_out(part):
        @pl.loop(0, PARTS)
        def _(row):
            rows = pl.ds(pl.multiple_of(row * TOK + part * PART, PART), PART)
            gated, _ = gelu_parts(pre[rows, WIDTH:])
            low = (take(hidden, rows) * gated).astype(low_type)
            mixed[rows, :] = low
            blocks[whole_block(place, row) + (parts[part],)] = jnp.dot(
                low, whole_matrix(rows_all), preferred_element_type=full_type
            ).astype(low_type)

    def norm_two(part):
        @pl.loop(0, PART // 32)
        def _(step):
            rows = pl.ds(pl.multiple_of(part * PART + step * 32, 32), 32)
            total = after[rows, :] + tokens_all[place.own + (rows,)].astype(full_type)
            after[rows, :] = total
            two_all[place.own + (rows,)] = scaled_norm(total, gains[1:2, :]).astype(low_type)

    landings = (landing_one, landing_two, landing_three)

    def cube_sum(array, part):
        return CubeSum(place, array, landings, semaphores, part * PART, PART)

    mixer_sums = [cube_sum(blocks, part) for part in range(2)]
    two_gathers = [CubeGather(place, two_all, semaphores, rows) for rows in parts]
    for part in range(2):
        project_out(part)
        mixer_sums[part].start()
        late_pump.start(PACE[4 + part])
    for part in range(2):
        mixer_sums[part].step(0)
    cot_gather.step(0)
    for part in range(2):
        mixer_sums[part].step(1)
    cot_gather.step(1)
    for part in range(2):
        mixer_sums[part].step(2, after)
        norm_two(part)
        two_gathers[part].step(0)
    late_pump.start(20)
    cot_gather.step(2)
    for part in range(2):
        two_gathers[part].step(1)
    for part in range(2):
        two_gathers[part].step(2)
    cot_gather.finish()
    cot_all = cube_one
    load_cot = pltpu.make_async_copy(cot_kept, cot_all, semaphores.take(1).at[0])
    load_cot.start()
    for item in late:
        item.relay()
    for part in range(2):
        mixer_sums[part].finish()
    keep_normed.wait()
    load_cot.wait()
    for item in late:
        item.finish()

    out_blocks = cube_two

    def mlp(part, y):
        rows = parts[part]
        at = (y, slice(None), slice(None), rows)
        index = y * 2 + part
        normed_two = two_all[at].reshape(4 * PART, width)
        cot = cot_all[at].reshape(4 * PART, width)
        for piece in range(2):
            cut = pl.ds(piece * (hidden_units // 2), hidden_units // 2)
            gate_part, up_part = (
                jnp.dot(
                    normed_two,
                    array[:, :, :, :, cut].reshape(width, hidden_units // 2),
                    preferred_element_type=full_type,
                )
                for array in (gate_all, up_all)
            )
            gated, bend = gelu_parts(gate_part)
            matrix = down_all[piece].reshape(hidden_units // 2, width)
            grad_active = cols_product(cot, matrix)
            for array, values in (
                (active, gated * up_part),
                (grad_gate, grad_active * up_part * bend),
                (grad_up, grad_active * gated),
            ):
                array[index, :, :, cut] = values.astype(low_type).reshape(
                    4, PART, hidden_units // 2
                )
        low, to_gate, to_up = (whole_matrix(array.at[index]) for array in (active, grad_gate, grad_up))
        for piece in range(4):
            cut = pl.ds(piece * (width // 4), width // 4)
            matrix = down_all[:, :, :, cut].reshape(hidden_units, width // 4)
            out_blocks[at + (cut,)] = (
                jnp.dot(low, matrix, preferred_element_type=full_type)
                .astype(low_type)
                .reshape(2, 2, PART, width // 4)
            )
            back = cols_product(to_gate, whole_matrix(gate_all.at[piece])) + cols_product(
                to_up, whole_matrix(up_all.at[piece])
            )
            blocks[at + (cut,)] = back.astype(low_type).reshape(2, 2, PART, width // 4)

    def by_tokens(array, cut):
        return jnp.concatenate(
            [
                array[y, :, :, rows, cut].reshape(4 * PART, cut.size)
                for y in range(2)
                for rows in parts
            ],
            axis=0,
        )

    def grad_rows(terms, sums):
        @pl.loop(0, 8)
        def _(step):
            side = by_tokens(two_all, pl.ds(pl.multiple_of(step * 256, 256), 256))
            sums[step // 2, step % 2] = (
                rows_product(side, whole_matrix(terms))
                .astype(low_type)
                .reshape(4, 64, hidden_units)
            )

    def norm_two_back(part):
        @pl.loop(0, PART // 32)
        def _(step):
            rows = pl.ds(pl.multiple_of(part * PART + step * 32, 32), 32)
            back, by_gain = norm_back(after[rows, :], gains[1:2, :], grad[rows, :])
            total = cot_all[place.own + (rows,)].astype(full_type) + back
            grad[rows, :] = total
            cot_all[place.own + (rows,)] = total.astype(low_type)
            grad_gains[1:2, :] += jnp.sum(by_gain, axis=0, keepdims=True)

    mixed_all = cube_one
    two_sums = [cube_sum(blocks, part) for part in range(2)]
    mixed_gathers = [CubeGather(place, cube_one, semaphores, rows) for rows in parts]
    two_gathers[0].finish()

    @pl.loop(0, 2)
    def _(y):
        mlp(0, y)

    two_sums[0].start()
    two_gathers[1].finish()
    mlp(1, 0)
    two_sums[0].step(0)
    mlp(1, 1)
    two_sums[1].start()

    @pl.loop(0, 4)
    def _(step):
        cut = pl.ds(pl.multiple_of(step * 512, 512), 512)
        side = by_tokens(cot_all, cut)
        for piece in range(2):
            half = pl.ds(piece * (hidden_units // 2), hidden_units // 2)
            down_all[piece, :, :, cut] = (
                rows_product(active[:, :, :, half].reshape(SPAN, hidden_units // 2), side)
                .astype(low_type)
                .reshape(2, hidden_units // 4, 512)
            )

    def tell_sibling(number):
        pl.semaphore_signal(
            free.at[number], inc=1, device_id=place.sibling(), device_id_type=MESH
        )

    gate_swap = move(Swap(), gate_all, active)
    up_swap = move(Swap(), up_all, grad_gate)
    down_swap = move(Swap(), down_all, down_landing)
    gate_return = move(Owners(), gate_all, gate_back)
    up_return = move(Owners(), up_all, up_back)
    down_return = move(RowOwners(), down_all, down_back)
    returns = [gate_return, up_return, down_return]
    tell_sibling(0)
    down_swap.start()
    two_sums[0].step(1)
    two_sums[1].step(0)
    grad_rows(grad_gate, gate_all)
    tell_sibling(1)
    pl.semaphore_wait(free.at[0], 1)
    gate_swap.start()
    grad_gains[...] = jnp.zeros_like(grad_gains)
    two_sums[0].step(2, grad)
    norm_two_back(0)
    mixed_gathers[0].step(0)
    two_sums[1].step(1)
    down_swap.finish()
    add_swapped(down_all, down_landing, place.core)
    grad_rows(grad_up, up_all)
    pl.semaphore_wait(free.at[1], 1)
    up_swap.start()
    two_sums[1].step(2, grad)
    norm_two_back(1)
    mixed_gathers[1].step(0)
    gate_swap.finish()
    add_swapped(gate_all, active, place.core)
    mixed_gathers[0].step(1)
    mixed_gathers[1].step(1)
    up_swap.finish()
    add_swapped(up_all, grad_gate, place.core)
    tell_sibling(2)
    mixed_gathers[0].step(2)
    mixed_gathers[1].step(2)
    for item in returns:
        item.start()
    for part in range(2):
        two_sums[part].finish()
        mixed_gathers[part].finish()

    out_sum = CubeSum(
        place,
        out_blocks,
        (cube_three.at[0], cube_three.at[1, 0], cube_three.at[1, 1, 0]),
        semaphores,
        0,
        TOK,
    )
    out_sum.start()

    @pl.loop(0, PARTS)
    def _(row):
        rows = row_block(row)
        branch = cols_product(mixed_all[whole_block(place, row)], whole_matrix(rows_all))
        gated, bend = gelu_parts(pre[rows, WIDTH:])
        grad_pre[rows, WIDTH:] = (branch * take(hidden, rows) * bend).astype(low_type)
        put(carries, rows, branch * gated)

    @pl.loop(0, 4)
    def _(step):
        cut = pl.ds(pl.multiple_of(step * 512, 512), 512)
        rows_all[:, :, :, cut] = (
            rows_product(mixed[...], mixed_all[:, :, :, :, cut].reshape(SPAN, 512))
            .astype(low_type)
            .reshape(2, 2, LANES, 512)
        )

    pl.semaphore_wait(free.at[2], 1)
    rows_swap = move(Swap(), rows_all, down_landing.at[:, pl.ds(0, LANES)])
    rows_swap.start()
    normed_again = cube_one
    load_normed = pltpu.make_async_copy(normed_kept, normed_again, semaphores.take(1).at[0])
    load_normed.start()

    def advance_back(step, state):
        factors, carried = state
        across = pl.ds(TOK - 1 - step, PARTS, stride=TOK)
        carried = [
            carries[piece, across, :] + factors[piece] * before
            for piece, before in enumerate(carried)
        ]
        for piece, now in enumerate(carried):
            carries[piece, across, :] = now
        return ([decays[piece, across, :] for piece in range(WIDTH // 128)], carried)

    zeros = [jnp.zeros((PARTS, 128), full_type)] * (WIDTH // 128)
    lax.fori_loop(0, TOK, advance_back, (zeros, zeros), unroll=8)
    rows_swap.finish()
    add_swapped(rows_all, down_landing, place.core)
    rows_return = move(RowOwners(), rows_all, rows_back)
    rows_return.start()
    grad_aux[...] = jnp.zeros_like(grad_aux)
    grad_blocks[...] = jnp.zeros_like(grad_blocks)

    @pl.loop(0, PARTS)
    def _(row):
        rows = row_block(row)
        padded[0:8, :] = jnp.broadcast_to(states_all[row, 0:1, :], (8, WIDTH))
        padded[8 : 8 + TOK, :] = take(hidden, rows)
        low = conv[rows, :]
        recur, gate = gate_logits(low)
        log_decay = -8.0 * recur * soft
        decay = take(decays, rows)
        scale = jnp.sqrt(-small_expm1(2.0 * log_decay))
        conv_full = low.astype(full_type)
        carried = take(carries, rows)
        total = (
            carried * decay * padded[7 : 7 + TOK, :]
            - carried * gate * conv_full * (decay * decay) / scale
        )
        grad_aux[4:5, :] += jnp.sum(total * 8.0 * recur * slope, axis=0, keepdims=True)
        to_recur = (total * (-8.0 * soft) * recur * (1.0 - recur)).astype(low_type)
        to_input = (carried * scale * conv_full * gate * (1.0 - gate)).astype(low_type)
        both = jnp.concatenate([to_recur, to_input], axis=1)
        grad_blocks[...] += rows_product(low, both)
        back = carried * scale * gate + cols_product(both, whole_matrix(gates_all))
        first = decay[0:1, :] * carried[0:1, :]
        padded[0:8, :] = jnp.zeros((8, WIDTH), full_type)
        padded[8 : 8 + TOK, :] = back
        padded[8 + TOK :, :] = jnp.zeros((8, WIDTH), full_type)
        spread = taps[0] * padded[0 : 8 + TOK, :]
        for tap in range(1, 4):
            spread = spread + taps[tap] * padded[tap : tap + 8 + TOK, :]
        grad_pre[rows, 0:WIDTH] = spread[8:, :].astype(low_type)
        grad_states[row] = spread[0:8, :]
        grad_states[row, 0:1, :] = first
        padded[0:8, :] = states_all[row]
        padded[8 : 8 + TOK, :] = pre[rows, 0:WIDTH]
        for tap in range(4):
            grad_aux[tap : tap + 1, :] += jnp.sum(
                back * padded[8 - tap : 8 - tap + TOK, :], axis=0, keepdims=True
            )

    states_return = move(Peers(by_part), grad_states, states_back)
    states_return.start()
    for block in range(2):
        rows = slice(block * pair, (block + 1) * pair)
        kinds = [
            grad_blocks[rows, kind * WIDTH : (kind + 1) * WIDTH][:, rows] for kind in range(2)
        ]
        blocks_low[block] = (
            jnp.concatenate(kinds, axis=1).astype(low_type).reshape(2, LANES, WIDTH)
        )

    out_sum.step(0)

    one_sums = [cube_sum(blocks, part) for part in range(2)]
    for part in range(2):

        @pl.loop(0, PARTS)
        def _(row):
            terms = grad_pre[pl.ds(pl.multiple_of(row * TOK + part * PART, PART), PART), :]
            for piece in range(COLUMNS):
                cut = pl.ds(piece * (width // 4), width // 4)
                blocks[whole_block(place, row) + (parts[part], cut)] = cols_product(
                    terms, whole_matrix(columns_all.at[piece])
                ).astype(low_type)

        one_sums[part].start()

    out_sum.step(1)
    one_sums[0].step(0)
    one_sums[1].step(0)
    out_sum.step(2, summed)

    @pl.loop(0, TOK // 32)
    def _(step):
        rows = pl.ds(pl.multiple_of(step * 32, 32), 32)
        cube_three[1, 1, 1, rows, :] = (after[rows, :] + summed[rows, :]).astype(low_type)

    local.start(cube_three.at[1, 1, 1], output)
    load_normed.wait()

    @pl.loop(0, 8)
    def _(step):
        cut = pl.ds(pl.multiple_of(step * 256, 256), 256)
        columns_all[step // 2, step % 2] = (
            rows_product(normed_again[:, :, :, :, cut].reshape(SPAN, 256), grad_pre[...])
            .astype(low_type)
            .reshape(4, 64, 2 * WIDTH)
        )

    mixer_swaps = [
        move(Swap(), columns_all, active),
        move(Swap(), blocks_low, blocks_landing),
    ]
    for item in mixer_swaps:
        item.start()
    one_sums[0].step(1)
    one_sums[1].step(1)
    mixer_swaps[0].finish()
    add_swapped(columns_all, active, place.core)
    columns_return = move(Owners(), columns_all, columns_back)
    columns_return.start()
    mixer_swaps[1].finish()
    add_swapped(blocks_low, blocks_landing, place.core)
    blocks_return = move(RowOwners(), blocks_low, blocks_back)
    blocks_return.start()
    one_sums[0].step(2, summed)
    one_sums[1].step(2, summed)
    load_tokens = pltpu.make_async_copy(
        tokens, cube_three.at[1, 0, 0], semaphores.take(1).at[0]
    )
    out_sum.finish()
    load_tokens.start()
    load_tokens.wait()

    @pl.loop(0, TOK // 32)
    def _(step):
        rows = pl.ds(pl.multiple_of(step * 32, 32), 32)
        values = cube_three[1, 0, 0, rows, :].astype(full_type)
        back, by_gain = norm_back(values, gains[0:1, :], summed[rows, :])
        cube_three[1, 0, 1, rows, :] = (grad[rows, :] + back).astype(low_type)
        grad_gains[0:1, :] += jnp.sum(by_gain, axis=0, keepdims=True)

    local.start(cube_three.at[1, 0, 1], grad_tokens)
    small_terms[...] = jnp.zeros_like(small_terms)
    for column, core, z in itertools.product(range(COLUMNS), range(2), range(4)):
        tile = (column * 8 + core * 4 + z) // 2
        small_terms[column, core, z, 0:2, 0:128] = grad_gains[:, tile * 128 : (tile + 1) * 128]
    for z in range(4):
        small_terms[place.part // 2, place.part % 2, z, 2:7, :] = grad_aux[0:5, :]
    small_swap = move(Swap(), small_terms, small_landing)
    small_swap.start()
    small_swap.finish()
    add_swapped(small_terms, small_landing, place.core)
    small_return = move(Owners(), small_terms, small_back)
    small_return.start()
    for part in range(2):
        one_sums[part].finish()
    for item in [states_return, small_return, columns_return, rows_return, blocks_return] + returns:
        item.finish()
    for copy in local.copies[1:]:
        copy.wait()


def block_call(arrays, rows, width, units):
    hbm = pl.BlockSpec(memory_space=pl.ANY)
    lanes = (WIDTH // 128, SPAN, 128)
    cube = (2, 2, 2, TOK, width)
    spread = (COLUMNS, 2, 4, rows)
    hidden_units = 4 * units
    outputs = [
        ((TOK, width), low_type),
        ((TOK, width), low_type),
        ((PARTS, 8, WIDTH), full_type),
        ((2, PARTS, 8, WIDTH), full_type),
        ((2, PARTS, rows, 2 * WIDTH), low_type),
        ((2, rows, PARTS * hidden_units), low_type),
        ((2, rows, PARTS * hidden_units), low_type),
        ((2, LANES, WIDTH), low_type),
        ((2, LANES, width), low_type),
        ((2, units, width), low_type),
        (cube, low_type),
        (cube, low_type),
    ]
    scratch = [
        (cube, low_type),
        (cube, low_type),
        (cube, low_type),
        (cube, low_type),
        ((2, 2, TOK, width), low_type),
        ((2, TOK, width), low_type),
        ((TOK, width), low_type),
        ((COLUMNS, 2, 4, 16, WIDTH), low_type),
        ((PARTS, 8, WIDTH), full_type),
        (spread + (2 * WIDTH,), low_type),
        ((2, 2, LANES, WIDTH), low_type),
        ((2, 2, LANES, 2 * WIDTH), low_type),
        ((2, 2, LANES, width), low_type),
        (spread + (hidden_units,), low_type),
        (spread + (hidden_units,), low_type),
        ((2, 2, units, width), low_type),
        ((SPAN, 2 * WIDTH), full_type),
        ((SPAN, WIDTH), low_type),
        (lanes, full_type),
        ((SPAN, WIDTH), low_type),
        (lanes, full_type),
        (lanes, full_type),
        ((TOK + 16, WIDTH), full_type),
        ((TOK, width), full_type),
        ((TOK, width), full_type),
        ((TOK, width), full_type),
        ((8, WIDTH), full_type),
        ((2, width), full_type),
        ((2, width), full_type),
        ((8, WIDTH), full_type),
        ((4, 4, 64, hidden_units), low_type),
        ((4, 4, 64, hidden_units), low_type),
        ((4, 4, 64, hidden_units), low_type),
        ((2, units, width), low_type),
        ((SPAN, 2 * WIDTH), low_type),
        ((WIDTH, 2 * WIDTH), full_type),
        ((2, 2, LANES, WIDTH), low_type),
        ((2, LANES, WIDTH), low_type),
        ((PARTS, 8, WIDTH), full_type),
        ((COLUMNS, 2, 4, 8, WIDTH), full_type),
        ((COLUMNS, 4, 8, WIDTH), full_type),
    ]
    return pl.pallas_call(
        block_kernel,
        out_shape=[jax.ShapeDtypeStruct(shape, kind) for shape, kind in outputs],
        in_specs=[hbm] * len(arrays),
        out_specs=[hbm] * len(outputs),
        scratch_shapes=[pltpu.VMEM(shape, kind) for shape, kind in scratch]
        + [pltpu.SemaphoreType.DMA((480,)), pltpu.SemaphoreType.REGULAR((3,))],
        compiler_params=pltpu.CompilerParams(
            collective_id=0, has_side_effects=True, vmem_limit_bytes=VMEM_BYTES
        ),
        name="hawk_block",
    )(*arrays)


def spread_lanes(values):
    gap = jnp.zeros((values.shape[0], LANES - CHUNK), values.dtype)
    pieces = []
    for start in range(0, values.shape[1], CHUNK):
        pieces += [values[:, start : start + CHUNK], gap]
    return jnp.concatenate(pieces, axis=1)


def joined_lanes(values):
    return [values[:, start : start + CHUNK] for start in range(0, values.shape[1], LANES)]


def prepare_kernel(
    fresh,
    gain_mixer,
    gain_mlp,
    conv_kernel,
    decay_param,
    proj_input,
    proj_gate,
    gate_recur,
    gate_input,
    proj_output,
    conv_state,
    recur_state,
    small,
    states,
    columns,
    gates,
    out_rows,
):
    z = lax.axis_index("narrow")
    keep = (1 - fresh[0]).astype(full_type)
    for kind, proj in enumerate((proj_input, proj_gate)):
        for part in range(PARTS):
            piece = proj[:, part * 4 * CHUNK : (part + 1) * 4 * CHUNK].astype(full_type)
            columns[part, :, kind * WIDTH : (kind + 1) * WIDTH] = spread_lanes(piece).astype(
                low_type
            )
    gates[CHUNK:, :] = jnp.zeros((LANES - CHUNK, WIDTH), low_type)
    gates[0:CHUNK, :] = jnp.concatenate(
        [spread_lanes(gate[...].astype(full_type)) for gate in (gate_recur, gate_input)], axis=1
    ).astype(low_type)
    out_rows[0:CHUNK, :] = proj_output[...]
    out_rows[CHUNK:, :] = jnp.zeros((LANES - CHUNK, out_rows.shape[1]), low_type)
    taps = jnp.concatenate([conv_kernel[...], decay_param[...]], axis=0).astype(full_type)
    taps = spread_lanes(taps)
    taps = jnp.concatenate(
        [jnp.where(z == place, taps, jnp.zeros_like(taps)) for place in range(4)], axis=1
    )
    gains = jnp.concatenate([gain_mixer[...], gain_mlp[...]], axis=0).astype(full_type)
    gains = [jnp.where(z % 2 == odd, gains, jnp.zeros_like(gains)) for odd in range(2)]
    gains = jnp.concatenate(gains + [jnp.zeros((2, WIDTH - 128), full_type)], axis=1)
    rest = jnp.zeros((9, WIDTH), full_type)
    small[...] = jnp.concatenate([taps, gains, rest], axis=0).astype(low_type)
    states[...] = jnp.zeros_like(states)
    for part in range(PARTS):
        cut = slice(part * 4 * CHUNK, (part + 1) * 4 * CHUNK)
        states[part, 0:1, :] = spread_lanes(recur_state[:, cut]) * keep
        states[part, 5:8, :] = spread_lanes(conv_state[:, 0, cut]) * keep


def finish_kernel(
    fresh,
    output,
    grad_tokens,
    states_back,
    small_back,
    columns_back,
    gate_back,
    up_back,
    blocks_back,
    rows_back,
    down_back,
    output_out,
    tokens_out,
    conv_out,
    recur_out,
    gain_one_out,
    input_out,
    gate_out,
    taps_out,
    decay_out,
    gate_recur_out,
    gate_input_out,
    rows_out,
    gain_two_out,
    mlp_gate_out,
    mlp_up_out,
    down_out,
):
    z = lax.axis_index("narrow")
    keep = (1 - fresh[0]).astype(full_type)
    def both(array, *index):
        return array[(0,) + index].astype(full_type) + array[(1,) + index].astype(full_type)

    output_out[0] = output[...]
    tokens_out[0] = grad_tokens[...]
    for source, target in ((gate_back, mlp_gate_out), (up_back, mlp_up_out), (down_back, down_out)):
        for start in range(0, target.shape[0], 8):
            part = slice(start, start + 8)
            target[part, :] = both(source, part)

    @pl.when(pl.program_id(0) == 0)
    def _():
        states = jnp.concatenate(
            [piece for part in range(PARTS) for piece in joined_lanes(states_back[part])], axis=1
        )
        recur_out[...] = states[0:1, :] * keep
        conv_out[:, 0, :] = states[5:8, :] * keep

        for kind, target in enumerate((input_out, gate_out)):
            pieces = []
            for part in range(PARTS):
                cut = slice(kind * WIDTH, (kind + 1) * WIDTH)
                pieces += joined_lanes(both(columns_back, part, slice(None), cut))
            target[...] = jnp.concatenate(pieces, axis=1)
        pair = 2 * LANES
        for kind, target in enumerate((gate_recur_out, gate_input_out)):
            values = both(blocks_back, slice(0, CHUNK))[:, kind * pair : (kind + 1) * pair]
            target[...] = jnp.concatenate(joined_lanes(values), axis=1)
        total = jnp.zeros((8, WIDTH), full_type)
        for half, part in itertools.product(range(2), range(PARTS)):
            total = total + small_back[half, part]
        rows = gain_one_out.shape[1]
        gains = jnp.where(z % 2 == 0, total[0:2, 0:rows], total[0:2, rows : 2 * rows])
        gain_one_out[...] = gains[0:1, :]
        gain_two_out[...] = gains[1:2, :]
        taps = total[2:7, 0:CHUNK]
        for place in range(1, 4):
            taps = jnp.where(z == place, total[2:7, place * LANES : place * LANES + CHUNK], taps)
        taps_out[...] = taps[0:4, :]
        decay_out[...] = taps[4:5, :]
        rows_out[...] = both(rows_back, slice(0, CHUNK))


def plain_call(kernel, name, flags, arrays, outputs, steps=1, cuts_in={}, cuts_out={}):
    def spec(shape, cut):
        block = tuple(size // steps if axis == cut else size for axis, size in enumerate(shape))
        return pl.BlockSpec(
            block, lambda step: tuple(step if axis == cut else 0 for axis in range(len(shape)))
        )

    return pl.pallas_call(
        kernel,
        grid=(steps,),
        out_shape=[jax.ShapeDtypeStruct(shape, kind) for shape, kind in outputs],
        in_specs=[pl.BlockSpec(memory_space=pltpu.SMEM)]
        + [spec(array.shape, cuts_in.get(place)) for place, array in enumerate(arrays)],
        out_specs=[spec(shape, cuts_out.get(place)) for place, (shape, kind) in enumerate(outputs)],
        compiler_params=pltpu.CompilerParams(vmem_limit_bytes=VMEM_BYTES),
        name=name,
    )(flags, *arrays)


def halves(
    tokens,
    conv_state,
    recur_state,
    fresh_rows,
    gain_mixer,
    proj_input,
    proj_gate,
    conv_kernel,
    decay_param,
    gate_recur,
    gate_input,
    proj_output,
    gain_mlp,
    mlp_gate,
    mlp_up,
    mlp_down,
    cotangent,
):
    width = tokens.shape[2]
    rows = width // 32
    units = mlp_down.shape[0]
    small, states, columns, gates, out_rows = plain_call(
        prepare_kernel,
        "prepare",
        fresh_rows,
        (
            gain_mixer[None],
            gain_mlp[None],
            conv_kernel,
            decay_param[None],
            proj_input,
            proj_gate,
            gate_recur,
            gate_input,
            proj_output,
            conv_state.transpose(1, 0, 2),
            recur_state,
        ),
        [
            ((16, WIDTH), low_type),
            ((PARTS, 8, WIDTH), full_type),
            ((PARTS, rows, 2 * WIDTH), low_type),
            ((LANES, WIDTH), low_type),
            ((LANES, width), low_type),
        ],
    )
    results = block_call(
        (
            tokens[0],
            small,
            states,
            columns,
            gates,
            out_rows,
            mlp_gate,
            mlp_up,
            mlp_down,
            cotangent[0],
        ),
        rows,
        width,
        units,
    )
    results = plain_call(
        finish_kernel,
        "finish",
        fresh_rows,
        results[:10],
        [
            (tokens.shape, low_type),
            (tokens.shape, low_type),
            ((conv_state.shape[1], 1, conv_state.shape[2]), full_type),
            (recur_state.shape, full_type),
            ((1, rows), full_type),
            (proj_input.shape, full_type),
            (proj_gate.shape, full_type),
            (conv_kernel.shape, full_type),
            ((1, CHUNK), full_type),
            (gate_recur.shape, full_type),
            (gate_input.shape, full_type),
            (proj_output.shape, full_type),
            ((1, rows), full_type),
            (mlp_gate.shape, full_type),
            (mlp_up.shape, full_type),
            (mlp_down.shape, full_type),
        ],
        4,
        {0: 0, 1: 0, 5: 1, 6: 1, 9: 1},
        {0: 1, 1: 1, 13: 0, 14: 0, 15: 0},
    )
    return tuple(
        result[0]
        if place in (4, 8, 12)
        else result.transpose(1, 0, 2)
        if place == 2
        else result
        for place, result in enumerate(results)
    )


def solution(mesh):
    sizes = (mesh.shape["wide"], mesh.shape["narrow"])
    return jax.shard_map(
        halves if sizes == (2 * COLUMNS, 2 * LOWS) else shards,
        mesh=mesh,
        in_specs=(
            P(("wide", "narrow"), None, None),
            P(("wide", "narrow"), None, None),
            P(("wide", "narrow"), None),
            P(("wide", "narrow")),
            P(("wide", "narrow")),
            P(("wide", "narrow"), None),
            P(("wide", "narrow"), None),
            P(None, ("wide", "narrow")),
            P(("wide", "narrow")),
            P(("wide", "narrow"), None),
            P(("wide", "narrow"), None),
            P(("wide", "narrow"), None),
            P(("wide", "narrow")),
            P(("wide", "narrow"), None),
            P(("wide", "narrow"), None),
            P(("wide", "narrow"), None),
            P(("wide", "narrow"), None, None),
        ),
        out_specs=(
            P(("wide", "narrow"), None, None),
            P(("wide", "narrow"), None, None),
            P(("wide", "narrow"), None, None),
            P(("wide", "narrow"), None),
            P(("wide", "narrow")),
            P(("wide", "narrow"), None),
            P(("wide", "narrow"), None),
            P(None, ("wide", "narrow")),
            P(("wide", "narrow")),
            P(("wide", "narrow"), None),
            P(("wide", "narrow"), None),
            P(("wide", "narrow"), None),
            P(("wide", "narrow")),
            P(("wide", "narrow"), None),
            P(("wide", "narrow"), None),
            P(("wide", "narrow"), None),
        ),
        check_vma=False,
    )
```
